256 devices in a mesh: sub: 4 (over x), tile: 64 (over y, z, core).
Axes of the slice: x: 4, y: 4, z: 8, core: 2. Of those that a mesh axis runs over, the one named last changes fastest.
Arguments:
- displacement: float32 [4, 3, 256, 32, 128], P('sub', None, 'tile'), may hold values from -3 to 3
- velocity: float32 [4, 3, 256, 32, 128], P('sub', None, 'tile'), may hold values from -6 to 6
- external_load: float32 [4, 3, 256, 32, 128], P('sub', None, 'tile'), may hold values from -6 to 6
- node_mass: float32 [4, 256, 32, 128], P('sub', 'tile'), may hold values from 1 to 4
- modulus: float32 [4, 256, 32, 128], P('sub', 'tile'), may hold values from 0.3 to 1.5
- stiffness: float32 [24, 24], replicated
- substeps: int32 [4], P('sub'), may hold values from 1 to 4, as said below
- interface_nodes: int32 [4, 8192], P('sub', 'tile'), may hold values from 0 to 16383, as said below
- factor_inverse: float32 [2, 24576, 384], P(None, 'tile')
- factor_lower: float32 [2, 24576, 384], P(None, 'tile')
Outputs:
- displacement_out: float32 [4, 3, 256, 32, 128], P('sub', None, 'tile')
- velocity_out: float32 [4, 3, 256, 32, 128], P('sub', None, 'tile')
The draws below stay inside these ranges and needn't reach their ends.
Inputs may be any that keep to these rules, and one draw needn't show every extreme that they name: Each substructure takes 1, 2 or 4 substeps; some substructure takes 4 and some takes 1. `interface_nodes`: within each tile's 128 slots of a substructure the nodes are distinct.
All inputs are finite; a program needn't handle non-finite values.
Results may differ from the reference program's by a relative error of at most 0.00011.
Values sent between devices are 32-bit elements; how exact they have to be, the bound alone decides.
No kernel may reach another device: no remote copies, remote signals or barrier semaphores. Data moves between devices by JAX's collectives and lax.ppermute only.
A program may use at most 192 MiB of HBM per device.

```python
import math
import jax
import jax.numpy as jnp
from jax import lax

CX = 4
CY = 32
CZ = 128
IFC = 128
MAXSUB = 4
NX = 256
TILES = 64
PAIRS = 2
IB = 384
SLOTS = 8192
IROWS = 24576


def block_identity(total_rows, block_cols):
    row_index = lax.broadcasted_iota(jnp.int32, (total_rows, block_cols), 0) % block_cols
    col_index = lax.broadcasted_iota(jnp.int32, (total_rows, block_cols), 1)
    return (row_index == col_index).astype(jnp.float32)


def factor_noise(key):
    return jax.random.normal(key, (PAIRS, IROWS, IB), jnp.float32)


def draw_stiffness(key, part):
    own_key = jax.random.fold_in(key, 13)
    noise = jax.random.normal(own_key, (24, 24), jnp.float32)
    return 2.5 * jnp.eye(24, dtype=jnp.float32) + 0.15 * (noise + noise.T)


def draw_factor_inverse(key, part):
    noise = factor_noise(jax.random.fold_in(key, 11))
    return 0.22 * (block_identity(IROWS, IB)[None] + 0.2 * IB ** (-0.5) * noise)


def draw_factor_lower(key, part):
    noise = factor_noise(jax.random.fold_in(key, 12))
    return -4.1 * (block_identity(IROWS, IB)[None] + 0.2 * IB ** (-0.5) * noise)


def draw_substeps(key, part):
    key = jax.random.fold_in(key, 31)
    count = 2 * PAIRS
    level_key, order_key = jax.random.split(key, 2)
    levels = jax.random.randint(level_key, (count,), 0, 3)
    counts = jnp.array([1, 2, 4], jnp.int32)[levels]
    counts = counts.at[0].set(4)
    counts = counts.at[1].set(1)
    order = jax.random.permutation(order_key, count)
    return counts[order].astype(jnp.int32)


def draw_interface_nodes(key, part):
    base_key = jax.random.fold_in(key, 21)
    node_count = CX * CY * CZ
    tile_count = SLOTS // IFC

    def one_block(block):
        block_key = jax.random.fold_in(base_key, block)
        inner = jax.random.permutation(block_key, node_count - 2)[:IFC - 2] + 1
        chosen = jnp.concatenate([jnp.array([0, node_count - 1], jnp.int32), inner.astype(jnp.int32)])
        return jax.random.permutation(jax.random.fold_in(block_key, 1), chosen)
    blocks = jax.vmap(one_block)(jnp.arange(2 * PAIRS * tile_count, dtype=jnp.int32))
    return blocks.reshape((2 * PAIRS, SLOTS)).astype(jnp.int32)


def block_levels(rng, extent, cuts, smallest, high):
    def one(axis_at, shards_of):
        steps = jax.random.uniform(jax.random.fold_in(jax.random.fold_in(rng, 6), axis_at), (shards_of,), jnp.float32, smallest / len(cuts), high / len(cuts))
        return jnp.repeat(jnp.exp(steps), extent[axis_at] // shards_of).reshape((-1,) + (1,) * (len(extent) - axis_at - 1))

    factor_of = one(*cuts[0])
    for cut in cuts[1:]:
        factor_of = factor_of * one(*cut)
    return factor_of


def gaussian(stream_key, shape, scale, bound, cuts=(), kind=jnp.bfloat16):
    values = jax.random.normal(stream_key, shape, jnp.float32) * scale
    if len(cuts) > 0:
        values = block_levels(stream_key, shape, cuts, -0.22, 0.18) * values
    return jnp.clip(values, min=-bound, max=bound).astype(kind)


def setup_inputs(seed: int = 0) -> dict:
    key_of = jax.random.split(jax.random.key(seed), 11)
    displacement = gaussian(key_of[0], (2 * PAIRS, 3, NX, CY, CZ), 0.5, 3.0, ((0, 4), (2, 64)), jnp.float32)
    velocity = gaussian(key_of[1], (2 * PAIRS, 3, NX, CY, CZ), 1.0, 6.0, ((0, 4), (2, 64)), jnp.float32)
    external_load = gaussian(key_of[2], (2 * PAIRS, 3, NX, CY, CZ), 1.0, 6.0, ((0, 4), (2, 64)), jnp.float32)
    node_mass = jnp.clip(jnp.exp(math.log(4.0) - 1.3862944 * jax.random.uniform(key_of[3], (2 * PAIRS, NX, CY, CZ), jnp.float32) ** block_levels(key_of[3], (2 * PAIRS, NX, CY, CZ), ((0, 4), (1, 64)), -0.2, 0.2)), 1.0, 4.0)
    modulus = jnp.clip(jnp.exp(math.log(1.5) - 1.60943787 * jax.random.uniform(key_of[4], (2 * PAIRS, NX, CY, CZ), jnp.float32) ** block_levels(key_of[4], (2 * PAIRS, NX, CY, CZ), ((0, 4), (1, 64)), -0.2, 0.2)), 0.3, 1.5)
    stiffness = draw_stiffness(jax.random.fold_in(key_of[10], 71), 0)
    substeps = draw_substeps(jax.random.fold_in(key_of[10], 71), 0)
    interface_nodes = draw_interface_nodes(jax.random.fold_in(key_of[10], 71), 0)
    factor_inverse = draw_factor_inverse(jax.random.fold_in(key_of[10], 71), 0)
    factor_lower = draw_factor_lower(jax.random.fold_in(key_of[10], 71), 0)
    return {"displacement": displacement, "velocity": velocity, "external_load": external_load, "node_mass": node_mass, "modulus": modulus, "stiffness": stiffness, "substeps": substeps, "interface_nodes": interface_nodes, "factor_inverse": factor_inverse, "factor_lower": factor_lower}


precise_mode = lax.Precision.HIGHEST
coarse_step = 0.1


def corner_list():
    return [(offset_x, offset_y, offset_z) for offset_x in (0, 1) for offset_y in (0, 1) for offset_z in (0, 1)]


def advance(displacement_ext, velocity_now, load_now, inverse_mass, modulus_ext, stiffness, first_x, total_x, step_size):
    layers = displacement_ext.shape[1]
    elements_x = layers - 1
    width_y = displacement_ext.shape[2]
    width_z = displacement_ext.shape[3]
    corners = []
    for offset_x, offset_y, offset_z in corner_list():
        corner_disp = displacement_ext[:, offset_x:offset_x + elements_x, offset_y:offset_y + width_y - 1, :]
        corners.append(jnp.roll(corner_disp, -offset_z, axis=3))
    element_disp = jnp.stack(corners, axis=1).reshape((24, elements_x, width_y - 1, width_z))
    position = first_x + jnp.arange(elements_x, dtype=jnp.int32)
    in_domain = (position >= 0) & (position <= total_x - 2)
    factor = jnp.where(in_domain[:, None, None], modulus_ext[:, :width_y - 1, :], 0.0)
    element_force = jnp.einsum("pq,qxyz->pxyz", stiffness, element_disp, precision=precise_mode) * factor[None]
    element_force = element_force.reshape((3, 8, elements_x, width_y - 1, width_z))
    internal = jnp.zeros(displacement_ext.shape, jnp.float32)
    for corner, (offset_x, offset_y, offset_z) in enumerate(corner_list()):
        contribution = jnp.roll(element_force[:, corner], offset_z, axis=3)
        internal = internal + jnp.pad(contribution, ((0, 0), (offset_x, 1 - offset_x), (offset_y, 1 - offset_y), (0, 0)))
    acceleration = (load_now - internal[:, 1:-1]) * inverse_mass
    new_velocity = velocity_now + step_size * acceleration
    new_displacement = displacement_ext[:, 1:-1] + step_size * new_velocity
    return new_displacement, new_velocity


def reference(displacement, velocity, external_load, node_mass, modulus, stiffness, substeps, interface_nodes, factor_inverse, factor_lower):
    final_disp = []
    final_velocity = []
    for substructure in range(2 * PAIRS):
        current_disp = displacement[substructure]
        current_velocity = velocity[substructure]
        element_mod = modulus[substructure]
        modulus_ext = jnp.concatenate([jnp.zeros((1, CY, CZ), jnp.float32), element_mod], axis=0)
        inverse_mass = 1.0 / node_mass[substructure]
        substep_count = substeps[substructure]
        step_size = coarse_step / substep_count.astype(jnp.float32)
        for substep in range(MAXSUB):
            displacement_ext = jnp.pad(current_disp, ((0, 0), (1, 1), (0, 0), (0, 0)))
            new_disp, new_velocity = advance(displacement_ext, current_velocity, external_load[substructure], inverse_mass, modulus_ext, stiffness, -1, NX, step_size)
            active = substep < substep_count
            current_disp = jnp.where(active, new_disp, current_disp)
            current_velocity = jnp.where(active, new_velocity, current_velocity)
        final_disp.append(current_disp)
        final_velocity.append(current_velocity)
    node_count = CX * CY * CZ
    slot_tile = jnp.arange(SLOTS, dtype=jnp.int32) // IFC
    coupled = []
    for pair_index in range(PAIRS):
        upper_side = 2 * pair_index
        other_side = upper_side + 1
        upper_nodes = (slot_tile * node_count + interface_nodes[upper_side]).astype(jnp.int32)
        other_nodes = (slot_tile * node_count + interface_nodes[other_side]).astype(jnp.int32)
        flat_upper = final_velocity[upper_side].reshape((3, -1))
        flat_other = final_velocity[other_side].reshape((3, -1))
        velocity_jump = jnp.take(flat_upper, upper_nodes, axis=1) - jnp.take(flat_other, other_nodes, axis=1)
        jump_blocks = velocity_jump.reshape((3, TILES, IFC)).transpose((1, 0, 2)).reshape((TILES, IB))
        inverse_blocks = factor_inverse[pair_index].reshape((TILES, IB, IB))
        lower_blocks = factor_lower[pair_index].reshape((TILES, IB, IB))

        def forward_step(previous, inputs):
            inverse_block, lower_block, jump_block = inputs
            current = jnp.dot(inverse_block, jump_block - jnp.dot(lower_block, previous, precision=precise_mode), precision=precise_mode)
            return current, current

        unused_last, solved = lax.scan(forward_step, jnp.zeros((IB,), jnp.float32), (inverse_blocks, lower_blocks, jump_blocks))

        def backward_step(carried, inputs):
            inverse_block, lower_block, solved_block = inputs
            multiplier = jnp.dot(inverse_block.T, solved_block - carried, precision=precise_mode)
            return jnp.dot(lower_block.T, multiplier, precision=precise_mode), multiplier

        unused_first, multipliers = lax.scan(backward_step, jnp.zeros((IB,), jnp.float32), (inverse_blocks, lower_blocks, solved), reverse=True)
        spread = multipliers.reshape((TILES, 3, IFC)).transpose((1, 0, 2)).reshape((3, SLOTS))
        upper_inverse = jnp.take((1.0 / node_mass[upper_side]).reshape(-1), upper_nodes)
        other_inverse = jnp.take((1.0 / node_mass[other_side]).reshape(-1), other_nodes)
        flat_upper = flat_upper.at[:, upper_nodes].add(-(spread * upper_inverse[None]))
        flat_other = flat_other.at[:, other_nodes].add(spread * other_inverse[None])
        coupled.append(flat_upper.reshape((3, NX, CY, CZ)))
        coupled.append(flat_other.reshape((3, NX, CY, CZ)))
    return jnp.stack(final_disp, axis=0), jnp.stack(coupled, axis=0)
```

```python
import jax
import jax.numpy as jnp
from jax import lax
from jax.experimental import pallas as pl
from jax.experimental.pallas import tpu as pltpu
from jax.sharding import PartitionSpec as P

MAXSUB = 4
IFC = 128
IB = 384
HALF = IB // 2
MASKS = (1, 2, 4, 12, 16, 48)
CORE, PAIR, SIDE = 0, 6, 7

precise_mode = lax.Precision.HIGHEST
coarse_step = 0.1
f32 = jnp.float32
bf16 = jnp.bfloat16
VM = pl.BlockSpec(memory_space=pltpu.VMEM)
SM = pl.BlockSpec(memory_space=pltpu.SMEM)
MAT = jax.ShapeDtypeStruct((IB, IB), f32)
HALFMAT = jax.ShapeDtypeStruct((HALF, IB), f32)
ROW = jax.ShapeDtypeStruct((1, IB), f32)


def swap(value, mask):
    return lax.ppermute(value, "tile", [(i, i ^ mask) for i in range(lax.axis_size("tile"))])


def cost(flops, nbytes):
    return pl.CostEstimate(flops=flops, bytes_accessed=nbytes, transcendentals=0)


def local_call(kernel, flags, operands, outs, flops=0):
    nbytes = sum(o.size * 4 for o in operands)
    return pl.pallas_call(
        kernel,
        out_shape=outs,
        in_specs=[SM] + [VM] * len(operands),
        out_specs=jax.tree.map(lambda _: VM, outs),
        cost_estimate=cost(flops, nbytes),
    )(flags, *operands)


def pair_call(kernel, flags, blocks, operands, outs, flops=0):
    count = len(operands)

    def whole(shape):
        return pl.BlockSpec(shape, lambda i, flags: (0,) * len(shape))

    many = isinstance(outs, (tuple, list))
    return pl.pallas_call(
        kernel,
        out_shape=outs,
        grid_spec=pltpu.PrefetchScalarGridSpec(
            num_scalar_prefetch=1,
            grid=(1,),
            in_specs=[pl.BlockSpec((1, IB, IB), lambda i, flags: (flags[PAIR], 0, 0)) for _ in blocks]
            + [whole(o.shape) for o in operands],
            out_specs=[whole(o.shape) for o in outs] if many else whole(outs.shape),
        ),
        cost_estimate=cost(flops, 4 * IB * IB * len(blocks) + sum(o.size * 4 for o in operands)),
    )(flags, *blocks, *operands)


def halves(value):
    high = value.astype(bf16)
    return high, (value - high.astype(f32)).astype(bf16)


def product(a, b):
    a_high, a_low = halves(a)
    b_high, b_low = halves(b)
    return (
        jnp.dot(a_low, b_high, preferred_element_type=f32)
        + jnp.dot(a_high, b_low, preferred_element_type=f32)
        + jnp.dot(a_high, b_high, preferred_element_type=f32)
    )


def eye_mask(size):
    return lax.broadcasted_iota(jnp.int32, (size, size), 0) == lax.broadcasted_iota(
        jnp.int32, (size, size), 1
    )


def column_to_row(column):
    eye = eye_mask(IFC)
    return jnp.concatenate(
        [
            jnp.sum(jnp.where(eye, column[k : k + IFC], 0.0), axis=0, keepdims=True)
            for k in range(0, IB, IFC)
        ],
        axis=1,
    )


def row_to_column(row):
    eye = eye_mask(IFC)
    return jnp.concatenate(
        [
            jnp.sum(jnp.where(eye, row[:, k : k + IFC], 0.0), axis=1, keepdims=True)
            for k in range(0, IB, IFC)
        ],
        axis=0,
    )


def apply(matrix, row):
    return column_to_row(jnp.sum(matrix * row, axis=1, keepdims=True))


def apply_transposed(matrix, row):
    return jnp.sum(matrix * row_to_column(row), axis=0, keepdims=True)


def transition_kernel(flags, inverse, lower, transition):
    transition[...] = -product(inverse[0], lower[0])


def store_half(flags, half, value_ref):
    @pl.when(flags[CORE] == 0)
    def _():
        half[...] = value_ref[:HALF]

    @pl.when(flags[CORE] == 1)
    def _():
        half[...] = value_ref[HALF:]


def first_merge_kernel(flags, own, other, high_ref, low_ref, merged, half, prefix, suffix):
    is_high = flags[0] == 1
    high = jnp.where(is_high, own[...], other[...])
    low = jnp.where(is_high, other[...], own[...])
    high_ref[...] = high
    low_ref[...] = low
    merged[...] = product(high, low)
    store_half(flags, half, merged)
    identity = eye_mask(IB).astype(f32)
    prefix[...] = jnp.where(is_high, other[...], identity)
    suffix[...] = jnp.where(is_high, identity, other[...])


def merge_kernel(level, last, flags, own, near, far, prefix, suffix, *outs):
    is_high = flags[level] == 1
    first = flags[CORE] == 0
    other = jnp.concatenate(
        [jnp.where(first, near[...], far[...]), jnp.where(first, far[...], near[...])], axis=0
    )
    high = jnp.where(is_high, own[...], other)
    low = jnp.where(is_high, other, own[...])
    high_ref, low_ref, new_prefix, new_suffix = outs[:4]
    high_ref[...] = high
    low_ref[...] = low
    if not last:
        merged, half = outs[4:]
        merged[...] = product(high, low)
        store_half(flags, half, merged)
    longer = product(
        jnp.where(is_high, prefix[...], high), jnp.where(is_high, low, suffix[...])
    )
    new_prefix[...] = jnp.where(is_high, longer, prefix[...])
    new_suffix[...] = jnp.where(is_high, suffix[...], longer)


def start_kernel(flags, inverse, picked, partner, offset):
    sign = (1 - 2 * flags[SIDE]).astype(f32)
    offset[...] = apply(inverse[0], sign * (picked[...] - partner[...]))


def forward_kernel(level, flags, own, other, high_matrix, total):
    is_high = flags[level] == 1
    high = jnp.where(is_high, own[...], other[...])
    low = jnp.where(is_high, other[...], own[...])
    total[...] = high + apply(high_matrix[...], low)


def backward_kernel(level, flags, own, other, low_matrix, total):
    is_high = flags[level] == 1
    high = jnp.where(is_high, own[...], other[...])
    low = jnp.where(is_high, other[...], own[...])
    total[...] = low + apply_transposed(low_matrix[...], high)


def gathered_kernel(wanted, operation, flags, *refs):
    others = refs[:5]
    matrices = refs[5:9]
    result = refs[9]
    result[...] = jnp.where(flags[0] == wanted, others[0][...], 0.0)
    for level in range(1, 5):

        @pl.when(flags[level] == wanted)
        def _():
            result[...] = result[...] + operation(matrices[level - 1][...], others[level][...])


def turn_kernel(flags, entering, other, prefix, transition, offset, solved, returning):
    before = entering[...] + jnp.where(flags[5] == 1, 1.0, 0.0) * apply(prefix[...], other[...])
    current = offset[...] + apply(transition[...], before)
    solved[...] = current
    returning[...] = -apply_transposed(transition[...], current)


def multiplier_kernel(flags, inverse, entering, other, suffix, solved, multiplier):
    after = entering[...] + jnp.where(flags[5] == 0, 1.0, 0.0) * apply_transposed(
        suffix[...], other[...]
    )
    multiplier[...] = apply_transposed(inverse[0], solved[...] - after)


def bound(level, kernel, *fixed):
    def run(*refs):
        kernel(level, *fixed, *refs)

    return run


def coupled_multipliers(flags, picked, factor_inverse, factor_lower):
    cube = 6 * IB**3
    square = 2 * IB * IB
    transition = pair_call(
        transition_kernel, flags, [factor_inverse, factor_lower], [], MAT, cube
    )
    other = swap(transition, MASKS[0])
    high, low, merged, half, prefix, suffix = local_call(
        first_merge_kernel,
        flags,
        [transition, other],
        (MAT, MAT, MAT, HALFMAT, MAT, MAT),
        cube,
    )
    highs, lows, prefixes, suffixes = [high], [low], [prefix], [suffix]
    for level in range(1, 5):
        last = level == 4
        near = swap(half, MASKS[level])
        far = swap(near, 1)
        outs = (MAT,) * 4 if last else (MAT,) * 5 + (HALFMAT,)
        made = local_call(
            bound(level, merge_kernel, last),
            flags,
            [merged, near, far, prefix, suffix],
            outs,
            2 * cube,
        )
        high, low, prefix, suffix = made[:4]
        if not last:
            merged, half = made[4:]
        highs.append(high)
        lows.append(low)
        prefixes.append(prefix)
        suffixes.append(suffix)

    count = lax.axis_size("sub")
    partner = lax.ppermute(picked, "sub", [(i, i ^ 1) for i in range(count)])
    offset = pair_call(start_kernel, flags, [factor_inverse], [picked, partner], ROW, square)
    total, others = offset, []
    for level in range(5):
        others.append(swap(total, MASKS[level]))
        total = local_call(
            bound(level, forward_kernel), flags, [total, others[-1], highs[level]], ROW, square
        )
    last_other = swap(total, MASKS[5])
    entering = local_call(
        bound(1, gathered_kernel, apply), flags, others + prefixes[:4], ROW, 4 * square
    )
    solved, returning = local_call(
        turn_kernel,
        flags,
        [entering, last_other, prefixes[4], transition, offset],
        (ROW, ROW),
        3 * square,
    )
    total, others = returning, []
    for level in range(5):
        others.append(swap(total, MASKS[level]))
        total = local_call(
            bound(level, backward_kernel), flags, [total, others[-1], lows[level]], ROW, square
        )
    last_other = swap(total, MASKS[5])
    entering = local_call(
        bound(0, gathered_kernel, apply_transposed), flags, others + suffixes[:4], ROW, 4 * square
    )
    return pair_call(
        multiplier_kernel,
        flags,
        [factor_inverse],
        [entering, last_other, suffixes[4], solved],
        ROW,
        2 * square,
    )


def shifted(value, axis, steps):
    count = lax.axis_size(axis)
    leading, last = (max(0, -steps), min(count, count - steps))
    return lax.ppermute(value, axis, [(source, source + steps) for source in range(leading, last)])


def padded(block, sides, width):
    for axis, dim in sides:
        count = lax.axis_size(axis)
        forward = [(i, i + 1) for i in range(count - 1)]
        backward = [(target, source) for source, target in forward]
        low = lax.ppermute(
            lax.slice_in_dim(block, block.shape[dim] - width, None, axis=dim), axis, forward
        )
        high = lax.ppermute(lax.slice_in_dim(block, 0, width, axis=dim), axis, backward)
        block = jnp.concatenate([low, block, high], axis=dim)
    return block


def corner_list():
    return [
        (offset_x, offset_y, offset_z)
        for offset_x in (0, 1)
        for offset_y in (0, 1)
        for offset_z in (0, 1)
    ]


def advance(
    displacement_ext,
    velocity_now,
    load_now,
    inverse_mass,
    modulus_ext,
    stiffness,
    first_x,
    total_x,
    step_size,
):
    layers = displacement_ext.shape[1]
    elements_x = layers - 1
    width_y = displacement_ext.shape[2]
    width_z = displacement_ext.shape[3]
    corners = []
    for offset_x, offset_y, offset_z in corner_list():
        corner_disp = displacement_ext[
            :, offset_x : offset_x + elements_x, offset_y : offset_y + width_y - 1, :
        ]
        corners.append(jnp.roll(corner_disp, -offset_z, axis=3))
    element_disp = jnp.stack(corners, axis=1).reshape((24, elements_x, width_y - 1, width_z))
    position = first_x + jnp.arange(elements_x, dtype=jnp.int32)
    in_domain = (position >= 0) & (position <= total_x - 2)
    factor = jnp.where(in_domain[:, None, None], modulus_ext[:, : width_y - 1, :], 0.0)
    element_force = (
        jnp.einsum("pq,qxyz->pxyz", stiffness, element_disp, precision=precise_mode) * factor[None]
    )
    element_force = element_force.reshape((3, 8, elements_x, width_y - 1, width_z))
    internal = jnp.zeros(displacement_ext.shape, jnp.float32)
    for corner, (offset_x, offset_y, offset_z) in enumerate(corner_list()):
        contribution = jnp.roll(element_force[:, corner], offset_z, axis=3)
        internal = internal + jnp.pad(
            contribution, ((0, 0), (offset_x, 1 - offset_x), (offset_y, 1 - offset_y), (0, 0))
        )
    acceleration = (load_now - internal[:, 1:-1]) * inverse_mass
    new_velocity = velocity_now + step_size * acceleration
    new_displacement = displacement_ext[:, 1:-1] + step_size * new_velocity
    return (new_displacement, new_velocity)


def body(
    displacement,
    velocity,
    external_load,
    node_mass,
    modulus,
    stiffness,
    substeps,
    interface_nodes,
    factor_inverse,
    factor_lower,
):
    current_disp = displacement[0]
    current_velocity = velocity[0]
    own_load = external_load[0]
    own_mass = node_mass[0]
    element_mod = modulus[0]
    width_x = current_disp.shape[1]
    tile_count = lax.axis_size("tile")
    total_x = width_x * tile_count
    first_layer = lax.axis_index("tile") * width_x
    substep_count = substeps[0]
    step_size = coarse_step / substep_count.astype(jnp.float32)
    below_row = shifted(element_mod[-1:], "tile", 1)
    modulus_ext = jnp.concatenate([below_row, element_mod], axis=0)
    inverse_mass = 1.0 / own_mass
    for substep in range(MAXSUB):
        displacement_ext = padded(current_disp, (("tile", 1),), 1)
        new_disp, new_velocity = advance(
            displacement_ext,
            current_velocity,
            own_load,
            inverse_mass,
            modulus_ext,
            stiffness,
            first_layer - 1,
            total_x,
            step_size,
        )
        active = substep < substep_count
        current_disp = jnp.where(active, new_disp, current_disp)
        current_velocity = jnp.where(active, new_velocity, current_velocity)
    flat_velocity = current_velocity.reshape((3, -1))
    slot_nodes = interface_nodes[0]
    picked = jnp.take(flat_velocity, slot_nodes, axis=1)
    sub, tile = lax.axis_index("sub"), lax.axis_index("tile")
    side_sign = (1 - 2 * (sub % 2)).astype(jnp.float32)
    flags = jnp.stack([(tile >> k) & 1 for k in range(6)] + [sub // 2, sub % 2]).astype(jnp.int32)
    multiplier = coupled_multipliers(flags, picked.reshape((1, -1)), factor_inverse, factor_lower)
    slot_inverse = jnp.take((1.0 / own_mass).reshape(-1), slot_nodes)
    correction = -side_sign * multiplier.reshape((3, -1)) * slot_inverse[None]
    flat_velocity = flat_velocity.at[:, slot_nodes].add(correction)
    coupled = flat_velocity.reshape(current_velocity.shape)
    return (current_disp[None], coupled[None])


def solution(mesh):
    in_specs = (
        P("sub", None, "tile", None, None),
        P("sub", None, "tile", None, None),
        P("sub", None, "tile", None, None),
        P("sub", "tile", None, None),
        P("sub", "tile", None, None),
        P(),
        P("sub"),
        P("sub", "tile"),
        P(None, "tile", None),
        P(None, "tile", None),
    )
    out_specs = (P("sub", None, "tile", None, None), P("sub", None, "tile", None, None))
    return jax.shard_map(body, mesh=mesh, in_specs=in_specs, out_specs=out_specs, check_vma=False)
```

```python
import jax
import jax.numpy as jnp
from jax import lax
from jax.experimental import pallas as pl
from jax.experimental.pallas import tpu as pltpu
from jax.sharding import PartitionSpec as P

IFC = 128
IB = 384
HALF = IB // 2
GRANT = 12 << 20
CX, CY, CZ = 4, 32, 128
DEEP = 3 * CX
FIELDS = 11
CORE, PAIR, SIDE, LAST, STEPS = 0, 6, 7, 8, 9
GROUPS = CY // 8
MASKS = (1, 2, 4, 12, 16, 48)

coarse_step = 0.1
f32 = jnp.float32
bf16 = jnp.bfloat16
VM = pl.BlockSpec(memory_space=pltpu.VMEM)
SM = pl.BlockSpec(memory_space=pltpu.SMEM)
MAT = jax.ShapeDtypeStruct((IB, IB), f32)
HALFMAT = jax.ShapeDtypeStruct((HALF, IB), f32)
ROW = jax.ShapeDtypeStruct((1, IB), f32)


def swap(value, mask):
    return lax.ppermute(value, "tile", [(i, i ^ mask) for i in range(lax.axis_size("tile"))])


def cost(flops, nbytes):
    return pl.CostEstimate(flops=flops, bytes_accessed=nbytes, transcendentals=0)


def local_call(kernel, flags, operands, outs, flops=0):
    nbytes = sum(o.size * 4 for o in operands)
    return pl.pallas_call(
        kernel,
        out_shape=outs,
        in_specs=[SM] + [VM] * len(operands),
        out_specs=jax.tree.map(lambda _: VM, outs),
        compiler_params=pltpu.CompilerParams(vmem_limit_bytes=GRANT),
        cost_estimate=cost(flops, nbytes),
    )(flags, *operands)


def pair_call(kernel, flags, blocks, operands, outs, flops=0):
    count = len(operands)

    def whole(shape):
        return pl.BlockSpec(shape, lambda i, flags: (0,) * len(shape))

    many = isinstance(outs, (tuple, list))
    return pl.pallas_call(
        kernel,
        out_shape=outs,
        grid_spec=pltpu.PrefetchScalarGridSpec(
            num_scalar_prefetch=1,
            grid=(1,),
            in_specs=[pl.BlockSpec((1, IB, IB), lambda i, flags: (flags[PAIR], 0, 0)) for _ in blocks]
            + [whole(o.shape) for o in operands],
            out_specs=[whole(o.shape) for o in outs] if many else whole(outs.shape),
        ),
        compiler_params=pltpu.CompilerParams(vmem_limit_bytes=GRANT),
        cost_estimate=cost(flops, 4 * IB * IB * len(blocks) + sum(o.size * 4 for o in operands)),
    )(flags, *blocks, *operands)


def halves(value):
    high = value.astype(bf16)
    return high, (value - high.astype(f32)).astype(bf16)


def product(a, b):
    a_high, a_low = halves(a)
    b_high, b_low = halves(b)
    return (
        jnp.dot(a_low, b_high, preferred_element_type=f32)
        + jnp.dot(a_high, b_low, preferred_element_type=f32)
        + jnp.dot(a_high, b_high, preferred_element_type=f32)
    )


def eye_mask(size):
    return lax.broadcasted_iota(jnp.int32, (size, size), 0) == lax.broadcasted_iota(
        jnp.int32, (size, size), 1
    )


def column_to_row(column):
    eye = eye_mask(IFC)
    return jnp.concatenate(
        [
            jnp.sum(jnp.where(eye, column[k : k + IFC], 0.0), axis=0, keepdims=True)
            for k in range(0, IB, IFC)
        ],
        axis=1,
    )


def row_to_column(row):
    eye = eye_mask(IFC)
    return jnp.concatenate(
        [
            jnp.sum(jnp.where(eye, row[:, k : k + IFC], 0.0), axis=1, keepdims=True)
            for k in range(0, IB, IFC)
        ],
        axis=0,
    )


def apply(matrix, row):
    return column_to_row(jnp.sum(matrix * row, axis=1, keepdims=True))


def apply_transposed(matrix, row):
    return jnp.sum(matrix * row_to_column(row), axis=0, keepdims=True)


def triple(value):
    high = value.astype(bf16)
    rest = value - high.astype(f32)
    middle = rest.astype(bf16)
    return high, middle, (rest - middle.astype(f32)).astype(bf16)


def slot_masks(nodes):
    index = lax.broadcasted_iota(jnp.int32, (IFC, IFC), 0)
    return index == nodes // CZ, index == nodes % CZ


def wide(value):
    return jnp.concatenate([value[8 * g : 8 * g + 8] for g in range(GROUPS)], axis=1)


def tall(value):
    return jnp.concatenate([value[:, CZ * g : CZ * g + CZ] for g in range(GROUPS)], axis=0)


def spread(values, parity):
    row = lax.broadcasted_iota(jnp.int32, (192, 24), 0) // 8
    rows = (row == lax.broadcasted_iota(jnp.int32, (192, 24), 1)).astype(f32).astype(bf16)
    block = lax.broadcasted_iota(jnp.int32, (24, 192), 1) // 8
    side = (block // 12 + parity) % 2
    dof = 8 * (block % 12 // 4) + 4 * side + block % 4
    columns = (dof == lax.broadcasted_iota(jnp.int32, (24, 192), 0)).astype(f32).astype(bf16)
    tall_values = jnp.dot(rows, values, preferred_element_type=f32).astype(bf16)
    full = jnp.dot(tall_values, columns, preferred_element_type=f32)
    same = (
        lax.broadcasted_iota(jnp.int32, (192, 192), 0) % 8
        == lax.broadcasted_iota(jnp.int32, (192, 192), 1) % 8
    )
    return jnp.where(same, full, 0.0).astype(bf16)


def substep_kernel(
    flags, step, own, outer, inner, stiffness, nodes,
    displacement_out, velocity_out, picked,
    disp, vel, load, inverse_mass, factor, stiff, features, upper,
):
    first = flags[CORE] == 0

    def place(source, low):
        layers = pl.ds(low, CX)
        for i in range(3):
            disp[i, layers] = source[pl.ds(CX * i, CX)]
            vel[i, layers] = source[pl.ds(CX * (3 + i), CX)]
            load[i, layers] = source[pl.ds(CX * (6 + i), CX)]
        mass = source[pl.ds(CX * 9, CX)]
        present = mass > 0.0
        inverse_mass[layers] = jnp.where(present, 1.0 / jnp.where(present, mass, 1.0), 0.0)
        for x in range(CX):
            value = source[CX * 10 + x]
            row = lax.broadcasted_iota(jnp.int32, (CY, CZ), 0)
            factor[low + x] = wide(jnp.where(row < CY - 1, value, 0.0))

    place(own, CX)

    @pl.when(first)
    def _():
        place(outer, 0)
        place(inner, 2 * CX)

    @pl.when(jnp.logical_not(first))
    def _():
        place(inner, 0)
        place(outer, 2 * CX)

    @pl.when(flags[LAST] == 1)
    def _():
        factor[2 * CX - 1] = jnp.zeros((8, GROUPS * CZ), f32)

    for parity in range(2):
        high, low = [spread(s, parity) for s in halves(stiffness[...])]
        stiff[parity] = jnp.concatenate([high, high, low], axis=1)
    length = step[0]

    def put_features(layer, parity):
        columns = []
        for i in range(3):
            base = disp[i, layer]
            turned = pltpu.roll(base, CZ - 1, 1)
            columns += [base, turned, pltpu.roll(base, CY - 1, 0), pltpu.roll(turned, CY - 1, 0)]
        start = pl.multiple_of(parity * 96, 16)
        for g in range(GROUPS):
            lanes = pl.ds(CZ * g, CZ)
            block = jnp.concatenate([c[8 * g : 8 * g + 8] for c in columns], axis=0)
            high, low = halves(block)
            features[pl.ds(start, 96), lanes] = high
            features[pl.ds(start + 192, 96), lanes] = low
            features[pl.ds(start + 384, 96), lanes] = high

    def element_layer(layer, finish):
        parity = layer % 2
        put_features(layer + 1, 1 - parity)
        force = jnp.dot(stiff[parity], features[...], preferred_element_type=f32)
        scale = factor[layer]
        weight = inverse_mass[layer]

        def corner(i, a, b, c):
            start = 8 * (8 * i + 4 * a + 2 * b + c)
            return force[start : start + 8] * scale

        for i in range(3):
            if finish:
                sums = [corner(i, 0, r // 2, r % 2) + upper[4 * i + r] for r in range(4)]
                s00, s01, s10, s11 = [tall(s) for s in sums]
                base = s00 + pltpu.roll(s10, 1, 0)
                turned = s01 + pltpu.roll(s11, 1, 0)
                internal = base + pltpu.roll(turned, 1, 1)
                speed = vel[i, layer] + length * ((load[i, layer] - internal) * weight)
                vel[i, layer] = speed
                disp[i, layer] = disp[i, layer] + length * speed
            for r in range(4):
                upper[4 * i + r] = corner(i, 1, r // 2, r % 2)

    def one_substep(k, carry):
        put_features(k, k % 2)
        element_layer(k, False)

        def inner_layer(layer, carry):
            element_layer(layer, True)
            return carry

        return lax.fori_loop(k + 1, DEEP - 1 - k, inner_layer, carry)

    lax.fori_loop(0, flags[STEPS], one_substep, 0)
    displacement_out[...] = disp[:, CX : 2 * CX]
    final = vel[:, CX : 2 * CX]
    velocity_out[...] = final
    in_row, in_column = slot_masks(nodes[...])
    chosen = in_column.astype(f32).astype(bf16)
    parts = []
    for i in range(3):
        pieces = triple(final[i].reshape(CX * CY, CZ))
        values = sum(jnp.dot(p, chosen, preferred_element_type=f32) for p in reversed(pieces))
        parts.append(jnp.sum(jnp.where(in_row, values, 0.0), axis=0, keepdims=True))
    picked[...] = jnp.concatenate(parts, axis=1)


def substeps_call(flags, step, own, outer, inner, stiffness, nodes):
    grid_shape = (3, CX, CY, CZ)
    return pl.pallas_call(
        substep_kernel,
        out_shape=(
            jax.ShapeDtypeStruct(grid_shape, f32),
            jax.ShapeDtypeStruct(grid_shape, f32),
            ROW,
        ),
        in_specs=[SM, SM] + [VM] * 5,
        out_specs=(VM, VM, VM),
        scratch_shapes=[
            pltpu.VMEM((3, DEEP, CY, CZ), f32),
            pltpu.VMEM((3, DEEP, CY, CZ), f32),
            pltpu.VMEM((3, DEEP, CY, CZ), f32),
            pltpu.VMEM((DEEP, CY, CZ), f32),
            pltpu.VMEM((DEEP, 8, GROUPS * CZ), f32),
            pltpu.VMEM((2, 192, 576), bf16),
            pltpu.VMEM((576, GROUPS * CZ), bf16),
            pltpu.VMEM((12, 8, GROUPS * CZ), f32),
        ],
        compiler_params=pltpu.CompilerParams(vmem_limit_bytes=20 << 20),
        cost_estimate=cost(32 * 2 * 192 * 576 * 512, 3 * 720896),
    )(flags, step, own, outer, inner, stiffness, nodes)

def transition_kernel(flags, inverse, lower, transition):
    transition[...] = -product(inverse[0], lower[0])


def store_half(flags, half, value_ref):
    @pl.when(flags[CORE] == 0)
    def _():
        half[...] = value_ref[:HALF]

    @pl.when(flags[CORE] == 1)
    def _():
        half[...] = value_ref[HALF:]


def first_merge_kernel(flags, own, other, high_ref, low_ref, merged, half, prefix, suffix):
    is_high = flags[0] == 1
    high = jnp.where(is_high, own[...], other[...])
    low = jnp.where(is_high, other[...], own[...])
    high_ref[...] = high
    low_ref[...] = low
    merged[...] = product(high, low)
    store_half(flags, half, merged)
    identity = eye_mask(IB).astype(f32)
    prefix[...] = jnp.where(is_high, other[...], identity)
    suffix[...] = jnp.where(is_high, identity, other[...])


def merge_kernel(level, last, flags, own, near, far, prefix, suffix, *outs):
    is_high = flags[level] == 1
    first = flags[CORE] == 0
    other = jnp.concatenate(
        [jnp.where(first, near[...], far[...]), jnp.where(first, far[...], near[...])], axis=0
    )
    high = jnp.where(is_high, own[...], other)
    low = jnp.where(is_high, other, own[...])
    high_ref, low_ref, new_prefix, new_suffix = outs[:4]
    high_ref[...] = high
    low_ref[...] = low
    if not last:
        merged, half = outs[4:]
        merged[...] = product(high, low)
        store_half(flags, half, merged)
    longer = product(
        jnp.where(is_high, prefix[...], high), jnp.where(is_high, low, suffix[...])
    )
    new_prefix[...] = jnp.where(is_high, longer, prefix[...])
    new_suffix[...] = jnp.where(is_high, suffix[...], longer)


def start_kernel(flags, inverse, picked, partner, offset):
    sign = (1 - 2 * flags[SIDE]).astype(f32)
    offset[...] = apply(inverse[0], sign * (picked[...] - partner[...]))


def forward_kernel(level, flags, own, other, high_matrix, total):
    is_high = flags[level] == 1
    high = jnp.where(is_high, own[...], other[...])
    low = jnp.where(is_high, other[...], own[...])
    total[...] = high + apply(high_matrix[...], low)


def backward_kernel(level, flags, own, other, low_matrix, total):
    is_high = flags[level] == 1
    high = jnp.where(is_high, own[...], other[...])
    low = jnp.where(is_high, other[...], own[...])
    total[...] = low + apply_transposed(low_matrix[...], high)


def gathered_kernel(wanted, operation, flags, *refs):
    others = refs[:5]
    matrices = refs[5:9]
    result = refs[9]
    result[...] = jnp.where(flags[0] == wanted, others[0][...], 0.0)
    for level in range(1, 5):

        @pl.when(flags[level] == wanted)
        def _():
            result[...] = result[...] + operation(matrices[level - 1][...], others[level][...])


def turn_kernel(flags, entering, other, prefix, transition, offset, solved, returning):
    before = entering[...] + jnp.where(flags[5] == 1, 1.0, 0.0) * apply(prefix[...], other[...])
    current = offset[...] + apply(transition[...], before)
    solved[...] = current
    returning[...] = -apply_transposed(transition[...], current)


def finish_kernel(
    flags, inverse, entering, other, suffix, solved, velocity, node_mass, nodes, velocity_out
):
    after = entering[...] + jnp.where(flags[5] == 0, 1.0, 0.0) * apply_transposed(
        suffix[...], other[...]
    )
    sign = (1 - 2 * flags[SIDE]).astype(f32)
    multiplier = sign * apply_transposed(inverse[0], solved[...] - after)
    in_row, in_column = slot_masks(nodes[...])
    chosen = in_column.astype(f32).astype(bf16)
    weight = 1.0 / node_mass[...]
    for i in range(3):
        held = jnp.where(in_row, multiplier[:, IFC * i : IFC * i + IFC], 0.0)
        change = sum(
            lax.dot_general(p, chosen, (((1,), (1,)), ((), ())), preferred_element_type=f32)
            for p in reversed(triple(held))
        )
        velocity_out[i] = velocity[i] - change.reshape(CX, CY, CZ) * weight


def bound(level, kernel, *fixed):
    def run(*refs):
        kernel(level, *fixed, *refs)

    return run


def first_products(flags, factor_inverse, factor_lower):
    cube = 6 * IB**3
    transition = pair_call(
        transition_kernel, flags, [factor_inverse, factor_lower], [], MAT, cube
    )
    other = swap(transition, MASKS[0])
    high, low, merged, half, prefix, suffix = local_call(
        first_merge_kernel,
        flags,
        [transition, other],
        (MAT, MAT, MAT, HALFMAT, MAT, MAT),
        cube,
    )
    return transition, (merged, half), [(high, low, prefix, suffix)]


def merge_level(flags, level, block, levels, gate=None):
    merged, half = block
    near = swap(half, MASKS[level])
    far = swap(near, 1)
    if gate is not None:
        far, _ = lax.optimization_barrier((far, gate))
    last = level == 4
    made = local_call(
        bound(level, merge_kernel, last),
        flags,
        [merged, near, far, *levels[-1][2:]],
        (MAT,) * 4 if last else (MAT,) * 5 + (HALFMAT,),
        12 * IB**3,
    )
    return made[4:], levels + [tuple(made[:4])]


def coupled_velocity(
    flags, picked, factor_inverse, transition, block, levels, velocity, node_mass, nodes
):
    square = 2 * IB * IB
    count = lax.axis_size("sub")
    partner = lax.ppermute(picked, "sub", [(i, i ^ 1) for i in range(count)])
    offset = pair_call(start_kernel, flags, [factor_inverse], [picked, partner], ROW, square)
    total, others = offset, []
    for level in range(5):
        others.append(swap(total, MASKS[level]))
        if level >= 2:
            gate = picked if level == 2 else total
            block, levels = merge_level(flags, level, block, levels, gate)
        total = local_call(
            bound(level, forward_kernel), flags, [total, others[-1], levels[level][0]], ROW, square
        )
    _, lows, prefixes, suffixes = zip(*levels)
    last_other = swap(total, MASKS[5])
    entering = local_call(
        bound(1, gathered_kernel, apply), flags, others + list(prefixes[:4]), ROW, 4 * square
    )
    solved, returning = local_call(
        turn_kernel,
        flags,
        [entering, last_other, prefixes[4], transition, offset],
        (ROW, ROW),
        3 * square,
    )
    total, others = returning, []
    for level in range(5):
        others.append(swap(total, MASKS[level]))
        total = local_call(
            bound(level, backward_kernel), flags, [total, others[-1], lows[level]], ROW, square
        )
    last_other = swap(total, MASKS[5])
    entering = local_call(
        bound(0, gathered_kernel, apply_transposed), flags, others + list(suffixes[:4]), ROW, 4 * square
    )
    return pair_call(
        finish_kernel,
        flags,
        [factor_inverse],
        [entering, last_other, suffixes[4], solved, velocity, node_mass, nodes],
        jax.ShapeDtypeStruct(velocity.shape, f32),
        2 * square,
    )


def outer_swap(value):
    count = lax.axis_size("tile")
    route = []
    for low in range(1, count - 1, 2):
        route += [(low, low + 1), (low + 1, low)]
    return lax.ppermute(value, "tile", route)


def body(
    displacement,
    velocity,
    external_load,
    node_mass,
    modulus,
    stiffness,
    substeps,
    interface_nodes,
    factor_inverse,
    factor_lower,
):
    sub, tile = lax.axis_index("sub"), lax.axis_index("tile")
    last = tile == lax.axis_size("tile") - 1
    flags = jnp.stack(
        [(tile >> k) & 1 for k in range(6)] + [sub // 2, sub % 2, last, substeps[0]]
    ).astype(jnp.int32)
    step = coarse_step / substeps.astype(f32)
    own = jnp.concatenate(
        [
            displacement.reshape(-1, CY, CZ),
            velocity.reshape(-1, CY, CZ),
            external_load.reshape(-1, CY, CZ),
            node_mass[0],
            modulus[0],
        ],
        axis=0,
    )
    own, factor_inverse, factor_lower = lax.optimization_barrier((own, factor_inverse, factor_lower))
    outer = outer_swap(own)
    inner = swap(own, 1)
    transition, block, levels = first_products(flags, factor_inverse, factor_lower)
    block, levels = merge_level(flags, 1, block, levels)
    outer, inner, block = lax.optimization_barrier((outer, inner, block))
    final_displacement, final_velocity, picked = substeps_call(
        flags, step, own, outer, inner, stiffness, interface_nodes
    )
    coupled = coupled_velocity(
        flags,
        picked,
        factor_inverse,
        transition,
        block,
        levels,
        final_velocity,
        node_mass[0],
        interface_nodes,
    )
    return final_displacement[None], coupled[None]


def solution(mesh):
    in_specs = (
        P("sub", None, "tile", None, None),
        P("sub", None, "tile", None, None),
        P("sub", None, "tile", None, None),
        P("sub", "tile", None, None),
        P("sub", "tile", None, None),
        P(),
        P("sub"),
        P("sub", "tile"),
        P(None, "tile", None),
        P(None, "tile", None),
    )
    out_specs = (P("sub", None, "tile", None, None), P("sub", None, "tile", None, None))
    return jax.shard_map(body, mesh=mesh, in_specs=in_specs, out_specs=out_specs, check_vma=False)
```

```python
import jax
import jax.numpy as jnp
from jax import lax
from jax.experimental import pallas as pl
from jax.experimental.pallas import tpu as pltpu
from jax.sharding import PartitionSpec as P

IFC = 128
IB = 384
HALF = IB // 2
GRANT = 12 << 20
CX, CY, CZ = 4, 32, 128
DEEP = 3 * CX
NEAR = CX - 1
PACKED = 37
CORE, PAIR, SIDE, LAST, STEPS = 0, 6, 7, 8, 9
GROUPS = CY // 8
MASKS = (1, 2, 4, 12, 16, 48)

coarse_step = 0.1
f32 = jnp.float32
bf16 = jnp.bfloat16
VM = pl.BlockSpec(memory_space=pltpu.VMEM)
SM = pl.BlockSpec(memory_space=pltpu.SMEM)
MAT = jax.ShapeDtypeStruct((IB, IB), f32)
HALFMAT = jax.ShapeDtypeStruct((HALF, IB), f32)
ROW = jax.ShapeDtypeStruct((1, IB), f32)


def swap(value, mask):
    return lax.ppermute(value, "tile", [(i, i ^ mask) for i in range(lax.axis_size("tile"))])


def cost(flops, nbytes):
    return pl.CostEstimate(flops=flops, bytes_accessed=nbytes, transcendentals=0)


def local_call(kernel, flags, operands, outs, flops=0):
    nbytes = sum(o.size * 4 for o in operands)
    return pl.pallas_call(
        kernel,
        out_shape=outs,
        in_specs=[SM] + [VM] * len(operands),
        out_specs=jax.tree.map(lambda _: VM, outs),
        compiler_params=pltpu.CompilerParams(vmem_limit_bytes=GRANT),
        cost_estimate=cost(flops, nbytes),
    )(flags, *operands)


def pair_call(kernel, flags, blocks, operands, outs, flops=0):
    count = len(operands)

    def whole(shape):
        return pl.BlockSpec(shape, lambda i, flags: (0,) * len(shape))

    many = isinstance(outs, (tuple, list))
    return pl.pallas_call(
        kernel,
        out_shape=outs,
        grid_spec=pltpu.PrefetchScalarGridSpec(
            num_scalar_prefetch=1,
            grid=(1,),
            in_specs=[pl.BlockSpec((1, IB, IB), lambda i, flags: (flags[PAIR], 0, 0)) for _ in blocks]
            + [whole(o.shape) for o in operands],
            out_specs=[whole(o.shape) for o in outs] if many else whole(outs.shape),
        ),
        compiler_params=pltpu.CompilerParams(vmem_limit_bytes=GRANT),
        cost_estimate=cost(flops, 4 * IB * IB * len(blocks) + sum(o.size * 4 for o in operands)),
    )(flags, *blocks, *operands)


def halves(value):
    high = value.astype(bf16)
    return high, (value - high.astype(f32)).astype(bf16)


def product(a, b):
    a_high, a_low = halves(a)
    b_high, b_low = halves(b)
    return (
        jnp.dot(a_low, b_high, preferred_element_type=f32)
        + jnp.dot(a_high, b_low, preferred_element_type=f32)
        + jnp.dot(a_high, b_high, preferred_element_type=f32)
    )


def eye_mask(size):
    return lax.broadcasted_iota(jnp.int32, (size, size), 0) == lax.broadcasted_iota(
        jnp.int32, (size, size), 1
    )


def column_to_row(column):
    eye = eye_mask(IFC)
    return jnp.concatenate(
        [
            jnp.sum(jnp.where(eye, column[k : k + IFC], 0.0), axis=0, keepdims=True)
            for k in range(0, IB, IFC)
        ],
        axis=1,
    )


def row_to_column(row):
    eye = eye_mask(IFC)
    return jnp.concatenate(
        [
            jnp.sum(jnp.where(eye, row[:, k : k + IFC], 0.0), axis=1, keepdims=True)
            for k in range(0, IB, IFC)
        ],
        axis=0,
    )


def apply(matrix, row):
    return column_to_row(jnp.sum(matrix * row, axis=1, keepdims=True))


def apply_transposed(matrix, row):
    return jnp.sum(matrix * row_to_column(row), axis=0, keepdims=True)


def triple(value):
    high = value.astype(bf16)
    rest = value - high.astype(f32)
    middle = rest.astype(bf16)
    return high, middle, (rest - middle.astype(f32)).astype(bf16)


def slot_masks(nodes):
    index = lax.broadcasted_iota(jnp.int32, (IFC, IFC), 0)
    return index == nodes // CZ, index == nodes % CZ


def wide(value):
    return jnp.concatenate([value[8 * g : 8 * g + 8] for g in range(GROUPS)], axis=1)


def tall(value):
    return jnp.concatenate([value[:, CZ * g : CZ * g + CZ] for g in range(GROUPS)], axis=0)


def spread(values, parity):
    row = lax.broadcasted_iota(jnp.int32, (192, 24), 0) // 8
    rows = (row == lax.broadcasted_iota(jnp.int32, (192, 24), 1)).astype(f32).astype(bf16)
    block = lax.broadcasted_iota(jnp.int32, (24, 192), 1) // 8
    side = (block // 12 + parity) % 2
    dof = 8 * (block % 12 // 4) + 4 * side + block % 4
    columns = (dof == lax.broadcasted_iota(jnp.int32, (24, 192), 0)).astype(f32).astype(bf16)
    tall_values = jnp.dot(rows, values, preferred_element_type=f32).astype(bf16)
    full = jnp.dot(tall_values, columns, preferred_element_type=f32)
    same = (
        lax.broadcasted_iota(jnp.int32, (192, 192), 0) % 8
        == lax.broadcasted_iota(jnp.int32, (192, 192), 1) % 8
    )
    return jnp.where(same, full, 0.0).astype(bf16)


def substep_kernel(
    flags, step, displacement, velocity, external_load, node_mass, modulus,
    outer, inner, stiffness, nodes,
    displacement_out, velocity_out, picked,
    disp, vel, load, inverse_mass, factor, stiff, features, upper,
):
    first = flags[CORE] == 0

    def put_mass(low, mass):
        present = mass > 0.0
        inverse_mass[pl.ds(low, mass.shape[0])] = jnp.where(
            present, 1.0 / jnp.where(present, mass, 1.0), 0.0
        )

    def put_factor(low, source, base):
        row = lax.broadcasted_iota(jnp.int32, (CY, CZ), 0)
        for x in range(CX):
            factor[low + x] = wide(jnp.where(row < CY - 1, source[base + x], 0.0))

    def place(source, low, shift):
        for i in range(3):
            disp[i, pl.ds(low, CX)] = source[pl.ds(CX * i, CX)]
            vel[i, pl.ds(low + shift, NEAR)] = source[pl.ds(12 + NEAR * i, NEAR)]
            load[i, pl.ds(low + shift, NEAR)] = source[pl.ds(21 + NEAR * i, NEAR)]
        put_mass(low + shift, source[pl.ds(30, NEAR)])
        put_factor(low, source, 33)

    disp[:, CX : 2 * CX] = displacement[...]
    vel[:, CX : 2 * CX] = velocity[...]
    load[:, CX : 2 * CX] = external_load[...]
    put_mass(CX, node_mass[...])
    put_factor(CX, modulus, 0)

    @pl.when(first)
    def _():
        place(outer, 0, 1)
        place(inner, 2 * CX, 0)

    @pl.when(jnp.logical_not(first))
    def _():
        place(inner, 0, 1)
        place(outer, 2 * CX, 0)

    @pl.when(flags[LAST] == 1)
    def _():
        factor[2 * CX - 1] = jnp.zeros((8, GROUPS * CZ), f32)

    for parity in range(2):
        high, low = [spread(s, parity) for s in halves(stiffness[...])]
        stiff[parity] = jnp.concatenate([high, high, low], axis=1)
    length = step[0]

    def put_features(layer, parity):
        columns = []
        for i in range(3):
            base = disp[i, layer]
            turned = pltpu.roll(base, CZ - 1, 1)
            columns += [base, turned, pltpu.roll(base, CY - 1, 0), pltpu.roll(turned, CY - 1, 0)]
        start = pl.multiple_of(parity * 96, 16)
        for g in range(GROUPS):
            lanes = pl.ds(CZ * g, CZ)
            block = jnp.concatenate([c[8 * g : 8 * g + 8] for c in columns], axis=0)
            high, low = halves(block)
            features[pl.ds(start, 96), lanes] = high
            features[pl.ds(start + 192, 96), lanes] = low
            features[pl.ds(start + 384, 96), lanes] = high

    def element_layer(layer, finish):
        parity = layer % 2
        put_features(layer + 1, 1 - parity)
        force = jnp.dot(stiff[parity], features[...], preferred_element_type=f32)
        scale = factor[layer]
        weight = inverse_mass[layer]

        def corner(i, a, b, c):
            start = 8 * (8 * i + 4 * a + 2 * b + c)
            return force[start : start + 8] * scale

        for i in range(3):
            if finish:
                sums = [corner(i, 0, r // 2, r % 2) + upper[4 * i + r] for r in range(4)]
                s00, s01, s10, s11 = [tall(s) for s in sums]
                base = s00 + pltpu.roll(s10, 1, 0)
                turned = s01 + pltpu.roll(s11, 1, 0)
                internal = base + pltpu.roll(turned, 1, 1)
                speed = vel[i, layer] + length * ((load[i, layer] - internal) * weight)
                vel[i, layer] = speed
                disp[i, layer] = disp[i, layer] + length * speed
            for r in range(4):
                upper[4 * i + r] = corner(i, 1, r // 2, r % 2)

    def one_substep(k, carry):
        put_features(k, k % 2)
        element_layer(k, False)

        def inner_layer(layer, carry):
            element_layer(layer, True)
            return carry

        return lax.fori_loop(k + 1, DEEP - 1 - k, inner_layer, carry)

    lax.fori_loop(0, flags[STEPS], one_substep, 0)
    displacement_out[...] = disp[:, CX : 2 * CX]
    final = vel[:, CX : 2 * CX]
    velocity_out[...] = final
    in_row, in_column = slot_masks(nodes[...])
    chosen = in_column.astype(f32).astype(bf16)
    parts = []
    for i in range(3):
        pieces = triple(final[i].reshape(CX * CY, CZ))
        values = sum(jnp.dot(p, chosen, preferred_element_type=f32) for p in reversed(pieces))
        parts.append(jnp.sum(jnp.where(in_row, values, 0.0), axis=0, keepdims=True))
    picked[...] = jnp.concatenate(parts, axis=1)


def pack_kernel(flags, displacement, velocity, external_load, node_mass, modulus, outer, inner):
    for target, start in ((outer, flags[CORE]), (inner, 1 - flags[CORE])):
        for i in range(3):
            target[pl.ds(CX * i, CX)] = displacement[i]
            target[pl.ds(12 + NEAR * i, NEAR)] = velocity[i, pl.ds(start, NEAR)]
            target[pl.ds(21 + NEAR * i, NEAR)] = external_load[i, pl.ds(start, NEAR)]
        target[pl.ds(30, NEAR)] = node_mass[pl.ds(start, NEAR)]
        target[pl.ds(33, CX)] = modulus[...]


def substeps_call(flags, step, state, outer, inner, stiffness, nodes):
    grid_shape = (3, CX, CY, CZ)
    return pl.pallas_call(
        substep_kernel,
        out_shape=(
            jax.ShapeDtypeStruct(grid_shape, f32),
            jax.ShapeDtypeStruct(grid_shape, f32),
            ROW,
        ),
        in_specs=[SM, SM] + [VM] * 9,
        out_specs=(VM, VM, VM),
        scratch_shapes=[
            pltpu.VMEM((3, DEEP, CY, CZ), f32),
            pltpu.VMEM((3, DEEP, CY, CZ), f32),
            pltpu.VMEM((3, DEEP, CY, CZ), f32),
            pltpu.VMEM((DEEP, CY, CZ), f32),
            pltpu.VMEM((DEEP, 8, GROUPS * CZ), f32),
            pltpu.VMEM((2, 192, 576), bf16),
            pltpu.VMEM((576, GROUPS * CZ), bf16),
            pltpu.VMEM((12, 8, GROUPS * CZ), f32),
        ],
        compiler_params=pltpu.CompilerParams(vmem_limit_bytes=20 << 20),
        cost_estimate=cost(32 * 2 * 192 * 576 * 512, 3 * 720896),
    )(flags, step, *state, outer, inner, stiffness, nodes)

def transition_kernel(flags, inverse, lower, transition):
    transition[...] = -product(inverse[0], lower[0])


def store_half(flags, half, value_ref):
    @pl.when(flags[CORE] == 0)
    def _():
        half[...] = value_ref[:HALF]

    @pl.when(flags[CORE] == 1)
    def _():
        half[...] = value_ref[HALF:]


def first_merge_kernel(flags, own, other, high_ref, low_ref, merged, half):
    is_high = flags[0] == 1
    high = jnp.where(is_high, own[...], other[...])
    low = jnp.where(is_high, other[...], own[...])
    high_ref[...] = high
    low_ref[...] = low
    merged[...] = product(high, low)
    store_half(flags, half, merged)


def first_reach_kernel(flags, other, prefix, suffix):
    is_high = flags[0] == 1
    identity = eye_mask(IB).astype(f32)
    prefix[...] = jnp.where(is_high, other[...], identity)
    suffix[...] = jnp.where(is_high, identity, other[...])


def merge_kernel(level, last, flags, own, near, far, high_ref, low_ref, *outs):
    is_high = flags[level] == 1
    first = flags[CORE] == 0
    other = jnp.concatenate(
        [jnp.where(first, near[...], far[...]), jnp.where(first, far[...], near[...])], axis=0
    )
    high = jnp.where(is_high, own[...], other)
    low = jnp.where(is_high, other, own[...])
    high_ref[...] = high
    low_ref[...] = low
    if not last:
        merged, half = outs
        merged[...] = product(high, low)
        store_half(flags, half, merged)


def reach_kernel(level, flags, high, low, prefix, suffix, new_prefix, new_suffix):
    is_high = flags[level] == 1
    longer = product(
        jnp.where(is_high, prefix[...], high[...]), jnp.where(is_high, low[...], suffix[...])
    )
    new_prefix[...] = jnp.where(is_high, longer, prefix[...])
    new_suffix[...] = jnp.where(is_high, suffix[...], longer)


def start_kernel(flags, inverse, picked, partner, offset):
    sign = (1 - 2 * flags[SIDE]).astype(f32)
    offset[...] = apply(inverse[0], sign * (picked[...] - partner[...]))


def forward_kernel(level, flags, own, other, high_matrix, total):
    is_high = flags[level] == 1
    high = jnp.where(is_high, own[...], other[...])
    low = jnp.where(is_high, other[...], own[...])
    total[...] = high + apply(high_matrix[...], low)


def backward_kernel(level, flags, own, other, low_matrix, total):
    is_high = flags[level] == 1
    high = jnp.where(is_high, own[...], other[...])
    low = jnp.where(is_high, other[...], own[...])
    total[...] = low + apply_transposed(low_matrix[...], high)


def gathered_kernel(wanted, operation, flags, *refs):
    others = refs[:5]
    matrices = refs[5:9]
    result = refs[9]
    result[...] = jnp.where(flags[0] == wanted, others[0][...], 0.0)
    for level in range(1, 5):

        @pl.when(flags[level] == wanted)
        def _():
            result[...] = result[...] + operation(matrices[level - 1][...], others[level][...])


def turn_kernel(flags, entering, other, prefix, transition, offset, solved, returning):
    before = entering[...] + jnp.where(flags[5] == 1, 1.0, 0.0) * apply(prefix[...], other[...])
    current = offset[...] + apply(transition[...], before)
    solved[...] = current
    returning[...] = -apply_transposed(transition[...], current)


def finish_kernel(
    flags, inverse, entering, other, suffix, solved, velocity, node_mass, nodes, velocity_out
):
    after = entering[...] + jnp.where(flags[5] == 0, 1.0, 0.0) * apply_transposed(
        suffix[...], other[...]
    )
    sign = (1 - 2 * flags[SIDE]).astype(f32)
    multiplier = sign * apply_transposed(inverse[0], solved[...] - after)
    in_row, in_column = slot_masks(nodes[...])
    chosen = in_column.astype(f32).astype(bf16)
    weight = 1.0 / node_mass[...]
    for i in range(3):
        held = jnp.where(in_row, multiplier[:, IFC * i : IFC * i + IFC], 0.0)
        change = sum(
            lax.dot_general(p, chosen, (((1,), (1,)), ((), ())), preferred_element_type=f32)
            for p in reversed(triple(held))
        )
        velocity_out[i] = velocity[i] - change.reshape(CX, CY, CZ) * weight


def bound(level, kernel, *fixed):
    def run(*refs):
        kernel(level, *fixed, *refs)

    return run


def first_products(flags, factor_inverse, factor_lower):
    cube = 6 * IB**3
    transition = pair_call(
        transition_kernel, flags, [factor_inverse, factor_lower], [], MAT, cube
    )
    other = swap(transition, MASKS[0])
    high, low, merged, half = local_call(
        first_merge_kernel, flags, [transition, other], (MAT, MAT, MAT, HALFMAT), cube
    )
    prefix, suffix = local_call(first_reach_kernel, flags, [other], (MAT, MAT))
    return transition, (merged, half), [(high, low, prefix, suffix)]


def merge_level(flags, level, block, levels, gate=None):
    cube = 6 * IB**3
    merged, half = block
    near = swap(half, MASKS[level])
    if gate is not None:
        near, _ = lax.optimization_barrier((near, gate))
    far = swap(near, 1)
    last = level == 4
    high, low, *block = local_call(
        bound(level, merge_kernel, last),
        flags,
        [merged, near, far],
        (MAT, MAT) if last else (MAT, MAT, MAT, HALFMAT),
        cube,
    )
    prefix, suffix = local_call(
        bound(level, reach_kernel), flags, [high, low, *levels[-1][2:]], (MAT, MAT), cube
    )
    return block, levels + [(high, low, prefix, suffix)]


def coupled_velocity(
    flags, picked, factor_inverse, transition, block, levels, velocity, node_mass, nodes
):
    square = 2 * IB * IB
    count = lax.axis_size("sub")
    partner = lax.ppermute(picked, "sub", [(i, i ^ 1) for i in range(count)])
    offset = pair_call(start_kernel, flags, [factor_inverse], [picked, partner], ROW, square)
    total, others = offset, []
    for level in range(5):
        others.append(swap(total, MASKS[level]))
        if level >= 2:
            gate = picked if level == 2 else total
            block, levels = merge_level(flags, level, block, levels, gate)
        total = local_call(
            bound(level, forward_kernel), flags, [total, others[-1], levels[level][0]], ROW, square
        )
    _, lows, prefixes, suffixes = zip(*levels)
    last_other = swap(total, MASKS[5])
    entering = local_call(
        bound(1, gathered_kernel, apply), flags, others + list(prefixes[:4]), ROW, 4 * square
    )
    solved, returning = local_call(
        turn_kernel,
        flags,
        [entering, last_other, prefixes[4], transition, offset],
        (ROW, ROW),
        3 * square,
    )
    total, others = returning, []
    for level in range(5):
        others.append(swap(total, MASKS[level]))
        total = local_call(
            bound(level, backward_kernel), flags, [total, others[-1], lows[level]], ROW, square
        )
    last_other = swap(total, MASKS[5])
    entering = local_call(
        bound(0, gathered_kernel, apply_transposed), flags, others + list(suffixes[:4]), ROW, 4 * square
    )
    return pair_call(
        finish_kernel,
        flags,
        [factor_inverse],
        [entering, last_other, suffixes[4], solved, velocity, node_mass, nodes],
        jax.ShapeDtypeStruct(velocity.shape, f32),
        2 * square,
    )


def outer_swap(value):
    count = lax.axis_size("tile")
    route = []
    for low in range(1, count - 1, 2):
        route += [(low, low + 1), (low + 1, low)]
    return lax.ppermute(value, "tile", route)


def body(
    displacement,
    velocity,
    external_load,
    node_mass,
    modulus,
    stiffness,
    substeps,
    interface_nodes,
    factor_inverse,
    factor_lower,
):
    sub, tile = lax.axis_index("sub"), lax.axis_index("tile")
    last = tile == lax.axis_size("tile") - 1
    flags = jnp.stack(
        [(tile >> k) & 1 for k in range(6)] + [sub // 2, sub % 2, last, substeps[0]]
    ).astype(jnp.int32)
    step = coarse_step / substeps.astype(f32)
    state = [displacement[0], velocity[0], external_load[0], node_mass[0], modulus[0]]
    packed = jax.ShapeDtypeStruct((PACKED, CY, CZ), f32)
    outer, inner = local_call(pack_kernel, flags, state, (packed, packed))
    outer = outer_swap(outer)
    inner = swap(inner, 1)
    transition, block, levels = first_products(flags, factor_inverse, factor_lower)
    block, levels = merge_level(flags, 1, block, levels)
    outer, _ = lax.optimization_barrier((outer, block[1]))
    final_displacement, final_velocity, picked = substeps_call(
        flags, step, state, outer, inner, stiffness, interface_nodes
    )
    coupled = coupled_velocity(
        flags,
        picked,
        factor_inverse,
        transition,
        block,
        levels,
        final_velocity,
        node_mass[0],
        interface_nodes,
    )
    return final_displacement[None], coupled[None]


def solution(mesh):
    in_specs = (
        P("sub", None, "tile", None, None),
        P("sub", None, "tile", None, None),
        P("sub", None, "tile", None, None),
        P("sub", "tile", None, None),
        P("sub", "tile", None, None),
        P(),
        P("sub"),
        P("sub", "tile"),
        P(None, "tile", None),
        P(None, "tile", None),
    )
    out_specs = (P("sub", None, "tile", None, None), P("sub", None, "tile", None, None))
    return jax.shard_map(body, mesh=mesh, in_specs=in_specs, out_specs=out_specs, check_vma=False)
```

```python
import jax
import jax.numpy as jnp
from jax import lax
from jax.experimental import pallas as pl
from jax.experimental.pallas import tpu as pltpu
from jax.sharding import PartitionSpec as P

IFC = 128
IB = 384
HALF = IB // 2
GRANT = 12 << 20
WIDE_GRANT = 60 << 20
CX, CY, CZ = 4, 32, 128
DEEP = 3 * CX
NEAR = CX - 1
PACKED = 37
CORE, PAIR, SIDE, LAST, STEPS = 0, 6, 7, 8, 9
GROUPS = CY // 8
MASKS = (1, 2, 4, 12, 16, 48)

coarse_step = 0.1
f32 = jnp.float32
bf16 = jnp.bfloat16
VM = pl.BlockSpec(memory_space=pltpu.VMEM)
SM = pl.BlockSpec(memory_space=pltpu.SMEM)
MAT = jax.ShapeDtypeStruct((IB, IB), f32)
HALFMAT = jax.ShapeDtypeStruct((HALF, IB), f32)
ROW = jax.ShapeDtypeStruct((1, IB), f32)


def swap(value, mask):
    return lax.ppermute(value, "tile", [(i, i ^ mask) for i in range(lax.axis_size("tile"))])


def cost(flops, nbytes):
    return pl.CostEstimate(flops=flops, bytes_accessed=nbytes, transcendentals=0)


def local_call(kernel, flags, operands, outs, flops=0):
    nbytes = sum(o.size * 4 for o in operands)
    return pl.pallas_call(
        kernel,
        out_shape=outs,
        in_specs=[SM] + [VM] * len(operands),
        out_specs=jax.tree.map(lambda _: VM, outs),
        compiler_params=pltpu.CompilerParams(vmem_limit_bytes=GRANT),
        cost_estimate=cost(flops, nbytes),
    )(flags, *operands)


def halves(value):
    high = value.astype(bf16)
    return high, (value - high.astype(f32)).astype(bf16)


def product(a, b):
    a_high, a_low = halves(a)
    b_high, b_low = halves(b)
    return (
        jnp.dot(a_low, b_high, preferred_element_type=f32)
        + jnp.dot(a_high, b_low, preferred_element_type=f32)
        + jnp.dot(a_high, b_high, preferred_element_type=f32)
    )


def eye_mask(size):
    return lax.broadcasted_iota(jnp.int32, (size, size), 0) == lax.broadcasted_iota(
        jnp.int32, (size, size), 1
    )


def column_to_row(column):
    eye = eye_mask(IFC)
    return jnp.concatenate(
        [
            jnp.sum(jnp.where(eye, column[k : k + IFC], 0.0), axis=0, keepdims=True)
            for k in range(0, IB, IFC)
        ],
        axis=1,
    )


def row_to_column(row):
    eye = eye_mask(IFC)
    return jnp.concatenate(
        [
            jnp.sum(jnp.where(eye, row[:, k : k + IFC], 0.0), axis=1, keepdims=True)
            for k in range(0, IB, IFC)
        ],
        axis=0,
    )


def apply(matrix, row):
    return column_to_row(jnp.sum(matrix * row, axis=1, keepdims=True))


def apply_transposed(matrix, row):
    return jnp.sum(matrix * row_to_column(row), axis=0, keepdims=True)


def triple(value):
    high = value.astype(bf16)
    rest = value - high.astype(f32)
    middle = rest.astype(bf16)
    return high, middle, (rest - middle.astype(f32)).astype(bf16)


def slot_masks(nodes):
    index = lax.broadcasted_iota(jnp.int32, (IFC, IFC), 0)
    return index == nodes // CZ, index == nodes % CZ


def wide(value):
    return jnp.concatenate([value[8 * g : 8 * g + 8] for g in range(GROUPS)], axis=1)


def tall(value):
    return jnp.concatenate([value[:, CZ * g : CZ * g + CZ] for g in range(GROUPS)], axis=0)


def spread(values):
    row = lax.broadcasted_iota(jnp.int32, (192, 24), 0) // 8
    rows = (row == lax.broadcasted_iota(jnp.int32, (192, 24), 1)).astype(f32).astype(bf16)
    block = lax.broadcasted_iota(jnp.int32, (24, 192), 1) // 8
    side = block // 12
    dof = 8 * (block % 12 // 4) + 4 * side + block % 4
    columns = (dof == lax.broadcasted_iota(jnp.int32, (24, 192), 0)).astype(f32).astype(bf16)
    tall_values = jnp.dot(rows, values, preferred_element_type=f32).astype(bf16)
    full = jnp.dot(tall_values, columns, preferred_element_type=f32)
    same = (
        lax.broadcasted_iota(jnp.int32, (192, 192), 0) % 8
        == lax.broadcasted_iota(jnp.int32, (192, 192), 1) % 8
    )
    return jnp.where(same, full, 0.0).astype(bf16)


def substep_kernel(
    flags, step, displacement, velocity, external_load, node_mass, modulus,
    outer, inner, stiffness, nodes,
    displacement_out, velocity_out, picked,
    disp, vel, load, inverse_mass, factor, stiff, even, odd, even_force, odd_force, upper,
):
    first = flags[CORE] == 0

    def put_mass(low, mass):
        present = mass > 0.0
        inverse_mass[pl.ds(low, mass.shape[0])] = jnp.where(
            present, 1.0 / jnp.where(present, mass, 1.0), 0.0
        )

    def put_factor(low, source, base):
        row = lax.broadcasted_iota(jnp.int32, (CY, CZ), 0)
        for x in range(CX):
            factor[low + x] = wide(jnp.where(row < CY - 1, source[base + x], 0.0))

    def place(source, low, shift):
        for i in range(3):
            disp[i, pl.ds(low, CX)] = source[pl.ds(CX * i, CX)]
            vel[i, pl.ds(low + shift, NEAR)] = source[pl.ds(12 + NEAR * i, NEAR)]
            load[i, pl.ds(low + shift, NEAR)] = source[pl.ds(21 + NEAR * i, NEAR)]
        put_mass(low + shift, source[pl.ds(30, NEAR)])
        put_factor(low, source, 33)

    disp[:, CX : 2 * CX] = displacement[...]
    vel[:, CX : 2 * CX] = velocity[...]
    load[:, CX : 2 * CX] = external_load[...]
    put_mass(CX, node_mass[...])
    put_factor(CX, modulus, 0)

    @pl.when(first)
    def _():
        place(outer, 0, 1)
        place(inner, 2 * CX, 0)

    @pl.when(jnp.logical_not(first))
    def _():
        place(inner, 0, 1)
        place(outer, 2 * CX, 0)

    @pl.when(flags[LAST] == 1)
    def _():
        factor[2 * CX - 1] = jnp.zeros((8, GROUPS * CZ), f32)

    high, low = [spread(s) for s in halves(stiffness[...])]
    stiff[...] = jnp.concatenate([high, high, low], axis=1)
    length = step[0]

    def put_features(layer, below, above):
        columns = []
        for i in range(3):
            base = disp[i, layer]
            turned = pltpu.roll(base, CZ - 1, 1)
            columns += [base, turned, pltpu.roll(base, CY - 1, 0), pltpu.roll(turned, CY - 1, 0)]
        for g in range(GROUPS):
            lanes = slice(CZ * g, CZ * g + CZ)
            block = jnp.concatenate([c[8 * g : 8 * g + 8] for c in columns], axis=0)
            high, low = halves(block)
            for target, start in ((below, 96), (above, 0)):
                if target is not None:
                    target[start : start + 96, lanes] = high
                    target[start + 192 : start + 288, lanes] = low
                    target[start + 384 : start + 480, lanes] = high

    def put_force(source, target):
        target[...] = jnp.dot(stiff[...], source[...], preferred_element_type=f32)

    def corner(force, scale, i, a, r):
        start = 8 * (8 * i + 4 * a + r)
        return force[start : start + 8] * scale

    def keep_upper(layer, force):
        scale = factor[layer]
        for i in range(3):
            for r in range(4):
                upper[4 * i + r] = corner(force, scale, i, 1, r)

    def finish_layer(layer, force):
        scale = factor[layer]
        weight = inverse_mass[layer]
        for i in range(3):
            sums = [corner(force, scale, i, 0, r) + upper[4 * i + r] for r in range(4)]
            s00, s01, s10, s11 = [tall(s) for s in sums]
            base = s00 + pltpu.roll(s10, 1, 0)
            turned = s01 + pltpu.roll(s11, 1, 0)
            internal = base + pltpu.roll(turned, 1, 1)
            speed = vel[i, layer] + length * ((load[i, layer] - internal) * weight)
            vel[i, layer] = speed
            disp[i, layer] = disp[i, layer] + length * speed

    def one_substep(k, carry):
        put_features(k, None, even)
        put_features(k + 1, even, odd)
        put_force(even, even_force)
        put_features(k + 2, odd, even)
        keep_upper(k, even_force)
        put_force(odd, odd_force)
        put_features(k + 3, even, odd)

        def two_layers(pair, carry):
            layer = k + 1 + 2 * pair
            put_force(even, even_force)
            put_features(layer + 3, odd, even)
            finish_layer(layer, odd_force)
            keep_upper(layer, odd_force)
            put_force(odd, odd_force)
            put_features(layer + 4, even, odd)
            finish_layer(layer + 1, even_force)
            keep_upper(layer + 1, even_force)
            return carry

        return lax.fori_loop(0, CX + 1 - k, two_layers, carry)

    lax.fori_loop(0, flags[STEPS], one_substep, 0)
    displacement_out[...] = disp[:, CX : 2 * CX]
    final = vel[:, CX : 2 * CX]
    velocity_out[...] = final
    in_row, in_column = slot_masks(nodes[...])
    chosen = in_column.astype(f32).astype(bf16)
    parts = []
    for i in range(3):
        pieces = triple(final[i].reshape(CX * CY, CZ))
        values = sum(jnp.dot(p, chosen, preferred_element_type=f32) for p in reversed(pieces))
        parts.append(jnp.sum(jnp.where(in_row, values, 0.0), axis=0, keepdims=True))
    picked[...] = jnp.concatenate(parts, axis=1)


def pack_kernel(flags, displacement, velocity, external_load, node_mass, modulus, outer, inner):
    for target, start in ((outer, flags[CORE]), (inner, 1 - flags[CORE])):
        for i in range(3):
            target[pl.ds(CX * i, CX)] = displacement[i]
            target[pl.ds(12 + NEAR * i, NEAR)] = velocity[i, pl.ds(start, NEAR)]
            target[pl.ds(21 + NEAR * i, NEAR)] = external_load[i, pl.ds(start, NEAR)]
        target[pl.ds(30, NEAR)] = node_mass[pl.ds(start, NEAR)]
        target[pl.ds(33, CX)] = modulus[...]


def substeps_call(flags, step, state, outer, inner, stiffness, nodes):
    grid_shape = (3, CX, CY, CZ)
    return pl.pallas_call(
        substep_kernel,
        out_shape=(
            jax.ShapeDtypeStruct(grid_shape, f32),
            jax.ShapeDtypeStruct(grid_shape, f32),
            ROW,
        ),
        in_specs=[SM, SM] + [VM] * 9,
        out_specs=(VM, VM, VM),
        scratch_shapes=[
            pltpu.VMEM((3, DEEP + 2, CY, CZ), f32),
            pltpu.VMEM((3, DEEP, CY, CZ), f32),
            pltpu.VMEM((3, DEEP, CY, CZ), f32),
            pltpu.VMEM((DEEP, CY, CZ), f32),
            pltpu.VMEM((DEEP, 8, GROUPS * CZ), f32),
            pltpu.VMEM((192, 576), bf16),
            pltpu.VMEM((576, GROUPS * CZ), bf16),
            pltpu.VMEM((576, GROUPS * CZ), bf16),
            pltpu.VMEM((192, GROUPS * CZ), f32),
            pltpu.VMEM((192, GROUPS * CZ), f32),
            pltpu.VMEM((12, 8, GROUPS * CZ), f32),
        ],
        compiler_params=pltpu.CompilerParams(vmem_limit_bytes=20 << 20),
        cost_estimate=cost(32 * 2 * 192 * 576 * 512, 3 * 720896),
    )(flags, step, *state, outer, inner, stiffness, nodes)

def transition_kernel(flags, inverses, lowers, transition, inverse, lower, arrived):
    copies = [
        pltpu.make_async_copy(source.at[flags[PAIR]], target, arrived.at[k])
        for k, (source, target) in enumerate(((inverses, inverse), (lowers, lower)))
    ]
    for copy in copies:
        copy.start()
    for copy in copies:
        copy.wait()
    transition[...] = -product(inverse[...], lower[...])


def transition_call(flags, inverses, lowers):
    far = pl.BlockSpec(memory_space=pltpu.HBM)
    return pl.pallas_call(
        transition_kernel,
        out_shape=(MAT, MAT),
        in_specs=[SM, far, far],
        out_specs=(VM, VM),
        scratch_shapes=[pltpu.VMEM((IB, IB), f32), pltpu.SemaphoreType.DMA((2,))],
        compiler_params=pltpu.CompilerParams(vmem_limit_bytes=WIDE_GRANT),
        cost_estimate=cost(6 * IB**3, 8 * IB * IB),
    )(flags, inverses, lowers)


def store_half(flags, half, value_ref):
    @pl.when(flags[CORE] == 0)
    def _():
        half[...] = value_ref[:HALF]

    @pl.when(flags[CORE] == 1)
    def _():
        half[...] = value_ref[HALF:]


def first_merge_kernel(flags, own, other, high_ref, low_ref, merged, half):
    is_high = flags[0] == 1
    high = jnp.where(is_high, own[...], other[...])
    low = jnp.where(is_high, other[...], own[...])
    high_ref[...] = high
    low_ref[...] = low
    merged[...] = product(high, low)
    store_half(flags, half, merged)


def first_reach_kernel(flags, other, prefix, suffix):
    is_high = flags[0] == 1
    identity = eye_mask(IB).astype(f32)
    prefix[...] = jnp.where(is_high, other[...], identity)
    suffix[...] = jnp.where(is_high, identity, other[...])


def merge_kernel(level, last, flags, own, near, far, high_ref, low_ref, *outs):
    is_high = flags[level] == 1
    first = flags[CORE] == 0
    other = jnp.concatenate(
        [jnp.where(first, near[...], far[...]), jnp.where(first, far[...], near[...])], axis=0
    )
    high = jnp.where(is_high, own[...], other)
    low = jnp.where(is_high, other, own[...])
    high_ref[...] = high
    low_ref[...] = low
    if not last:
        merged, half = outs
        merged[...] = product(high, low)
        store_half(flags, half, merged)


def reach_kernel(level, flags, high, low, prefix, suffix, new_prefix, new_suffix):
    is_high = flags[level] == 1
    longer = product(
        jnp.where(is_high, prefix[...], high[...]), jnp.where(is_high, low[...], suffix[...])
    )
    new_prefix[...] = jnp.where(is_high, longer, prefix[...])
    new_suffix[...] = jnp.where(is_high, suffix[...], longer)


def start_kernel(flags, inverse, picked, partner, offset):
    sign = (1 - 2 * flags[SIDE]).astype(f32)
    offset[...] = apply(inverse[...], sign * (picked[...] - partner[...]))


def forward_kernel(level, flags, own, other, high_matrix, total):
    is_high = flags[level] == 1
    high = jnp.where(is_high, own[...], other[...])
    low = jnp.where(is_high, other[...], own[...])
    total[...] = high + apply(high_matrix[...], low)


def backward_kernel(level, flags, own, other, low_matrix, total):
    is_high = flags[level] == 1
    high = jnp.where(is_high, own[...], other[...])
    low = jnp.where(is_high, other[...], own[...])
    total[...] = low + apply_transposed(low_matrix[...], high)


def gathered_kernel(wanted, operation, flags, *refs):
    others = refs[:5]
    matrices = refs[5:9]
    result = refs[9]
    result[...] = jnp.where(flags[0] == wanted, others[0][...], 0.0)
    for level in range(1, 5):

        @pl.when(flags[level] == wanted)
        def _():
            result[...] = result[...] + operation(matrices[level - 1][...], others[level][...])


def turn_kernel(flags, entering, other, prefix, transition, offset, solved, returning):
    before = entering[...] + jnp.where(flags[5] == 1, 1.0, 0.0) * apply(prefix[...], other[...])
    current = offset[...] + apply(transition[...], before)
    solved[...] = current
    returning[...] = -apply_transposed(transition[...], current)


def finish_kernel(
    flags, inverse, entering, other, suffix, solved, velocity, node_mass, nodes, velocity_out
):
    after = entering[...] + jnp.where(flags[5] == 0, 1.0, 0.0) * apply_transposed(
        suffix[...], other[...]
    )
    sign = (1 - 2 * flags[SIDE]).astype(f32)
    multiplier = sign * apply_transposed(inverse[...], solved[...] - after)
    in_row, in_column = slot_masks(nodes[...])
    chosen = in_column.astype(f32).astype(bf16)
    weight = 1.0 / node_mass[...]
    for i in range(3):
        held = jnp.where(in_row, multiplier[:, IFC * i : IFC * i + IFC], 0.0)
        change = sum(
            lax.dot_general(p, chosen, (((1,), (1,)), ((), ())), preferred_element_type=f32)
            for p in reversed(triple(held))
        )
        velocity_out[i] = velocity[i] - change.reshape(CX, CY, CZ) * weight


def bound(level, kernel, *fixed):
    def run(*refs):
        kernel(level, *fixed, *refs)

    return run


def after(value, *earlier):
    return lax.optimization_barrier((value, *earlier))[0]


def first_products(flags, transition, gate):
    cube = 6 * IB**3
    other = after(swap(transition, MASKS[0]), gate)
    high, low, merged, half = local_call(
        first_merge_kernel, flags, [transition, other], (MAT, MAT, MAT, HALFMAT), cube
    )
    prefix, suffix = local_call(first_reach_kernel, flags, [other], (MAT, MAT))
    return (merged, half), [(high, low, prefix, suffix)]


def merge_level(flags, level, block, levels, gate=None):
    cube = 6 * IB**3
    merged, half = block
    near = swap(half, MASKS[level])
    if gate is not None:
        near = after(near, gate)
    far = swap(near, 1)
    last = level == 4
    high, low, *block = local_call(
        bound(level, merge_kernel, last),
        flags,
        [merged, near, far],
        (MAT, MAT) if last else (MAT, MAT, MAT, HALFMAT),
        cube,
    )
    prefix, suffix = local_call(
        bound(level, reach_kernel), flags, [high, low, *levels[-1][2:]], (MAT, MAT), cube
    )
    return block, levels + [(high, low, prefix, suffix)]


def coupled_velocity(
    flags, picked, inverse, transition, block, levels, velocity, node_mass, nodes
):
    square = 2 * IB * IB
    count = lax.axis_size("sub")
    partner = lax.ppermute(picked, "sub", [(i, i ^ 1) for i in range(count)])
    offset = local_call(start_kernel, flags, [inverse, picked, partner], ROW, square)
    total, others = offset, []
    for level in range(5):
        others.append(swap(total, MASKS[level]))
        if level >= 2:
            gate = picked if level == 2 else total
            block, levels = merge_level(flags, level, block, levels, gate)
        others[-1] = after(others[-1], levels[max(level - 1, 1)][2])
        total = local_call(
            bound(level, forward_kernel), flags, [total, others[-1], levels[level][0]], ROW, square
        )
    _, lows, prefixes, suffixes = zip(*levels)
    last_other = swap(total, MASKS[5])
    entering = local_call(
        bound(1, gathered_kernel, apply), flags, others + list(prefixes[:4]), ROW, 4 * square
    )
    solved, returning = local_call(
        turn_kernel,
        flags,
        [entering, last_other, prefixes[4], transition, offset],
        (ROW, ROW),
        3 * square,
    )
    total, others = returning, []
    for level in range(5):
        others.append(swap(total, MASKS[level]))
        total = local_call(
            bound(level, backward_kernel), flags, [total, others[-1], lows[level]], ROW, square
        )
    last_other = swap(total, MASKS[5])
    entering = local_call(
        bound(0, gathered_kernel, apply_transposed), flags, others + list(suffixes[:4]), ROW, 4 * square
    )
    return local_call(
        finish_kernel,
        flags,
        [inverse, entering, last_other, suffixes[4], solved, velocity, node_mass, nodes],
        jax.ShapeDtypeStruct(velocity.shape, f32),
        2 * square,
    )


def outer_swap(value):
    count = lax.axis_size("tile")
    route = []
    for low in range(1, count - 1, 2):
        route += [(low, low + 1), (low + 1, low)]
    return lax.ppermute(value, "tile", route)


def body(
    displacement,
    velocity,
    external_load,
    node_mass,
    modulus,
    stiffness,
    substeps,
    interface_nodes,
    factor_inverse,
    factor_lower,
):
    sub, tile = lax.axis_index("sub"), lax.axis_index("tile")
    last = tile == lax.axis_size("tile") - 1
    flags = jnp.stack(
        [(tile >> k) & 1 for k in range(6)] + [sub // 2, sub % 2, last, substeps[0]]
    ).astype(jnp.int32)
    step = coarse_step / substeps.astype(f32)
    state = [displacement[0], velocity[0], external_load[0], node_mass[0], modulus[0]]
    packed = jax.ShapeDtypeStruct((PACKED, CY, CZ), f32)
    transition, inverse = transition_call(flags, factor_inverse, factor_lower)
    outer, inner = local_call(pack_kernel, flags, state, (packed, packed))
    block, levels = first_products(flags, transition, outer)
    outer = outer_swap(outer)
    inner = swap(inner, 1)
    block, levels = merge_level(flags, 1, block, levels)
    outer = after(outer, block[1])
    final_displacement, final_velocity, picked = substeps_call(
        flags, step, state, outer, inner, stiffness, interface_nodes
    )
    coupled = coupled_velocity(
        flags,
        picked,
        inverse,
        transition,
        block,
        levels,
        final_velocity,
        node_mass[0],
        interface_nodes,
    )
    return final_displacement[None], coupled[None]


def solution(mesh):
    in_specs = (
        P("sub", None, "tile", None, None),
        P("sub", None, "tile", None, None),
        P("sub", None, "tile", None, None),
        P("sub", "tile", None, None),
        P("sub", "tile", None, None),
        P(),
        P("sub"),
        P("sub", "tile"),
        P(None, "tile", None),
        P(None, "tile", None),
    )
    out_specs = (P("sub", None, "tile", None, None), P("sub", None, "tile", None, None))
    return jax.shard_map(body, mesh=mesh, in_specs=in_specs, out_specs=out_specs, check_vma=False)
```

```python
import jax
import jax.numpy as jnp
from jax import lax
from jax.experimental import pallas as pl
from jax.experimental.pallas import tpu as pltpu
from jax.sharding import PartitionSpec as P

IFC = 128
IB = 384
HALF = IB // 2
GRANT = 12 << 20
CX, CY, CZ = 4, 32, 128
DEEP = 3 * CX
NEAR = CX - 1
PACKED = 37
CORE, PAIR, SIDE, LAST, STEPS = 0, 6, 7, 8, 9
GROUPS = CY // 8
MASKS = (1, 2, 4, 12, 16, 48)
OPPOSITE = 10

coarse_step = 0.1
f32 = jnp.float32
bf16 = jnp.bfloat16
VM = pl.BlockSpec(memory_space=pltpu.VMEM)
SM = pl.BlockSpec(memory_space=pltpu.SMEM)
MAT = jax.ShapeDtypeStruct((IB, IB), f32)
HALFMAT = jax.ShapeDtypeStruct((HALF, IB), f32)
ROW = jax.ShapeDtypeStruct((1, IB), f32)


def swap(value, mask):
    return lax.ppermute(value, "tile", [(i, i ^ mask) for i in range(lax.axis_size("tile"))])


def cost(flops, nbytes):
    return pl.CostEstimate(flops=flops, bytes_accessed=nbytes, transcendentals=0)


def local_call(kernel, flags, operands, outs, flops=0):
    nbytes = sum(o.size * 4 for o in operands)
    return pl.pallas_call(
        kernel,
        out_shape=outs,
        in_specs=[SM] + [VM] * len(operands),
        out_specs=jax.tree.map(lambda _: VM, outs),
        compiler_params=pltpu.CompilerParams(vmem_limit_bytes=GRANT),
        cost_estimate=cost(flops, nbytes),
    )(flags, *operands)


def halves(value):
    high = value.astype(bf16)
    return high, (value - high.astype(f32)).astype(bf16)


def product(a, b):
    a_high, a_low = halves(a)
    b_high, b_low = halves(b)
    return (
        jnp.dot(a_low, b_high, preferred_element_type=f32)
        + jnp.dot(a_high, b_low, preferred_element_type=f32)
        + jnp.dot(a_high, b_high, preferred_element_type=f32)
    )


def eye_mask(size):
    return lax.broadcasted_iota(jnp.int32, (size, size), 0) == lax.broadcasted_iota(
        jnp.int32, (size, size), 1
    )


def column_to_row(column):
    eye = eye_mask(IFC)
    return jnp.concatenate(
        [
            jnp.sum(jnp.where(eye, column[k : k + IFC], 0.0), axis=0, keepdims=True)
            for k in range(0, IB, IFC)
        ],
        axis=1,
    )


def row_to_column(row):
    eye = eye_mask(IFC)
    return jnp.concatenate(
        [
            jnp.sum(jnp.where(eye, row[:, k : k + IFC], 0.0), axis=1, keepdims=True)
            for k in range(0, IB, IFC)
        ],
        axis=0,
    )


def apply(matrix, row):
    return column_to_row(jnp.sum(matrix * row, axis=1, keepdims=True))


def apply_transposed(matrix, row):
    return jnp.sum(matrix * row_to_column(row), axis=0, keepdims=True)


def triple(value):
    high = value.astype(bf16)
    rest = value - high.astype(f32)
    middle = rest.astype(bf16)
    return high, middle, (rest - middle.astype(f32)).astype(bf16)


def slot_masks(nodes):
    index = lax.broadcasted_iota(jnp.int32, (IFC, IFC), 0)
    return index == nodes // CZ, index == nodes % CZ


def wide(value):
    return jnp.concatenate([value[8 * g : 8 * g + 8] for g in range(GROUPS)], axis=1)


def tall(value):
    return jnp.concatenate([value[:, CZ * g : CZ * g + CZ] for g in range(GROUPS)], axis=0)


def spread(values):
    row = lax.broadcasted_iota(jnp.int32, (192, 24), 0) // 8
    rows = (row == lax.broadcasted_iota(jnp.int32, (192, 24), 1)).astype(f32).astype(bf16)
    block = lax.broadcasted_iota(jnp.int32, (24, 192), 1) // 8
    side = block // 12
    dof = 8 * (block % 12 // 4) + 4 * side + block % 4
    columns = (dof == lax.broadcasted_iota(jnp.int32, (24, 192), 0)).astype(f32).astype(bf16)
    tall_values = jnp.dot(rows, values, preferred_element_type=f32).astype(bf16)
    full = jnp.dot(tall_values, columns, preferred_element_type=f32)
    same = (
        lax.broadcasted_iota(jnp.int32, (192, 192), 0) % 8
        == lax.broadcasted_iota(jnp.int32, (192, 192), 1) % 8
    )
    return jnp.where(same, full, 0.0).astype(bf16)


def substep_kernel(
    flags, step, displacement, velocity, external_load, node_mass, modulus,
    outer, inner, stiffness, nodes,
    displacement_out, velocity_out, picked,
    disp, vel, load, inverse_mass, factor, stiff, even, odd, even_force, odd_force, upper,
):
    first = flags[CORE] == 0

    def put_mass(low, mass):
        present = mass > 0.0
        inverse_mass[pl.ds(low, mass.shape[0])] = jnp.where(
            present, 1.0 / jnp.where(present, mass, 1.0), 0.0
        )

    def put_factor(low, source, base):
        row = lax.broadcasted_iota(jnp.int32, (CY, CZ), 0)
        for x in range(CX):
            factor[low + x] = wide(jnp.where(row < CY - 1, source[base + x], 0.0))

    def place(source, low, shift):
        for i in range(3):
            disp[i, pl.ds(low, CX)] = source[pl.ds(CX * i, CX)]
            vel[i, pl.ds(low + shift, NEAR)] = source[pl.ds(12 + NEAR * i, NEAR)]
            load[i, pl.ds(low + shift, NEAR)] = source[pl.ds(21 + NEAR * i, NEAR)]
        put_mass(low + shift, source[pl.ds(30, NEAR)])
        put_factor(low, source, 33)

    disp[:, CX : 2 * CX] = displacement[...]
    vel[:, CX : 2 * CX] = velocity[...]
    load[:, CX : 2 * CX] = external_load[...]
    put_mass(CX, node_mass[...])
    put_factor(CX, modulus, 0)

    @pl.when(first)
    def _():
        place(outer, 0, 1)
        place(inner, 2 * CX, 0)

    @pl.when(jnp.logical_not(first))
    def _():
        place(inner, 0, 1)
        place(outer, 2 * CX, 0)

    @pl.when(flags[LAST] == 1)
    def _():
        factor[2 * CX - 1] = jnp.zeros((8, GROUPS * CZ), f32)

    high, low = [spread(s) for s in halves(stiffness[...])]
    stiff[...] = jnp.concatenate([high, high, low], axis=1)
    length = step[0]

    def put_features(layer, below, above):
        columns = []
        for i in range(3):
            base = disp[i, layer]
            turned = pltpu.roll(base, CZ - 1, 1)
            columns += [base, turned, pltpu.roll(base, CY - 1, 0), pltpu.roll(turned, CY - 1, 0)]
        for g in range(GROUPS):
            lanes = slice(CZ * g, CZ * g + CZ)
            block = jnp.concatenate([c[8 * g : 8 * g + 8] for c in columns], axis=0)
            high, low = halves(block)
            for target, start in ((below, 96), (above, 0)):
                if target is not None:
                    target[start : start + 96, lanes] = high
                    target[start + 192 : start + 288, lanes] = low
                    target[start + 384 : start + 480, lanes] = high

    def put_force(source, target):
        target[...] = jnp.dot(stiff[...], source[...], preferred_element_type=f32)

    def corner(force, scale, i, a, r):
        start = 8 * (8 * i + 4 * a + r)
        return force[start : start + 8] * scale

    def keep_upper(layer, force):
        scale = factor[layer]
        for i in range(3):
            for r in range(4):
                upper[4 * i + r] = corner(force, scale, i, 1, r)

    def finish_layer(layer, force):
        scale = factor[layer]
        weight = inverse_mass[layer]
        for i in range(3):
            sums = [corner(force, scale, i, 0, r) + upper[4 * i + r] for r in range(4)]
            s00, s01, s10, s11 = [tall(s) for s in sums]
            base = s00 + pltpu.roll(s10, 1, 0)
            turned = s01 + pltpu.roll(s11, 1, 0)
            internal = base + pltpu.roll(turned, 1, 1)
            speed = vel[i, layer] + length * ((load[i, layer] - internal) * weight)
            vel[i, layer] = speed
            disp[i, layer] = disp[i, layer] + length * speed

    def one_substep(k, carry):
        put_features(k, None, even)
        put_features(k + 1, even, odd)
        put_force(even, even_force)
        put_features(k + 2, odd, even)
        keep_upper(k, even_force)
        put_force(odd, odd_force)
        put_features(k + 3, even, odd)

        def two_layers(pair, carry):
            layer = k + 1 + 2 * pair
            put_force(even, even_force)
            put_features(layer + 3, odd, even)
            finish_layer(layer, odd_force)
            keep_upper(layer, odd_force)
            put_force(odd, odd_force)
            put_features(layer + 4, even, odd)
            finish_layer(layer + 1, even_force)
            keep_upper(layer + 1, even_force)
            return carry

        return lax.fori_loop(0, CX + 1 - k, two_layers, carry)

    lax.fori_loop(0, flags[STEPS], one_substep, 0)
    displacement_out[...] = disp[:, CX : 2 * CX]
    final = vel[:, CX : 2 * CX]
    velocity_out[...] = final
    in_row, in_column = slot_masks(nodes[...])
    chosen = in_column.astype(f32).astype(bf16)
    parts = []
    for i in range(3):
        pieces = triple(final[i].reshape(CX * CY, CZ))
        values = sum(jnp.dot(p, chosen, preferred_element_type=f32) for p in reversed(pieces))
        parts.append(jnp.sum(jnp.where(in_row, values, 0.0), axis=0, keepdims=True))
    picked[...] = jnp.concatenate(parts, axis=1)


def pack_kernel(flags, displacement, velocity, external_load, node_mass, modulus, outer, inner):
    for target, start in ((outer, flags[CORE]), (inner, 1 - flags[CORE])):
        for i in range(3):
            target[pl.ds(CX * i, CX)] = displacement[i]
            target[pl.ds(12 + NEAR * i, NEAR)] = velocity[i, pl.ds(start, NEAR)]
            target[pl.ds(21 + NEAR * i, NEAR)] = external_load[i, pl.ds(start, NEAR)]
        target[pl.ds(30, NEAR)] = node_mass[pl.ds(start, NEAR)]
        target[pl.ds(33, CX)] = modulus[...]


def substeps_call(flags, step, state, outer, inner, stiffness, nodes):
    grid_shape = (3, CX, CY, CZ)
    return pl.pallas_call(
        substep_kernel,
        out_shape=(
            jax.ShapeDtypeStruct(grid_shape, f32),
            jax.ShapeDtypeStruct(grid_shape, f32),
            ROW,
        ),
        in_specs=[SM, SM] + [VM] * 9,
        out_specs=(VM, VM, VM),
        scratch_shapes=[
            pltpu.VMEM((3, DEEP + 2, CY, CZ), f32),
            pltpu.VMEM((3, DEEP, CY, CZ), f32),
            pltpu.VMEM((3, DEEP, CY, CZ), f32),
            pltpu.VMEM((DEEP, CY, CZ), f32),
            pltpu.VMEM((DEEP, 8, GROUPS * CZ), f32),
            pltpu.VMEM((192, 576), bf16),
            pltpu.VMEM((576, GROUPS * CZ), bf16),
            pltpu.VMEM((576, GROUPS * CZ), bf16),
            pltpu.VMEM((192, GROUPS * CZ), f32),
            pltpu.VMEM((192, GROUPS * CZ), f32),
            pltpu.VMEM((12, 8, GROUPS * CZ), f32),
        ],
        compiler_params=pltpu.CompilerParams(vmem_limit_bytes=20 << 20),
        cost_estimate=cost(32 * 2 * 192 * 576 * 512, 3 * 720896),
    )(flags, step, *state, outer, inner, stiffness, nodes)

def transition_kernel(flags, inverses, lowers, transition, inverse):
    inverse[...] = inverses[flags[PAIR]]
    transition[...] = -product(inverse[...], lowers[flags[PAIR]])


def store_half(flags, half, value_ref):
    @pl.when(flags[CORE] == 0)
    def _():
        half[...] = value_ref[:HALF]

    @pl.when(flags[CORE] == 1)
    def _():
        half[...] = value_ref[HALF:]


def first_merge_kernel(flags, own, other, high_ref, low_ref, merged, half):
    is_high = flags[0] == 1
    high = jnp.where(is_high, own[...], other[...])
    low = jnp.where(is_high, other[...], own[...])
    high_ref[...] = high
    low_ref[...] = low
    merged[...] = product(high, low)
    store_half(flags, half, merged)


def first_reach_kernel(flags, other, prefix, suffix):
    is_high = flags[0] == 1
    identity = eye_mask(IB).astype(f32)
    prefix[...] = jnp.where(is_high, other[...], identity)
    suffix[...] = jnp.where(is_high, identity, other[...])


def whole(first, near, far):
    return jnp.concatenate(
        [jnp.where(first, near[...], far[...]), jnp.where(first, far[...], near[...])], axis=0
    )


def merge_kernel(level, last, flags, own, near, far, high_ref, low_ref, *outs):
    is_high = flags[level] == 1
    other = whole(flags[CORE] == 0, near, far)
    high = jnp.where(is_high, own[...], other)
    low = jnp.where(is_high, other, own[...])
    high_ref[...] = high
    low_ref[...] = low
    if not last:
        merged, half = outs
        merged[...] = product(high, low)
        store_half(flags, half, merged)


def row_kernel(
    flags, own, near, far, near_across, far_across, near_opposite, far_opposite,
    high_ref, low_ref, row_high_ref, row_low_ref, merged, half,
):
    first = flags[CORE] == 0
    is_high = flags[2] == 1
    in_upper = flags[3] == 1
    other = whole(first, near, far)
    across = whole(first, near_across, far_across)
    opposite = whole(first, near_opposite, far_opposite)
    high = jnp.where(is_high, own[...], other)
    low = jnp.where(is_high, other, own[...])
    high_ref[...] = high
    low_ref[...] = low
    mine = product(high, low)
    theirs = product(
        jnp.where(is_high, opposite, across), jnp.where(is_high, across, opposite)
    )
    row_high = jnp.where(in_upper, mine, theirs)
    row_low = jnp.where(in_upper, theirs, mine)
    row_high_ref[...] = row_high
    row_low_ref[...] = row_low
    merged[...] = product(row_high, row_low)
    store_half(flags, half, merged)


def reach_kernel(level, flags, high, low, prefix, suffix, new_prefix, new_suffix):
    is_high = flags[level] == 1
    longer = product(
        jnp.where(is_high, prefix[...], high[...]), jnp.where(is_high, low[...], suffix[...])
    )
    new_prefix[...] = jnp.where(is_high, longer, prefix[...])
    new_suffix[...] = jnp.where(is_high, suffix[...], longer)


def start_kernel(flags, inverse, picked, partner, offset):
    sign = (1 - 2 * flags[SIDE]).astype(f32)
    offset[...] = apply(inverse[...], sign * (picked[...] - partner[...]))


def forward_kernel(level, flags, own, other, high_matrix, total):
    is_high = flags[level] == 1
    high = jnp.where(is_high, own[...], other[...])
    low = jnp.where(is_high, other[...], own[...])
    total[...] = high + apply(high_matrix[...], low)


def backward_kernel(level, flags, own, other, low_matrix, total):
    is_high = flags[level] == 1
    high = jnp.where(is_high, own[...], other[...])
    low = jnp.where(is_high, other[...], own[...])
    total[...] = low + apply_transposed(low_matrix[...], high)


def gathered_kernel(wanted, operation, flags, *refs):
    others = refs[:5]
    matrices = refs[5:9]
    result = refs[9]
    result[...] = jnp.where(flags[0] == wanted, others[0][...], 0.0)
    for level in range(1, 5):

        @pl.when(flags[level] == wanted)
        def _():
            result[...] = result[...] + operation(matrices[level - 1][...], others[level][...])


def turn_kernel(flags, entering, other, prefix, transition, offset, solved, returning):
    before = entering[...] + jnp.where(flags[5] == 1, 1.0, 0.0) * apply(prefix[...], other[...])
    current = offset[...] + apply(transition[...], before)
    solved[...] = current
    returning[...] = -apply_transposed(transition[...], current)


def finish_kernel(
    flags, inverse, entering, other, suffix, solved, velocity, node_mass, nodes, velocity_out
):
    after = entering[...] + jnp.where(flags[5] == 0, 1.0, 0.0) * apply_transposed(
        suffix[...], other[...]
    )
    sign = (1 - 2 * flags[SIDE]).astype(f32)
    multiplier = sign * apply_transposed(inverse[...], solved[...] - after)
    in_row, in_column = slot_masks(nodes[...])
    chosen = in_column.astype(f32).astype(bf16)
    weight = 1.0 / node_mass[...]
    for i in range(3):
        held = jnp.where(in_row, multiplier[:, IFC * i : IFC * i + IFC], 0.0)
        change = sum(
            lax.dot_general(p, chosen, (((1,), (1,)), ((), ())), preferred_element_type=f32)
            for p in reversed(triple(held))
        )
        velocity_out[i] = velocity[i] - change.reshape(CX, CY, CZ) * weight


def bound(level, kernel, *fixed):
    def run(*refs):
        kernel(level, *fixed, *refs)

    return run


def after(value, *earlier):
    return lax.optimization_barrier((value, *earlier))[0]


def first_products(flags, transition, gate):
    cube = 6 * IB**3
    other = after(swap(transition, MASKS[0]), gate)
    high, low, merged, half = local_call(
        first_merge_kernel, flags, [transition, other], (MAT, MAT, MAT, HALFMAT), cube
    )
    prefix, suffix = local_call(first_reach_kernel, flags, [other], (MAT, MAT))
    return (merged, half), [(high, low, prefix, suffix)]


def merge_level(flags, level, block, levels, gate=None):
    cube = 6 * IB**3
    merged, half = block
    near = swap(half, MASKS[level])
    if gate is not None:
        near = after(near, gate)
    far = swap(near, 1)
    last = level == 4
    high, low, *block = local_call(
        bound(level, merge_kernel, last),
        flags,
        [merged, near, far],
        (MAT, MAT) if last else (MAT, MAT, MAT, HALFMAT),
        cube,
    )
    prefix, suffix = local_call(
        bound(level, reach_kernel), flags, [high, low, *levels[-1][2:]], (MAT, MAT), cube
    )
    return block, levels + [(high, low, prefix, suffix)]


def row_levels(flags, block, levels, gate):
    cube = 6 * IB**3
    merged, half = block
    blocks = []
    for mask in (MASKS[2], MASKS[3], OPPOSITE):
        near = after(swap(half, mask), gate)
        blocks += [near, swap(near, 1)]
    high, low, row_high, row_low, *block = local_call(
        row_kernel, flags, [merged, *blocks], (MAT,) * 5 + (HALFMAT,), 3 * cube
    )
    for level, pair in ((2, (high, low)), (3, (row_high, row_low))):
        reach = local_call(
            bound(level, reach_kernel), flags, [*pair, *levels[-1][2:]], (MAT, MAT), cube
        )
        levels = levels + [(*pair, *reach)]
    return block, levels


def coupled_velocity(
    flags, picked, inverse, transition, block, levels, velocity, node_mass, nodes
):
    square = 2 * IB * IB
    count = lax.axis_size("sub")
    partner = lax.ppermute(picked, "sub", [(i, i ^ 1) for i in range(count)])
    offset = local_call(start_kernel, flags, [inverse, picked, partner], ROW, square)
    total, others = offset, []
    for level in range(5):
        others.append(swap(total, MASKS[level]))
        if level == 2:
            block, levels = row_levels(flags, block, levels, others[-1])
        if level == 4:
            block, levels = merge_level(flags, level, block, levels, others[-1])
        others[-1] = after(others[-1], levels[max(level - 1, 1)][2])
        total = local_call(
            bound(level, forward_kernel), flags, [total, others[-1], levels[level][0]], ROW, square
        )
    _, lows, prefixes, suffixes = zip(*levels)
    last_other = swap(total, MASKS[5])
    entering = local_call(
        bound(1, gathered_kernel, apply), flags, others + list(prefixes[:4]), ROW, 4 * square
    )
    solved, returning = local_call(
        turn_kernel,
        flags,
        [entering, last_other, prefixes[4], transition, offset],
        (ROW, ROW),
        3 * square,
    )
    total, others = returning, []
    for level in range(5):
        others.append(swap(total, MASKS[level]))
        total = local_call(
            bound(level, backward_kernel), flags, [total, others[-1], lows[level]], ROW, square
        )
    last_other = swap(total, MASKS[5])
    entering = local_call(
        bound(0, gathered_kernel, apply_transposed), flags, others + list(suffixes[:4]), ROW, 4 * square
    )
    return local_call(
        finish_kernel,
        flags,
        [inverse, entering, last_other, suffixes[4], solved, velocity, node_mass, nodes],
        jax.ShapeDtypeStruct(velocity.shape, f32),
        2 * square,
    )


def outer_swap(value):
    count = lax.axis_size("tile")
    route = []
    for low in range(1, count - 1, 2):
        route += [(low, low + 1), (low + 1, low)]
    return lax.ppermute(value, "tile", route)


def body(
    displacement,
    velocity,
    external_load,
    node_mass,
    modulus,
    stiffness,
    substeps,
    interface_nodes,
    factor_inverse,
    factor_lower,
):
    sub, tile = lax.axis_index("sub"), lax.axis_index("tile")
    last = tile == lax.axis_size("tile") - 1
    flags = jnp.stack(
        [(tile >> k) & 1 for k in range(6)] + [sub // 2, sub % 2, last, substeps[0]]
    ).astype(jnp.int32)
    step = coarse_step / substeps.astype(f32)
    state = [displacement[0], velocity[0], external_load[0], node_mass[0], modulus[0]]
    packed = jax.ShapeDtypeStruct((PACKED, CY, CZ), f32)
    transition, inverse = local_call(
        transition_kernel, flags, [factor_inverse, factor_lower], (MAT, MAT), 6 * IB**3
    )
    outer, inner = local_call(pack_kernel, flags, state, (packed, packed))
    block, levels = first_products(flags, transition, outer)
    outer = outer_swap(outer)
    inner = swap(inner, 1)
    block, levels = merge_level(flags, 1, block, levels)
    outer = after(outer, block[1])
    final_displacement, final_velocity, picked = substeps_call(
        flags, step, state, outer, inner, stiffness, interface_nodes
    )
    coupled = coupled_velocity(
        flags,
        picked,
        inverse,
        transition,
        block,
        levels,
        final_velocity,
        node_mass[0],
        interface_nodes,
    )
    return final_displacement[None], coupled[None]


def solution(mesh):
    in_specs = (
        P("sub", None, "tile", None, None),
        P("sub", None, "tile", None, None),
        P("sub", None, "tile", None, None),
        P("sub", "tile", None, None),
        P("sub", "tile", None, None),
        P(),
        P("sub"),
        P("sub", "tile"),
        P(None, "tile", None),
        P(None, "tile", None),
    )
    out_specs = (P("sub", None, "tile", None, None), P("sub", None, "tile", None, None))
    return jax.shard_map(body, mesh=mesh, in_specs=in_specs, out_specs=out_specs, check_vma=False)
```

```python
import jax
import jax.numpy as jnp
from jax import lax
from jax.experimental import pallas as pl
from jax.experimental.pallas import tpu as pltpu
from jax.sharding import PartitionSpec as P

IFC = 128
IB = 384
HALF = IB // 2
GRANT = 12 << 20
CX, CY, CZ = 4, 32, 128
DEEP = 3 * CX
NEAR = CX - 1
PACKED = 37
CORE, PAIR, SIDE, LAST, STEPS = 0, 6, 7, 8, 9
GROUPS = CY // 8
MASKS = (1, 2, 4, 12, 16, 48)
ROW_MASKS = (4, 10, 12)
ROW_TILES = 16

coarse_step = 0.1
f32 = jnp.float32
bf16 = jnp.bfloat16
VM = pl.BlockSpec(memory_space=pltpu.VMEM)
SM = pl.BlockSpec(memory_space=pltpu.SMEM)
MAT = jax.ShapeDtypeStruct((IB, IB), f32)
HALFMAT = jax.ShapeDtypeStruct((HALF, IB), f32)
ROW = jax.ShapeDtypeStruct((1, IB), f32)


def swap(value, mask):
    return lax.ppermute(value, "tile", [(i, i ^ mask) for i in range(lax.axis_size("tile"))])


def cost(flops, nbytes):
    return pl.CostEstimate(flops=flops, bytes_accessed=nbytes, transcendentals=0)


def local_call(kernel, flags, operands, outs, flops=0):
    nbytes = sum(o.size * 4 for o in operands)
    return pl.pallas_call(
        kernel,
        out_shape=outs,
        in_specs=[SM] + [VM] * len(operands),
        out_specs=jax.tree.map(lambda _: VM, outs),
        compiler_params=pltpu.CompilerParams(vmem_limit_bytes=GRANT),
        cost_estimate=cost(flops, nbytes),
    )(flags, *operands)


def halves(value):
    high = value.astype(bf16)
    return high, (value - high.astype(f32)).astype(bf16)


def product(a, b):
    a_high, a_low = halves(a)
    b_high, b_low = halves(b)
    return (
        jnp.dot(a_low, b_high, preferred_element_type=f32)
        + jnp.dot(a_high, b_low, preferred_element_type=f32)
        + jnp.dot(a_high, b_high, preferred_element_type=f32)
    )


def eye_mask(size):
    return lax.broadcasted_iota(jnp.int32, (size, size), 0) == lax.broadcasted_iota(
        jnp.int32, (size, size), 1
    )


def column_to_row(column):
    eye = eye_mask(IFC)
    return jnp.concatenate(
        [
            jnp.sum(jnp.where(eye, column[k : k + IFC], 0.0), axis=0, keepdims=True)
            for k in range(0, IB, IFC)
        ],
        axis=1,
    )


def row_to_column(row):
    eye = eye_mask(IFC)
    return jnp.concatenate(
        [
            jnp.sum(jnp.where(eye, row[:, k : k + IFC], 0.0), axis=1, keepdims=True)
            for k in range(0, IB, IFC)
        ],
        axis=0,
    )


def apply(matrix, row):
    return column_to_row(jnp.sum(matrix * row, axis=1, keepdims=True))


def apply_transposed(matrix, row):
    return jnp.sum(matrix * row_to_column(row), axis=0, keepdims=True)


def triple(value):
    high = value.astype(bf16)
    rest = value - high.astype(f32)
    middle = rest.astype(bf16)
    return high, middle, (rest - middle.astype(f32)).astype(bf16)


def slot_masks(nodes):
    index = lax.broadcasted_iota(jnp.int32, (IFC, IFC), 0)
    return index == nodes // CZ, index == nodes % CZ


def wide(value):
    return jnp.concatenate([value[8 * g : 8 * g + 8] for g in range(GROUPS)], axis=1)


def tall(value):
    return jnp.concatenate([value[:, CZ * g : CZ * g + CZ] for g in range(GROUPS)], axis=0)


def spread(values):
    row = lax.broadcasted_iota(jnp.int32, (192, 24), 0) // 8
    rows = (row == lax.broadcasted_iota(jnp.int32, (192, 24), 1)).astype(f32).astype(bf16)
    block = lax.broadcasted_iota(jnp.int32, (24, 192), 1) // 8
    side = block // 12
    dof = 8 * (block % 12 // 4) + 4 * side + block % 4
    columns = (dof == lax.broadcasted_iota(jnp.int32, (24, 192), 0)).astype(f32).astype(bf16)
    tall_values = jnp.dot(rows, values, preferred_element_type=f32).astype(bf16)
    full = jnp.dot(tall_values, columns, preferred_element_type=f32)
    same = (
        lax.broadcasted_iota(jnp.int32, (192, 192), 0) % 8
        == lax.broadcasted_iota(jnp.int32, (192, 192), 1) % 8
    )
    return jnp.where(same, full, 0.0).astype(bf16)


def substep_kernel(
    flags, step, displacement, velocity, external_load, node_mass, modulus,
    outer, inner, stiffness, nodes,
    displacement_out, velocity_out, picked,
    disp, vel, load, inverse_mass, factor, stiff, even, odd, even_force, odd_force, upper,
):
    first = flags[CORE] == 0

    def put_mass(low, mass):
        present = mass > 0.0
        inverse_mass[pl.ds(low, mass.shape[0])] = jnp.where(
            present, 1.0 / jnp.where(present, mass, 1.0), 0.0
        )

    def put_factor(low, source, base):
        row = lax.broadcasted_iota(jnp.int32, (CY, CZ), 0)
        for x in range(CX):
            factor[low + x] = wide(jnp.where(row < CY - 1, source[base + x], 0.0))

    def place(source, low, shift):
        for i in range(3):
            disp[i, pl.ds(low, CX)] = source[pl.ds(CX * i, CX)]
            vel[i, pl.ds(low + shift, NEAR)] = source[pl.ds(12 + NEAR * i, NEAR)]
            load[i, pl.ds(low + shift, NEAR)] = source[pl.ds(21 + NEAR * i, NEAR)]
        put_mass(low + shift, source[pl.ds(30, NEAR)])
        put_factor(low, source, 33)

    disp[:, CX : 2 * CX] = displacement[...]
    vel[:, CX : 2 * CX] = velocity[...]
    load[:, CX : 2 * CX] = external_load[...]
    put_mass(CX, node_mass[...])
    put_factor(CX, modulus, 0)

    @pl.when(first)
    def _():
        place(outer, 0, 1)
        place(inner, 2 * CX, 0)

    @pl.when(jnp.logical_not(first))
    def _():
        place(inner, 0, 1)
        place(outer, 2 * CX, 0)

    @pl.when(flags[LAST] == 1)
    def _():
        factor[2 * CX - 1] = jnp.zeros((8, GROUPS * CZ), f32)

    high, low = [spread(s) for s in halves(stiffness[...])]
    stiff[...] = jnp.concatenate([high, high, low], axis=1)
    length = step[0]

    def put_features(layer, below, above):
        columns = []
        for i in range(3):
            base = disp[i, layer]
            turned = pltpu.roll(base, CZ - 1, 1)
            columns += [base, turned, pltpu.roll(base, CY - 1, 0), pltpu.roll(turned, CY - 1, 0)]
        for g in range(GROUPS):
            lanes = slice(CZ * g, CZ * g + CZ)
            block = jnp.concatenate([c[8 * g : 8 * g + 8] for c in columns], axis=0)
            high, low = halves(block)
            for target, start in ((below, 96), (above, 0)):
                if target is not None:
                    target[start : start + 96, lanes] = high
                    target[start + 192 : start + 288, lanes] = low
                    target[start + 384 : start + 480, lanes] = high

    def put_force(source, target):
        target[...] = jnp.dot(stiff[...], source[...], preferred_element_type=f32)

    def corner(force, scale, i, a, r):
        start = 8 * (8 * i + 4 * a + r)
        return force[start : start + 8] * scale

    def keep_upper(layer, force):
        scale = factor[layer]
        for i in range(3):
            for r in range(4):
                upper[4 * i + r] = corner(force, scale, i, 1, r)

    def finish_layer(layer, force):
        scale = factor[layer]
        weight = inverse_mass[layer]
        for i in range(3):
            sums = [corner(force, scale, i, 0, r) + upper[4 * i + r] for r in range(4)]
            s00, s01, s10, s11 = [tall(s) for s in sums]
            base = s00 + pltpu.roll(s10, 1, 0)
            turned = s01 + pltpu.roll(s11, 1, 0)
            internal = base + pltpu.roll(turned, 1, 1)
            speed = vel[i, layer] + length * ((load[i, layer] - internal) * weight)
            vel[i, layer] = speed
            disp[i, layer] = disp[i, layer] + length * speed

    def one_substep(k, carry):
        put_features(k, None, even)
        put_features(k + 1, even, odd)
        put_force(even, even_force)
        put_features(k + 2, odd, even)
        keep_upper(k, even_force)
        put_force(odd, odd_force)
        put_features(k + 3, even, odd)

        def two_layers(pair, carry):
            layer = k + 1 + 2 * pair
            put_force(even, even_force)
            put_features(layer + 3, odd, even)
            finish_layer(layer, odd_force)
            keep_upper(layer, odd_force)
            put_force(odd, odd_force)
            put_features(layer + 4, even, odd)
            finish_layer(layer + 1, even_force)
            keep_upper(layer + 1, even_force)
            return carry

        return lax.fori_loop(0, CX + 1 - k, two_layers, carry)

    lax.fori_loop(0, flags[STEPS], one_substep, 0)
    displacement_out[...] = disp[:, CX : 2 * CX]
    final = vel[:, CX : 2 * CX]
    velocity_out[...] = final
    in_row, in_column = slot_masks(nodes[...])
    chosen = in_column.astype(f32).astype(bf16)
    parts = []
    for i in range(3):
        pieces = triple(final[i].reshape(CX * CY, CZ))
        values = sum(jnp.dot(p, chosen, preferred_element_type=f32) for p in reversed(pieces))
        parts.append(jnp.sum(jnp.where(in_row, values, 0.0), axis=0, keepdims=True))
    picked[...] = jnp.concatenate(parts, axis=1)


def pack_kernel(flags, displacement, velocity, external_load, node_mass, modulus, outer, inner):
    for target, start in ((outer, flags[CORE]), (inner, 1 - flags[CORE])):
        for i in range(3):
            target[pl.ds(CX * i, CX)] = displacement[i]
            target[pl.ds(12 + NEAR * i, NEAR)] = velocity[i, pl.ds(start, NEAR)]
            target[pl.ds(21 + NEAR * i, NEAR)] = external_load[i, pl.ds(start, NEAR)]
        target[pl.ds(30, NEAR)] = node_mass[pl.ds(start, NEAR)]
        target[pl.ds(33, CX)] = modulus[...]


def substeps_call(flags, step, state, outer, inner, stiffness, nodes):
    grid_shape = (3, CX, CY, CZ)
    return pl.pallas_call(
        substep_kernel,
        out_shape=(
            jax.ShapeDtypeStruct(grid_shape, f32),
            jax.ShapeDtypeStruct(grid_shape, f32),
            ROW,
        ),
        in_specs=[SM, SM] + [VM] * 9,
        out_specs=(VM, VM, VM),
        scratch_shapes=[
            pltpu.VMEM((3, DEEP + 2, CY, CZ), f32),
            pltpu.VMEM((3, DEEP, CY, CZ), f32),
            pltpu.VMEM((3, DEEP, CY, CZ), f32),
            pltpu.VMEM((DEEP, CY, CZ), f32),
            pltpu.VMEM((DEEP, 8, GROUPS * CZ), f32),
            pltpu.VMEM((192, 576), bf16),
            pltpu.VMEM((576, GROUPS * CZ), bf16),
            pltpu.VMEM((576, GROUPS * CZ), bf16),
            pltpu.VMEM((192, GROUPS * CZ), f32),
            pltpu.VMEM((192, GROUPS * CZ), f32),
            pltpu.VMEM((12, 8, GROUPS * CZ), f32),
        ],
        compiler_params=pltpu.CompilerParams(vmem_limit_bytes=20 << 20),
        cost_estimate=cost(32 * 2 * 192 * 576 * 512, 3 * 720896),
    )(flags, step, *state, outer, inner, stiffness, nodes)

def transition_kernel(flags, inverse, lower, transition):
    transition[...] = -product(inverse[...], lower[...])


def store_half(flags, half, value_ref):
    @pl.when(flags[CORE] == 0)
    def _():
        half[...] = value_ref[:HALF]

    @pl.when(flags[CORE] == 1)
    def _():
        half[...] = value_ref[HALF:]


def first_merge_kernel(flags, own, other, high_ref, low_ref, merged, half):
    is_high = flags[0] == 1
    high = jnp.where(is_high, own[...], other[...])
    low = jnp.where(is_high, other[...], own[...])
    high_ref[...] = high
    low_ref[...] = low
    merged[...] = product(high, low)
    store_half(flags, half, merged)


def first_reach_kernel(flags, other, prefix, suffix):
    is_high = flags[0] == 1
    identity = eye_mask(IB).astype(f32)
    prefix[...] = jnp.where(is_high, other[...], identity)
    suffix[...] = jnp.where(is_high, identity, other[...])


def whole(first, near, far):
    return jnp.concatenate(
        [jnp.where(first, near[...], far[...]), jnp.where(first, far[...], near[...])], axis=0
    )


def merge_kernel(level, last, flags, own, near, far, high_ref, low_ref, *outs):
    is_high = flags[level] == 1
    other = whole(flags[CORE] == 0, near, far)
    high = jnp.where(is_high, own[...], other)
    low = jnp.where(is_high, other, own[...])
    high_ref[...] = high
    low_ref[...] = low
    if not last:
        merged, half = outs
        merged[...] = product(high, low)
        store_half(flags, half, merged)


def block_index(flags):
    return flags[2] + 2 * flags[3]


def sort_kernel(flags, own, near, far, near_far, far_far, near_across, far_across, blocks):
    first = flags[CORE] == 0
    mine = block_index(flags)
    blocks[mine] = own[...]
    for change, pieces in enumerate(((near, far), (near_far, far_far), (near_across, far_across))):
        blocks[mine ^ (change + 1)] = whole(first, *pieces)


def row_kernel(flags, blocks, high, low, merged, half):
    low[...] = product(blocks[1], blocks[0])
    high[...] = product(blocks[3], blocks[2])
    merged[...] = product(high[...], low[...])
    store_half(flags, half, merged)


def row_reach_kernel(flags, blocks, high, low, prefix, suffix, new_prefix, new_suffix):
    base = 2 * flags[3]
    is_high = flags[2] == 1
    longer = product(
        jnp.where(is_high, prefix[...], blocks[base + 1]),
        jnp.where(is_high, blocks[base], suffix[...]),
    )
    new_prefix[...] = jnp.where(is_high, longer, prefix[...])
    new_suffix[...] = jnp.where(is_high, suffix[...], longer)
    in_upper = flags[3] == 1
    longer = product(
        jnp.where(in_upper, new_prefix[...], high[...]),
        jnp.where(in_upper, low[...], new_suffix[...]),
    )
    new_prefix[...] = jnp.where(in_upper, longer, new_prefix[...])
    new_suffix[...] = jnp.where(in_upper, new_suffix[...], longer)


def ordered(flags, rows):
    mine = block_index(flags)
    result = []
    for block in range(4):
        change = mine ^ block
        value = rows[0][...]
        for k in range(1, 4):
            value = jnp.where(change == k, rows[k][...], value)
        result.append(value)
    return mine, result


def row_forward_kernel(flags, own, one, two, three, blocks, total, entering):
    mine, rows = ordered(flags, (own, one, two, three))
    state = rows[0]
    before = jnp.zeros_like(state)
    for block in range(1, 4):
        before = jnp.where(mine == block, state, before)
        state = rows[block] + apply(blocks[block], state)
    total[...] = state
    entering[...] = before


def row_backward_kernel(flags, own, one, two, three, blocks, total, entering):
    mine, rows = ordered(flags, (own, one, two, three))
    state = rows[3]
    before = jnp.zeros_like(state)
    for block in range(2, -1, -1):
        before = jnp.where(mine == block, state, before)
        state = rows[block] + apply_transposed(blocks[block], state)
    total[...] = state
    entering[...] = before


def below_row(flags, hop):
    first_row = flags[4] + flags[5] == 0
    return jnp.where(first_row, 0.0, hop[...])


def hop_kernel(flags, total, hop, merged, leaving):
    leaving[...] = total[...] + apply(merged[...], below_row(flags, hop))


def reach_kernel(level, flags, high, low, prefix, suffix, new_prefix, new_suffix):
    is_high = flags[level] == 1
    longer = product(
        jnp.where(is_high, prefix[...], high[...]), jnp.where(is_high, low[...], suffix[...])
    )
    new_prefix[...] = jnp.where(is_high, longer, prefix[...])
    new_suffix[...] = jnp.where(is_high, suffix[...], longer)


def start_kernel(flags, inverse, picked, partner, offset):
    sign = (1 - 2 * flags[SIDE]).astype(f32)
    offset[...] = apply(inverse[...], sign * (picked[...] - partner[...]))


def forward_kernel(level, flags, own, other, high_matrix, total):
    is_high = flags[level] == 1
    high = jnp.where(is_high, own[...], other[...])
    low = jnp.where(is_high, other[...], own[...])
    total[...] = high + apply(high_matrix[...], low)


def backward_kernel(level, flags, own, other, low_matrix, total):
    is_high = flags[level] == 1
    high = jnp.where(is_high, own[...], other[...])
    low = jnp.where(is_high, other[...], own[...])
    total[...] = low + apply_transposed(low_matrix[...], high)


def forward_part_kernel(flags, other_0, other_1, in_row, prefix_0, prefix_1, result):
    result[...] = jnp.where(flags[0] == 1, other_0[...], 0.0) + apply(prefix_1[...], in_row[...])

    @pl.when(flags[1] == 1)
    def _():
        result[...] = result[...] + apply(prefix_0[...], other_1[...])


def backward_part_kernel(
    flags, other_0, other_1, in_row, other_4, suffix_0, suffix_1, suffix_3, result
):
    result[...] = jnp.where(flags[0] == 0, other_0[...], 0.0) + apply_transposed(
        suffix_1[...], in_row[...]
    )

    @pl.when(flags[1] == 0)
    def _():
        result[...] = result[...] + apply_transposed(suffix_0[...], other_1[...])

    @pl.when(flags[4] == 0)
    def _():
        result[...] = result[...] + apply_transposed(suffix_3[...], other_4[...])


def turn_kernel(flags, entering, hop, prefix, transition, offset, solved, returning):
    before = entering[...] + apply(prefix[...], below_row(flags, hop))
    current = offset[...] + apply(transition[...], before)
    solved[...] = current
    returning[...] = -apply_transposed(transition[...], current)


def finish_kernel(
    flags, inverse, entering, other, suffix, solved, velocity, node_mass, nodes, velocity_out
):
    after = entering[...] + jnp.where(flags[5] == 0, 1.0, 0.0) * apply_transposed(
        suffix[...], other[...]
    )
    sign = (1 - 2 * flags[SIDE]).astype(f32)
    multiplier = sign * apply_transposed(inverse[...], solved[...] - after)
    in_row, in_column = slot_masks(nodes[...])
    chosen = in_column.astype(f32).astype(bf16)
    weight = 1.0 / node_mass[...]
    for i in range(3):
        held = jnp.where(in_row, multiplier[:, IFC * i : IFC * i + IFC], 0.0)
        change = sum(
            lax.dot_general(p, chosen, (((1,), (1,)), ((), ())), preferred_element_type=f32)
            for p in reversed(triple(held))
        )
        velocity_out[i] = velocity[i] - change.reshape(CX, CY, CZ) * weight


def bound(level, kernel, *fixed):
    def run(*refs):
        kernel(level, *fixed, *refs)

    return run


def after(value, *earlier):
    return lax.optimization_barrier((value, *earlier))[0]


def first_products(flags, transition, gate):
    cube = 6 * IB**3
    other = after(swap(transition, MASKS[0]), gate)
    high, low, merged, half = local_call(
        first_merge_kernel, flags, [transition, other], (MAT, MAT, MAT, HALFMAT), cube
    )
    prefix, suffix = local_call(first_reach_kernel, flags, [other], (MAT, MAT))
    return (merged, half), [(high, low, prefix, suffix)]


def merge_level(flags, level, block, levels, gate=None):
    cube = 6 * IB**3
    merged, half = block
    near = swap(half, MASKS[level])
    if gate is not None:
        near = after(near, gate)
    far = swap(near, 1)
    last = level == 4
    high, low, *block = local_call(
        bound(level, merge_kernel, last),
        flags,
        [merged, near, far],
        (MAT, MAT) if last else (MAT, MAT, MAT, HALFMAT),
        cube,
    )
    prefix, suffix = local_call(
        bound(level, reach_kernel), flags, [high, low, *levels[-1][2:]], (MAT, MAT), cube
    )
    return block, levels + [(high, low, prefix, suffix)]


def sorted_blocks(flags, block, gate):
    merged, half = block
    pieces = []
    for mask in ROW_MASKS:
        near = after(swap(half, mask), gate)
        pieces += [near, swap(near, 1)]
    return local_call(
        sort_kernel, flags, [merged, *pieces], jax.ShapeDtypeStruct((4, IB, IB), f32)
    )


def coupled_velocity(
    flags, picked, inverse, transition, block, levels, velocity, node_mass, nodes
):
    square = 2 * IB * IB
    cube = 6 * IB**3
    prefix_0, suffix_0 = levels[0][2:]
    prefix_1, suffix_1 = levels[1][2:]
    count = lax.axis_size("sub")
    partner = lax.ppermute(picked, "sub", [(i, i ^ 1) for i in range(count)])
    offset = local_call(start_kernel, flags, [inverse, picked, partner], ROW, square)
    total, others = offset, []
    for level in range(2):
        others.append(after(swap(total, MASKS[level]), prefix_1))
        total = local_call(
            bound(level, forward_kernel), flags, [total, others[-1], levels[level][0]], ROW, square
        )
    arrived = [swap(total, mask) for mask in ROW_MASKS]
    blocks = sorted_blocks(flags, block, total)
    total, in_row = local_call(
        row_forward_kernel, flags, [total, *arrived, blocks], (ROW, ROW), 3 * square
    )
    high, low, *row = local_call(
        row_kernel, flags, [after(blocks, total)], (MAT, MAT, MAT, HALFMAT), 3 * cube
    )
    merged = row[0]
    hop = up_row(total)
    hop = after(hop, merged)
    leaving = local_call(hop_kernel, flags, [total, hop, merged], ROW, square)
    hop = up_row(leaving)
    prefix_3, suffix_3 = local_call(
        row_reach_kernel, flags, [blocks, high, low, prefix_1, suffix_1], (MAT, MAT), 2 * cube
    )
    row[1] = after(row[1], hop)
    hop = after(hop, prefix_3)
    leaving = local_call(hop_kernel, flags, [total, hop, merged], ROW, square)
    hop = up_row(leaving)
    entering = local_call(
        forward_part_kernel, flags, [*others, in_row, prefix_0, prefix_1], ROW, 2 * square
    )
    hop = after(hop, entering)
    solved, returning = local_call(
        turn_kernel,
        flags,
        [entering, hop, prefix_3, transition, offset],
        (ROW, ROW),
        3 * square,
    )
    total, others = returning, []
    for level in range(2):
        others.append(swap(total, MASKS[level]))
        total = local_call(
            bound(level, backward_kernel), flags, [total, others[-1], levels[level][1]], ROW, square
        )
    arrived = [swap(total, mask) for mask in ROW_MASKS]
    row, levels = merge_level(
        flags, 4, row, levels + [None, (None, None, prefix_3, suffix_3)], solved
    )
    _, low, _, suffix_4 = levels[4]
    arrived[-1] = after(arrived[-1], low)
    total, in_row = local_call(
        row_backward_kernel, flags, [total, *arrived, blocks], (ROW, ROW), 3 * square
    )
    others.append(swap(total, MASKS[4]))
    total = local_call(
        bound(4, backward_kernel), flags, [total, after(others[-1], suffix_4), low], ROW, square
    )
    last_other = swap(total, MASKS[5])
    entering = local_call(
        backward_part_kernel,
        flags,
        [others[0], others[1], in_row, others[2], suffix_0, suffix_1, suffix_3],
        ROW,
        3 * square,
    )
    return local_call(
        finish_kernel,
        flags,
        [inverse, entering, after(last_other, entering), suffix_4, solved, velocity, node_mass, nodes],
        jax.ShapeDtypeStruct(velocity.shape, f32),
        2 * square,
    )


def up_row(value):
    count = lax.axis_size("tile")
    return lax.ppermute(value, "tile", [(i, (i + ROW_TILES) % count) for i in range(count)])


def outer_swap(value):
    count = lax.axis_size("tile")
    route = []
    for low in range(1, count - 1, 2):
        route += [(low, low + 1), (low + 1, low)]
    return lax.ppermute(value, "tile", route)


def body(
    displacement,
    velocity,
    external_load,
    node_mass,
    modulus,
    stiffness,
    substeps,
    interface_nodes,
    factor_inverse,
    factor_lower,
):
    sub, tile = lax.axis_index("sub"), lax.axis_index("tile")
    last = tile == lax.axis_size("tile") - 1
    flags = jnp.stack(
        [(tile >> k) & 1 for k in range(6)] + [sub // 2, sub % 2, last, substeps[0]]
    ).astype(jnp.int32)
    step = coarse_step / substeps.astype(f32)
    state = [displacement[0], velocity[0], external_load[0], node_mass[0], modulus[0]]
    packed = jax.ShapeDtypeStruct((PACKED, CY, CZ), f32)
    inverse = lax.dynamic_index_in_dim(factor_inverse, sub // 2, 0, keepdims=False)
    lower = lax.dynamic_index_in_dim(factor_lower, sub // 2, 0, keepdims=False)
    transition = local_call(transition_kernel, flags, [inverse, lower], MAT, 6 * IB**3)
    outer, inner = local_call(pack_kernel, flags, state, (packed, packed))
    block, levels = first_products(flags, transition, outer)
    outer = outer_swap(outer)
    inner = swap(inner, 1)
    block = (block[0], after(block[1], inner))
    block, levels = merge_level(flags, 1, block, levels)
    outer = after(outer, block[1])
    final_displacement, final_velocity, picked = substeps_call(
        flags, step, state, outer, inner, stiffness, interface_nodes
    )
    coupled = coupled_velocity(
        flags,
        picked,
        inverse,
        transition,
        block,
        levels,
        final_velocity,
        node_mass[0],
        interface_nodes,
    )
    return final_displacement[None], coupled[None]


def solution(mesh):
    in_specs = (
        P("sub", None, "tile", None, None),
        P("sub", None, "tile", None, None),
        P("sub", None, "tile", None, None),
        P("sub", "tile", None, None),
        P("sub", "tile", None, None),
        P(),
        P("sub"),
        P("sub", "tile"),
        P(None, "tile", None),
        P(None, "tile", None),
    )
    out_specs = (P("sub", None, "tile", None, None), P("sub", None, "tile", None, None))
    return jax.shard_map(body, mesh=mesh, in_specs=in_specs, out_specs=out_specs, check_vma=False)
```

```python
import jax
import jax.numpy as jnp
from jax import lax
from jax.experimental import pallas as pl
from jax.experimental.pallas import tpu as pltpu
from jax.sharding import PartitionSpec as P

IFC = 128
IB = 384
HALF = IB // 2
GRANT = 12 << 20
CX, CY, CZ = 4, 32, 128
DEEP = 3 * CX
NEAR = CX - 1
PACKED = 37
CORE, PAIR, SIDE, LAST, STEPS = 0, 6, 7, 8, 9
GROUPS = CY // 8
MASKS = (1, 2, 4, 12, 16, 48)
SPLIT_MASKS = (4, 12)
OPPOSITE = 10
ROW_TILES = 16

coarse_step = 0.1
f32 = jnp.float32
bf16 = jnp.bfloat16
VM = pl.BlockSpec(memory_space=pltpu.VMEM)
SM = pl.BlockSpec(memory_space=pltpu.SMEM)
MAT = jax.ShapeDtypeStruct((IB, IB), f32)
HALFMAT = jax.ShapeDtypeStruct((HALF, IB), f32)
ROW = jax.ShapeDtypeStruct((1, IB), f32)


def swap(value, mask):
    return lax.ppermute(value, "tile", [(i, i ^ mask) for i in range(lax.axis_size("tile"))])


def cost(flops, nbytes):
    return pl.CostEstimate(flops=flops, bytes_accessed=nbytes, transcendentals=0)


def local_call(kernel, flags, operands, outs, flops=0):
    nbytes = sum(o.size * 4 for o in operands)
    return pl.pallas_call(
        kernel,
        out_shape=outs,
        in_specs=[SM] + [VM] * len(operands),
        out_specs=jax.tree.map(lambda _: VM, outs),
        compiler_params=pltpu.CompilerParams(vmem_limit_bytes=GRANT),
        cost_estimate=cost(flops, nbytes),
    )(flags, *operands)


def halves(value):
    high = value.astype(bf16)
    return high, (value - high.astype(f32)).astype(bf16)


def product(a, b):
    a_high, a_low = halves(a)
    b_high, b_low = halves(b)
    return (
        jnp.dot(a_low, b_high, preferred_element_type=f32)
        + jnp.dot(a_high, b_low, preferred_element_type=f32)
        + jnp.dot(a_high, b_high, preferred_element_type=f32)
    )


def eye_mask(size):
    return lax.broadcasted_iota(jnp.int32, (size, size), 0) == lax.broadcasted_iota(
        jnp.int32, (size, size), 1
    )


def column_to_row(column):
    eye = eye_mask(IFC)
    return jnp.concatenate(
        [
            jnp.sum(jnp.where(eye, column[k : k + IFC], 0.0), axis=0, keepdims=True)
            for k in range(0, IB, IFC)
        ],
        axis=1,
    )


def row_to_column(row):
    eye = eye_mask(IFC)
    return jnp.concatenate(
        [
            jnp.sum(jnp.where(eye, row[:, k : k + IFC], 0.0), axis=1, keepdims=True)
            for k in range(0, IB, IFC)
        ],
        axis=0,
    )


def apply(matrix, row):
    return column_to_row(jnp.sum(matrix * row, axis=1, keepdims=True))


def apply_transposed(matrix, row):
    return jnp.sum(matrix * row_to_column(row), axis=0, keepdims=True)


def triple(value):
    high = value.astype(bf16)
    rest = value - high.astype(f32)
    middle = rest.astype(bf16)
    return high, middle, (rest - middle.astype(f32)).astype(bf16)


def slot_masks(nodes):
    index = lax.broadcasted_iota(jnp.int32, (IFC, IFC), 0)
    return index == nodes // CZ, index == nodes % CZ


def wide(value):
    return jnp.concatenate([value[8 * g : 8 * g + 8] for g in range(GROUPS)], axis=1)


def tall(value):
    return jnp.concatenate([value[:, CZ * g : CZ * g + CZ] for g in range(GROUPS)], axis=0)


def spread(values):
    row = lax.broadcasted_iota(jnp.int32, (192, 24), 0) // 8
    rows = (row == lax.broadcasted_iota(jnp.int32, (192, 24), 1)).astype(f32).astype(bf16)
    block = lax.broadcasted_iota(jnp.int32, (24, 192), 1) // 8
    side = block // 12
    dof = 8 * (block % 12 // 4) + 4 * side + block % 4
    columns = (dof == lax.broadcasted_iota(jnp.int32, (24, 192), 0)).astype(f32).astype(bf16)
    tall_values = jnp.dot(rows, values, preferred_element_type=f32).astype(bf16)
    full = jnp.dot(tall_values, columns, preferred_element_type=f32)
    same = (
        lax.broadcasted_iota(jnp.int32, (192, 192), 0) % 8
        == lax.broadcasted_iota(jnp.int32, (192, 192), 1) % 8
    )
    return jnp.where(same, full, 0.0).astype(bf16)


def substep_kernel(
    flags, step, displacement, velocity, external_load, node_mass, modulus,
    outer, inner, stiffness, nodes,
    displacement_out, velocity_out, picked,
    disp, vel, load, inverse_mass, factor, stiff, even, odd, even_force, odd_force, upper,
):
    first = flags[CORE] == 0

    def put_mass(low, mass):
        present = mass > 0.0
        inverse_mass[pl.ds(low, mass.shape[0])] = jnp.where(
            present, 1.0 / jnp.where(present, mass, 1.0), 0.0
        )

    def put_factor(low, source, base):
        row = lax.broadcasted_iota(jnp.int32, (CY, CZ), 0)
        for x in range(CX):
            factor[low + x] = wide(jnp.where(row < CY - 1, source[base + x], 0.0))

    def place(source, low, shift):
        for i in range(3):
            disp[i, pl.ds(low, CX)] = source[pl.ds(CX * i, CX)]
            vel[i, pl.ds(low + shift, NEAR)] = source[pl.ds(12 + NEAR * i, NEAR)]
            load[i, pl.ds(low + shift, NEAR)] = source[pl.ds(21 + NEAR * i, NEAR)]
        put_mass(low + shift, source[pl.ds(30, NEAR)])
        put_factor(low, source, 33)

    disp[:, CX : 2 * CX] = displacement[...]
    vel[:, CX : 2 * CX] = velocity[...]
    load[:, CX : 2 * CX] = external_load[...]
    put_mass(CX, node_mass[...])
    put_factor(CX, modulus, 0)

    @pl.when(first)
    def _():
        place(outer, 0, 1)
        place(inner, 2 * CX, 0)

    @pl.when(jnp.logical_not(first))
    def _():
        place(inner, 0, 1)
        place(outer, 2 * CX, 0)

    @pl.when(flags[LAST] == 1)
    def _():
        factor[2 * CX - 1] = jnp.zeros((8, GROUPS * CZ), f32)

    high, low = [spread(s) for s in halves(stiffness[...])]
    stiff[...] = jnp.concatenate([high, high, low], axis=1)
    length = step[0]

    def put_features(layer, below, above):
        columns = []
        for i in range(3):
            base = disp[i, layer]
            turned = pltpu.roll(base, CZ - 1, 1)
            columns += [base, turned, pltpu.roll(base, CY - 1, 0), pltpu.roll(turned, CY - 1, 0)]
        for g in range(GROUPS):
            lanes = slice(CZ * g, CZ * g + CZ)
            block = jnp.concatenate([c[8 * g : 8 * g + 8] for c in columns], axis=0)
            high, low = halves(block)
            for target, start in ((below, 96), (above, 0)):
                if target is not None:
                    target[start : start + 96, lanes] = high
                    target[start + 192 : start + 288, lanes] = low
                    target[start + 384 : start + 480, lanes] = high

    def put_force(source, target):
        target[...] = jnp.dot(stiff[...], source[...], preferred_element_type=f32)

    def corner(force, scale, i, a, r):
        start = 8 * (8 * i + 4 * a + r)
        return force[start : start + 8] * scale

    def keep_upper(layer, force):
        scale = factor[layer]
        for i in range(3):
            for r in range(4):
                upper[4 * i + r] = corner(force, scale, i, 1, r)

    def finish_layer(layer, force):
        scale = factor[layer]
        weight = inverse_mass[layer]
        for i in range(3):
            sums = [corner(force, scale, i, 0, r) + upper[4 * i + r] for r in range(4)]
            s00, s01, s10, s11 = [tall(s) for s in sums]
            base = s00 + pltpu.roll(s10, 1, 0)
            turned = s01 + pltpu.roll(s11, 1, 0)
            internal = base + pltpu.roll(turned, 1, 1)
            speed = vel[i, layer] + length * ((load[i, layer] - internal) * weight)
            vel[i, layer] = speed
            disp[i, layer] = disp[i, layer] + length * speed

    def one_substep(k, carry):
        put_features(k, None, even)
        put_features(k + 1, even, odd)
        put_force(even, even_force)
        put_features(k + 2, odd, even)
        keep_upper(k, even_force)
        put_force(odd, odd_force)
        put_features(k + 3, even, odd)

        def two_layers(pair, carry):
            layer = k + 1 + 2 * pair
            put_force(even, even_force)
            put_features(layer + 3, odd, even)
            finish_layer(layer, odd_force)
            keep_upper(layer, odd_force)
            put_force(odd, odd_force)
            put_features(layer + 4, even, odd)
            finish_layer(layer + 1, even_force)
            keep_upper(layer + 1, even_force)
            return carry

        return lax.fori_loop(0, CX + 1 - k, two_layers, carry)

    lax.fori_loop(0, flags[STEPS], one_substep, 0)
    displacement_out[...] = disp[:, CX : 2 * CX]
    final = vel[:, CX : 2 * CX]
    velocity_out[...] = final
    in_row, in_column = slot_masks(nodes[...])
    chosen = in_column.astype(f32).astype(bf16)
    parts = []
    for i in range(3):
        pieces = triple(final[i].reshape(CX * CY, CZ))
        values = sum(jnp.dot(p, chosen, preferred_element_type=f32) for p in reversed(pieces))
        parts.append(jnp.sum(jnp.where(in_row, values, 0.0), axis=0, keepdims=True))
    picked[...] = jnp.concatenate(parts, axis=1)


def pack_kernel(flags, displacement, velocity, external_load, node_mass, modulus, outer, inner):
    for target, start in ((outer, flags[CORE]), (inner, 1 - flags[CORE])):
        for i in range(3):
            target[pl.ds(CX * i, CX)] = displacement[i]
            target[pl.ds(12 + NEAR * i, NEAR)] = velocity[i, pl.ds(start, NEAR)]
            target[pl.ds(21 + NEAR * i, NEAR)] = external_load[i, pl.ds(start, NEAR)]
        target[pl.ds(30, NEAR)] = node_mass[pl.ds(start, NEAR)]
        target[pl.ds(33, CX)] = modulus[...]


def substeps_call(flags, step, state, outer, inner, stiffness, nodes):
    grid_shape = (3, CX, CY, CZ)
    return pl.pallas_call(
        substep_kernel,
        out_shape=(
            jax.ShapeDtypeStruct(grid_shape, f32),
            jax.ShapeDtypeStruct(grid_shape, f32),
            ROW,
        ),
        in_specs=[SM, SM] + [VM] * 9,
        out_specs=(VM, VM, VM),
        scratch_shapes=[
            pltpu.VMEM((3, DEEP + 2, CY, CZ), f32),
            pltpu.VMEM((3, DEEP, CY, CZ), f32),
            pltpu.VMEM((3, DEEP, CY, CZ), f32),
            pltpu.VMEM((DEEP, CY, CZ), f32),
            pltpu.VMEM((DEEP, 8, GROUPS * CZ), f32),
            pltpu.VMEM((192, 576), bf16),
            pltpu.VMEM((576, GROUPS * CZ), bf16),
            pltpu.VMEM((576, GROUPS * CZ), bf16),
            pltpu.VMEM((192, GROUPS * CZ), f32),
            pltpu.VMEM((192, GROUPS * CZ), f32),
            pltpu.VMEM((12, 8, GROUPS * CZ), f32),
        ],
        compiler_params=pltpu.CompilerParams(vmem_limit_bytes=20 << 20),
        cost_estimate=cost(32 * 2 * 192 * 576 * 512, 3 * 720896),
    )(flags, step, *state, outer, inner, stiffness, nodes)

def transition_kernel(flags, inverse, lower, transition):
    transition[...] = -product(inverse[...], lower[...])


def store_half(flags, half, value_ref):
    @pl.when(flags[CORE] == 0)
    def _():
        half[...] = value_ref[:HALF]

    @pl.when(flags[CORE] == 1)
    def _():
        half[...] = value_ref[HALF:]


def first_merge_kernel(flags, own, other, high_ref, low_ref, merged, half):
    is_high = flags[0] == 1
    high = jnp.where(is_high, own[...], other[...])
    low = jnp.where(is_high, other[...], own[...])
    high_ref[...] = high
    low_ref[...] = low
    merged[...] = product(high, low)
    store_half(flags, half, merged)


def first_reach_kernel(flags, other, prefix, suffix):
    is_high = flags[0] == 1
    identity = eye_mask(IB).astype(f32)
    prefix[...] = jnp.where(is_high, other[...], identity)
    suffix[...] = jnp.where(is_high, identity, other[...])


def whole(first, near, far):
    return jnp.concatenate(
        [jnp.where(first, near[...], far[...]), jnp.where(first, far[...], near[...])], axis=0
    )


def merge_kernel(level, last, flags, own, near, far, high_ref, low_ref, *outs):
    is_high = flags[level] == 1
    other = whole(flags[CORE] == 0, near, far)
    high = jnp.where(is_high, own[...], other)
    low = jnp.where(is_high, other, own[...])
    high_ref[...] = high
    low_ref[...] = low
    if not last:
        merged, half = outs
        merged[...] = product(high, low)
        store_half(flags, half, merged)


def block_index(flags):
    return flags[2] + 2 * flags[3]


def sort_kernel(flags, own, near, far, near_far, far_far, near_across, far_across, blocks):
    first = flags[CORE] == 0
    mine = block_index(flags)
    blocks[mine] = own[...]
    for change, pieces in enumerate(((near, far), (near_far, far_far), (near_across, far_across))):
        blocks[mine ^ (change + 1)] = whole(first, *pieces)


def row_kernel(flags, blocks, high, low, merged, half):
    low[...] = product(blocks[1], blocks[0])
    high[...] = product(blocks[3], blocks[2])
    merged[...] = product(high[...], low[...])
    store_half(flags, half, merged)


def row_reach_kernel(flags, blocks, high, low, prefix, suffix, new_prefix, new_suffix):
    base = 2 * flags[3]
    is_high = flags[2] == 1
    longer = product(
        jnp.where(is_high, prefix[...], blocks[base + 1]),
        jnp.where(is_high, blocks[base], suffix[...]),
    )
    new_prefix[...] = jnp.where(is_high, longer, prefix[...])
    new_suffix[...] = jnp.where(is_high, suffix[...], longer)
    in_upper = flags[3] == 1
    longer = product(
        jnp.where(in_upper, new_prefix[...], high[...]),
        jnp.where(in_upper, low[...], new_suffix[...]),
    )
    new_prefix[...] = jnp.where(in_upper, longer, new_prefix[...])
    new_suffix[...] = jnp.where(in_upper, new_suffix[...], longer)


def ordered(flags, rows):
    mine = block_index(flags)
    first = flags[CORE] == 0
    own, split, other_split, opposite = [row[...] for row in rows]
    one = jnp.where(first, split, other_split)
    three = jnp.where(first, other_split, split)
    result = []
    for block in range(4):
        change = mine ^ block
        value = jnp.where(change == 1, one, own)
        value = jnp.where(change == 2, opposite, value)
        result.append(jnp.where(change == 3, three, value))
    return mine, result


def row_forward_kernel(flags, own, split, other_split, opposite, blocks, total, entering):
    mine, rows = ordered(flags, (own, split, other_split, opposite))
    state = rows[0]
    before = jnp.zeros_like(state)
    for block in range(1, 4):
        before = jnp.where(mine == block, state, before)
        state = rows[block] + apply(blocks[block], state)
    total[...] = state
    entering[...] = before


def row_backward_kernel(flags, own, split, other_split, opposite, blocks, total, entering):
    mine, rows = ordered(flags, (own, split, other_split, opposite))
    state = rows[3]
    before = jnp.zeros_like(state)
    for block in range(2, -1, -1):
        before = jnp.where(mine == block, state, before)
        state = rows[block] + apply_transposed(blocks[block], state)
    total[...] = state
    entering[...] = before


def below_row(flags, hop):
    first_row = flags[4] + flags[5] == 0
    return jnp.where(first_row, 0.0, hop[...])


def hop_kernel(flags, total, hop, merged, leaving):
    leaving[...] = total[...] + apply(merged[...], below_row(flags, hop))


def reach_kernel(level, flags, high, low, prefix, suffix, new_prefix, new_suffix):
    is_high = flags[level] == 1
    longer = product(
        jnp.where(is_high, prefix[...], high[...]), jnp.where(is_high, low[...], suffix[...])
    )
    new_prefix[...] = jnp.where(is_high, longer, prefix[...])
    new_suffix[...] = jnp.where(is_high, suffix[...], longer)


def start_kernel(flags, inverse, picked, partner, offset):
    sign = (1 - 2 * flags[SIDE]).astype(f32)
    offset[...] = apply(inverse[...], sign * (picked[...] - partner[...]))


def forward_kernel(level, flags, own, other, high_matrix, total):
    is_high = flags[level] == 1
    high = jnp.where(is_high, own[...], other[...])
    low = jnp.where(is_high, other[...], own[...])
    total[...] = high + apply(high_matrix[...], low)


def backward_kernel(level, flags, own, other, low_matrix, total):
    is_high = flags[level] == 1
    high = jnp.where(is_high, own[...], other[...])
    low = jnp.where(is_high, other[...], own[...])
    total[...] = low + apply_transposed(low_matrix[...], high)


def forward_part_kernel(flags, other_0, other_1, in_row, prefix_0, prefix_1, result):
    result[...] = jnp.where(flags[0] == 1, other_0[...], 0.0) + apply(prefix_1[...], in_row[...])

    @pl.when(flags[1] == 1)
    def _():
        result[...] = result[...] + apply(prefix_0[...], other_1[...])


def backward_part_kernel(
    flags, other_0, other_1, in_row, other_4, suffix_0, suffix_1, suffix_3, result
):
    result[...] = jnp.where(flags[0] == 0, other_0[...], 0.0) + apply_transposed(
        suffix_1[...], in_row[...]
    )

    @pl.when(flags[1] == 0)
    def _():
        result[...] = result[...] + apply_transposed(suffix_0[...], other_1[...])

    @pl.when(flags[4] == 0)
    def _():
        result[...] = result[...] + apply_transposed(suffix_3[...], other_4[...])


def turn_kernel(flags, entering, hop, prefix, transition, offset, solved, returning):
    before = entering[...] + apply(prefix[...], below_row(flags, hop))
    current = offset[...] + apply(transition[...], before)
    solved[...] = current
    returning[...] = -apply_transposed(transition[...], current)


def finish_kernel(
    flags, inverse, entering, other, suffix, solved, velocity, node_mass, nodes, velocity_out
):
    after = entering[...] + jnp.where(flags[5] == 0, 1.0, 0.0) * apply_transposed(
        suffix[...], other[...]
    )
    sign = (1 - 2 * flags[SIDE]).astype(f32)
    multiplier = sign * apply_transposed(inverse[...], solved[...] - after)
    in_row, in_column = slot_masks(nodes[...])
    chosen = in_column.astype(f32).astype(bf16)
    weight = 1.0 / node_mass[...]
    for i in range(3):
        held = jnp.where(in_row, multiplier[:, IFC * i : IFC * i + IFC], 0.0)
        change = sum(
            lax.dot_general(p, chosen, (((1,), (1,)), ((), ())), preferred_element_type=f32)
            for p in reversed(triple(held))
        )
        velocity_out[i] = velocity[i] - change.reshape(CX, CY, CZ) * weight


def bound(level, kernel, *fixed):
    def run(*refs):
        kernel(level, *fixed, *refs)

    return run


def after(value, *earlier):
    return lax.optimization_barrier((value, *earlier))[0]


def first_products(flags, transition, gate):
    cube = 6 * IB**3
    other = after(swap(transition, MASKS[0]), gate)
    high, low, merged, half = local_call(
        first_merge_kernel, flags, [transition, other], (MAT, MAT, MAT, HALFMAT), cube
    )
    prefix, suffix = local_call(first_reach_kernel, flags, [other], (MAT, MAT))
    return (merged, half), [(high, low, prefix, suffix)]


def merge_level(flags, level, block, levels, near):
    cube = 6 * IB**3
    merged, half = block
    far = swap(near, 1)
    last = level == 4
    high, low, *block = local_call(
        bound(level, merge_kernel, last),
        flags,
        [merged, near, far],
        (MAT, MAT) if last else (MAT, MAT, MAT, HALFMAT),
        cube,
    )
    prefix, suffix = local_call(
        bound(level, reach_kernel), flags, [high, low, *levels[-1][2:]], (MAT, MAT), cube
    )
    return block, levels + [(high, low, prefix, suffix)]


def split_swap(value):
    masks = [SPLIT_MASKS[i & 1] for i in range(lax.axis_size("tile"))]
    return lax.ppermute(value, "tile", [(i, i ^ mask) for i, mask in enumerate(masks)])


def row_exchange(total):
    opposite = swap(total, OPPOSITE)
    split = split_swap(total)
    return [split, swap(split, 1), opposite]


def sorted_blocks(flags, fetched, gate):
    merged, nears = fetched
    pieces = []
    for near in nears:
        near = after(near, *gate)
        pieces += [near, swap(near, 1)]
    return local_call(
        sort_kernel, flags, [merged, *pieces], jax.ShapeDtypeStruct((4, IB, IB), f32)
    )


def coupled_velocity(
    flags, picked, inverse, transition, fetched, levels, velocity, node_mass, nodes
):
    square = 2 * IB * IB
    cube = 6 * IB**3
    prefix_0, suffix_0 = levels[0][2:]
    prefix_1, suffix_1 = levels[1][2:]
    count = lax.axis_size("sub")
    partner = lax.ppermute(picked, "sub", [(i, i ^ 1) for i in range(count)])
    offset = local_call(start_kernel, flags, [inverse, picked, partner], ROW, square)
    total, others = offset, []
    for level in range(2):
        others.append(after(swap(total, MASKS[level]), prefix_1))
        total = local_call(
            bound(level, forward_kernel), flags, [total, others[-1], levels[level][0]], ROW, square
        )
    arrived = row_exchange(total)
    blocks = sorted_blocks(flags, fetched, (arrived[0], arrived[2]))
    total, in_row = local_call(
        row_forward_kernel, flags, [total, *arrived, blocks], (ROW, ROW), 3 * square
    )
    high, low, *row = local_call(
        row_kernel, flags, [after(blocks, total)], (MAT, MAT, MAT, HALFMAT), 3 * cube
    )
    merged = row[0]
    hop = up_row(total)
    hop = after(hop, merged)
    leaving = local_call(hop_kernel, flags, [total, hop, merged], ROW, square)
    hop = up_row(leaving)
    prefix_3, suffix_3 = local_call(
        row_reach_kernel, flags, [blocks, high, low, prefix_1, suffix_1], (MAT, MAT), 2 * cube
    )
    hop = after(hop, prefix_3)
    leaving = local_call(hop_kernel, flags, [total, hop, merged], ROW, square)
    hop = up_row(leaving)
    entering = local_call(
        forward_part_kernel, flags, [*others, in_row, prefix_0, prefix_1], ROW, 2 * square
    )
    hop = after(hop, entering)
    row[1] = after(row[1], entering)
    solved, returning = local_call(
        turn_kernel,
        flags,
        [entering, hop, prefix_3, transition, offset],
        (ROW, ROW),
        3 * square,
    )
    total, others = returning, []
    for level in range(2):
        others.append(swap(total, MASKS[level]))
        total = local_call(
            bound(level, backward_kernel), flags, [total, others[-1], levels[level][1]], ROW, square
        )
    arrived = row_exchange(total)
    near = after(swap(row[1], MASKS[4]), total)
    row, levels = merge_level(
        flags, 4, row, levels + [None, (None, None, prefix_3, suffix_3)], near
    )
    _, low, _, suffix_4 = levels[4]
    arrived[-1] = after(arrived[-1], low)
    total, in_row = local_call(
        row_backward_kernel, flags, [total, *arrived, blocks], (ROW, ROW), 3 * square
    )
    others.append(swap(total, MASKS[4]))
    total = local_call(
        bound(4, backward_kernel), flags, [total, after(others[-1], suffix_4), low], ROW, square
    )
    last_other = swap(total, MASKS[5])
    entering = local_call(
        backward_part_kernel,
        flags,
        [others[0], others[1], in_row, others[2], suffix_0, suffix_1, suffix_3],
        ROW,
        3 * square,
    )
    return local_call(
        finish_kernel,
        flags,
        [inverse, entering, after(last_other, entering), suffix_4, solved, velocity, node_mass, nodes],
        jax.ShapeDtypeStruct(velocity.shape, f32),
        2 * square,
    )


def up_row(value):
    count = lax.axis_size("tile")
    return lax.ppermute(value, "tile", [(i, (i + ROW_TILES) % count) for i in range(count)])


def outer_swap(value):
    count = lax.axis_size("tile")
    route = []
    for low in range(1, count - 1, 2):
        route += [(low, low + 1), (low + 1, low)]
    return lax.ppermute(value, "tile", route)


def body(
    displacement,
    velocity,
    external_load,
    node_mass,
    modulus,
    stiffness,
    substeps,
    interface_nodes,
    factor_inverse,
    factor_lower,
):
    sub, tile = lax.axis_index("sub"), lax.axis_index("tile")
    last = tile == lax.axis_size("tile") - 1
    flags = jnp.stack(
        [(tile >> k) & 1 for k in range(6)] + [sub // 2, sub % 2, last, substeps[0]]
    ).astype(jnp.int32)
    step = coarse_step / substeps.astype(f32)
    state = [displacement[0], velocity[0], external_load[0], node_mass[0], modulus[0]]
    packed = jax.ShapeDtypeStruct((PACKED, CY, CZ), f32)
    inverse = lax.dynamic_index_in_dim(factor_inverse, sub // 2, 0, keepdims=False)
    lower = lax.dynamic_index_in_dim(factor_lower, sub // 2, 0, keepdims=False)
    transition = local_call(transition_kernel, flags, [inverse, lower], MAT, 6 * IB**3)
    outer, inner = local_call(pack_kernel, flags, state, (packed, packed))
    block, levels = first_products(flags, transition, outer)
    inner = swap(inner, 1)
    near = swap(after(block[1], inner), MASKS[1])
    outer = outer_swap(after(outer, near))
    block, levels = merge_level(flags, 1, block, levels, near)
    merged, half = block
    fetched = merged, [swap(half, mask) for mask in (SPLIT_MASKS[0], OPPOSITE, SPLIT_MASKS[1])]
    outer = after(outer, half)
    final_displacement, final_velocity, picked = substeps_call(
        flags, step, state, outer, inner, stiffness, interface_nodes
    )
    coupled = coupled_velocity(
        flags,
        picked,
        inverse,
        transition,
        fetched,
        levels,
        final_velocity,
        node_mass[0],
        interface_nodes,
    )
    return final_displacement[None], coupled[None]


def solution(mesh):
    in_specs = (
        P("sub", None, "tile", None, None),
        P("sub", None, "tile", None, None),
        P("sub", None, "tile", None, None),
        P("sub", "tile", None, None),
        P("sub", "tile", None, None),
        P(),
        P("sub"),
        P("sub", "tile"),
        P(None, "tile", None),
        P(None, "tile", None),
    )
    out_specs = (P("sub", None, "tile", None, None), P("sub", None, "tile", None, None))
    return jax.shard_map(body, mesh=mesh, in_specs=in_specs, out_specs=out_specs, check_vma=False)
```

```python
import jax
import jax.numpy as jnp
from jax import lax
from jax.experimental import pallas as pl
from jax.experimental.pallas import tpu as pltpu
from jax.sharding import PartitionSpec as P

IFC = 128
IB = 384
HALF = IB // 2
GRANT = 12 << 20
CX, CY, CZ = 4, 32, 128
DEEP = 3 * CX
NEAR = CX - 1
PACKED = 37
CORE, PAIR, SIDE, LAST, STEPS = 0, 6, 7, 8, 9
GROUPS = CY // 8
MASKS = (1, 2, 4, 12, 16, 48)
SPLIT_MASKS = (4, 12)
OPPOSITE = 10
ROW_TILES = 16

coarse_step = 0.1
f32 = jnp.float32
bf16 = jnp.bfloat16
VM = pl.BlockSpec(memory_space=pltpu.VMEM)
SM = pl.BlockSpec(memory_space=pltpu.SMEM)
MAT = jax.ShapeDtypeStruct((IB, IB), f32)
HALFMAT = jax.ShapeDtypeStruct((HALF, IB), f32)
ROW = jax.ShapeDtypeStruct((1, IB), f32)


def swap(value, mask):
    return lax.ppermute(value, "tile", [(i, i ^ mask) for i in range(lax.axis_size("tile"))])


def cost(flops, nbytes):
    return pl.CostEstimate(flops=flops, bytes_accessed=nbytes, transcendentals=0)


def local_call(kernel, flags, operands, outs, flops=0):
    nbytes = sum(o.size * 4 for o in operands)
    return pl.pallas_call(
        kernel,
        out_shape=outs,
        in_specs=[SM] + [VM] * len(operands),
        out_specs=jax.tree.map(lambda _: VM, outs),
        compiler_params=pltpu.CompilerParams(vmem_limit_bytes=GRANT),
        cost_estimate=cost(flops, nbytes),
    )(flags, *operands)


def halves(value):
    high = value.astype(bf16)
    return high, (value - high.astype(f32)).astype(bf16)


def product(a, b):
    a_high, a_low = halves(a)
    b_high, b_low = halves(b)
    return (
        jnp.dot(a_low, b_high, preferred_element_type=f32)
        + jnp.dot(a_high, b_low, preferred_element_type=f32)
        + jnp.dot(a_high, b_high, preferred_element_type=f32)
    )


def eye_mask(size):
    return lax.broadcasted_iota(jnp.int32, (size, size), 0) == lax.broadcasted_iota(
        jnp.int32, (size, size), 1
    )


def column_to_row(column):
    eye = eye_mask(IFC)
    return jnp.concatenate(
        [
            jnp.sum(jnp.where(eye, column[k : k + IFC], 0.0), axis=0, keepdims=True)
            for k in range(0, IB, IFC)
        ],
        axis=1,
    )


def row_to_column(row):
    eye = eye_mask(IFC)
    return jnp.concatenate(
        [
            jnp.sum(jnp.where(eye, row[:, k : k + IFC], 0.0), axis=1, keepdims=True)
            for k in range(0, IB, IFC)
        ],
        axis=0,
    )


def apply(matrix, row):
    return column_to_row(jnp.sum(matrix * row, axis=1, keepdims=True))


def apply_transposed(matrix, row):
    return jnp.sum(matrix * row_to_column(row), axis=0, keepdims=True)


def triple(value):
    high = value.astype(bf16)
    rest = value - high.astype(f32)
    middle = rest.astype(bf16)
    return high, middle, (rest - middle.astype(f32)).astype(bf16)


def slot_masks(nodes):
    index = lax.broadcasted_iota(jnp.int32, (IFC, IFC), 0)
    return index == nodes // CZ, index == nodes % CZ


def wide(value):
    return jnp.concatenate([value[8 * g : 8 * g + 8] for g in range(GROUPS)], axis=1)


def tall(value):
    return jnp.concatenate([value[:, CZ * g : CZ * g + CZ] for g in range(GROUPS)], axis=0)


def spread(values):
    row = lax.broadcasted_iota(jnp.int32, (192, 24), 0) // 8
    rows = (row == lax.broadcasted_iota(jnp.int32, (192, 24), 1)).astype(f32).astype(bf16)
    block = lax.broadcasted_iota(jnp.int32, (24, 192), 1) // 8
    side = block // 12
    dof = 8 * (block % 12 // 4) + 4 * side + block % 4
    columns = (dof == lax.broadcasted_iota(jnp.int32, (24, 192), 0)).astype(f32).astype(bf16)
    tall_values = jnp.dot(rows, values, preferred_element_type=f32).astype(bf16)
    full = jnp.dot(tall_values, columns, preferred_element_type=f32)
    same = (
        lax.broadcasted_iota(jnp.int32, (192, 192), 0) % 8
        == lax.broadcasted_iota(jnp.int32, (192, 192), 1) % 8
    )
    return jnp.where(same, full, 0.0).astype(bf16)


def substep_kernel(
    flags, step, displacement, velocity, external_load, node_mass, modulus,
    outer, inner, stiffness, nodes,
    displacement_out, velocity_out, picked,
    disp, vel, load, inverse_mass, factor, stiff, even, odd, even_force, odd_force, upper,
):
    first = flags[CORE] == 0

    def put_mass(low, mass):
        present = mass > 0.0
        inverse_mass[pl.ds(low, mass.shape[0])] = jnp.where(
            present, 1.0 / jnp.where(present, mass, 1.0), 0.0
        )

    def put_factor(low, source, base):
        row = lax.broadcasted_iota(jnp.int32, (CY, CZ), 0)
        for x in range(CX):
            factor[low + x] = wide(jnp.where(row < CY - 1, source[base + x], 0.0))

    def place(source, low, shift):
        for i in range(3):
            disp[i, pl.ds(low, CX)] = source[pl.ds(CX * i, CX)]
            vel[i, pl.ds(low + shift, NEAR)] = source[pl.ds(12 + NEAR * i, NEAR)]
            load[i, pl.ds(low + shift, NEAR)] = source[pl.ds(21 + NEAR * i, NEAR)]
        put_mass(low + shift, source[pl.ds(30, NEAR)])
        put_factor(low, source, 33)

    disp[:, CX : 2 * CX] = displacement[...]
    vel[:, CX : 2 * CX] = velocity[...]
    load[:, CX : 2 * CX] = external_load[...]
    put_mass(CX, node_mass[...])
    put_factor(CX, modulus, 0)

    @pl.when(first)
    def _():
        place(outer, 0, 1)
        place(inner, 2 * CX, 0)

    @pl.when(jnp.logical_not(first))
    def _():
        place(inner, 0, 1)
        place(outer, 2 * CX, 0)

    @pl.when(flags[LAST] == 1)
    def _():
        factor[2 * CX - 1] = jnp.zeros((8, GROUPS * CZ), f32)

    high, low = [spread(s) for s in halves(stiffness[...])]
    stiff[...] = jnp.concatenate([high, high, low], axis=1)
    length = step[0]

    def put_features(layer, below, above):
        columns = []
        for i in range(3):
            base = disp[i, layer]
            turned = pltpu.roll(base, CZ - 1, 1)
            columns += [base, turned, pltpu.roll(base, CY - 1, 0), pltpu.roll(turned, CY - 1, 0)]
        for g in range(GROUPS):
            lanes = slice(CZ * g, CZ * g + CZ)
            block = jnp.concatenate([c[8 * g : 8 * g + 8] for c in columns], axis=0)
            high, low = halves(block)
            for target, start in ((below, 96), (above, 0)):
                if target is not None:
                    target[start : start + 96, lanes] = high
                    target[start + 192 : start + 288, lanes] = low
                    target[start + 384 : start + 480, lanes] = high

    def put_force(source, target):
        target[...] = jnp.dot(stiff[...], source[...], preferred_element_type=f32)

    def corner(force, scale, i, a, r):
        start = 8 * (8 * i + 4 * a + r)
        return force[start : start + 8] * scale

    def keep_upper(layer, force):
        scale = factor[layer]
        for i in range(3):
            for r in range(4):
                upper[4 * i + r] = corner(force, scale, i, 1, r)

    def finish_layer(layer, force):
        scale = factor[layer]
        weight = inverse_mass[layer]
        for i in range(3):
            sums = [corner(force, scale, i, 0, r) + upper[4 * i + r] for r in range(4)]
            s00, s01, s10, s11 = [tall(s) for s in sums]
            base = s00 + pltpu.roll(s10, 1, 0)
            turned = s01 + pltpu.roll(s11, 1, 0)
            internal = base + pltpu.roll(turned, 1, 1)
            speed = vel[i, layer] + length * ((load[i, layer] - internal) * weight)
            vel[i, layer] = speed
            disp[i, layer] = disp[i, layer] + length * speed

    def one_substep(k, carry):
        put_features(k, None, even)
        put_features(k + 1, even, odd)
        put_force(even, even_force)
        put_features(k + 2, odd, even)
        keep_upper(k, even_force)
        put_force(odd, odd_force)
        put_features(k + 3, even, odd)

        def two_layers(pair, carry):
            layer = k + 1 + 2 * pair
            put_force(even, even_force)
            put_features(layer + 3, odd, even)
            finish_layer(layer, odd_force)
            keep_upper(layer, odd_force)
            put_force(odd, odd_force)
            put_features(layer + 4, even, odd)
            finish_layer(layer + 1, even_force)
            keep_upper(layer + 1, even_force)
            return carry

        return lax.fori_loop(0, CX + 1 - k, two_layers, carry)

    lax.fori_loop(0, flags[STEPS], one_substep, 0)
    displacement_out[...] = disp[:, CX : 2 * CX]
    final = vel[:, CX : 2 * CX]
    velocity_out[...] = final
    in_row, in_column = slot_masks(nodes[...])
    chosen = in_column.astype(f32).astype(bf16)
    parts = []
    for i in range(3):
        pieces = triple(final[i].reshape(CX * CY, CZ))
        values = sum(jnp.dot(p, chosen, preferred_element_type=f32) for p in reversed(pieces))
        parts.append(jnp.sum(jnp.where(in_row, values, 0.0), axis=0, keepdims=True))
    picked[...] = jnp.concatenate(parts, axis=1)


def pack_kernel(flags, displacement, velocity, external_load, node_mass, modulus, outer, inner):
    for target, start in ((outer, flags[CORE]), (inner, 1 - flags[CORE])):
        for i in range(3):
            target[pl.ds(CX * i, CX)] = displacement[i]
            target[pl.ds(12 + NEAR * i, NEAR)] = velocity[i, pl.ds(start, NEAR)]
            target[pl.ds(21 + NEAR * i, NEAR)] = external_load[i, pl.ds(start, NEAR)]
        target[pl.ds(30, NEAR)] = node_mass[pl.ds(start, NEAR)]
        target[pl.ds(33, CX)] = modulus[...]


def substeps_call(flags, step, state, outer, inner, stiffness, nodes):
    grid_shape = (3, CX, CY, CZ)
    return pl.pallas_call(
        substep_kernel,
        out_shape=(
            jax.ShapeDtypeStruct(grid_shape, f32),
            jax.ShapeDtypeStruct(grid_shape, f32),
            ROW,
        ),
        in_specs=[SM, SM] + [VM] * 9,
        out_specs=(VM, VM, VM),
        scratch_shapes=[
            pltpu.VMEM((3, DEEP + 2, CY, CZ), f32),
            pltpu.VMEM((3, DEEP, CY, CZ), f32),
            pltpu.VMEM((3, DEEP, CY, CZ), f32),
            pltpu.VMEM((DEEP, CY, CZ), f32),
            pltpu.VMEM((DEEP, 8, GROUPS * CZ), f32),
            pltpu.VMEM((192, 576), bf16),
            pltpu.VMEM((576, GROUPS * CZ), bf16),
            pltpu.VMEM((576, GROUPS * CZ), bf16),
            pltpu.VMEM((192, GROUPS * CZ), f32),
            pltpu.VMEM((192, GROUPS * CZ), f32),
            pltpu.VMEM((12, 8, GROUPS * CZ), f32),
        ],
        compiler_params=pltpu.CompilerParams(vmem_limit_bytes=20 << 20),
        cost_estimate=cost(32 * 2 * 192 * 576 * 512, 3 * 720896),
    )(flags, step, *state, outer, inner, stiffness, nodes)

def transition_kernel(flags, inverse, lower, transition):
    transition[...] = -product(inverse[...], lower[...])


def store_half(flags, half, value_ref):
    @pl.when(flags[CORE] == 0)
    def _():
        half[...] = value_ref[:HALF]

    @pl.when(flags[CORE] == 1)
    def _():
        half[...] = value_ref[HALF:]


def first_merge_kernel(flags, own, other, high_ref, low_ref, merged, half):
    is_high = flags[0] == 1
    high = jnp.where(is_high, own[...], other[...])
    low = jnp.where(is_high, other[...], own[...])
    high_ref[...] = high
    low_ref[...] = low
    merged[...] = product(high, low)
    store_half(flags, half, merged)


def first_reach_kernel(flags, other, prefix, suffix):
    is_high = flags[0] == 1
    identity = eye_mask(IB).astype(f32)
    prefix[...] = jnp.where(is_high, other[...], identity)
    suffix[...] = jnp.where(is_high, identity, other[...])


def whole(first, near, far):
    return jnp.concatenate(
        [jnp.where(first, near[...], far[...]), jnp.where(first, far[...], near[...])], axis=0
    )


def merge_kernel(level, last, flags, own, near, far, high_ref, low_ref, *outs):
    is_high = flags[level] == 1
    other = whole(flags[CORE] == 0, near, far)
    high = jnp.where(is_high, own[...], other)
    low = jnp.where(is_high, other, own[...])
    high_ref[...] = high
    low_ref[...] = low
    if not last:
        merged, half = outs
        merged[...] = product(high, low)
        store_half(flags, half, merged)


def block_index(flags):
    return flags[2] + 2 * flags[3]


def sort_kernel(flags, own, near, far, near_far, far_far, near_across, far_across, blocks):
    first = flags[CORE] == 0
    mine = block_index(flags)
    blocks[mine] = own[...]
    for change, pieces in enumerate(((near, far), (near_far, far_far), (near_across, far_across))):
        blocks[mine ^ (change + 1)] = whole(first, *pieces)


def row_kernel(flags, blocks, high, low, merged, half):
    low[...] = product(blocks[1], blocks[0])
    high[...] = product(blocks[3], blocks[2])
    merged[...] = product(high[...], low[...])
    store_half(flags, half, merged)


def row_reach_kernel(flags, blocks, high, low, prefix, suffix, new_prefix, new_suffix):
    base = 2 * flags[3]
    is_high = flags[2] == 1
    longer = product(
        jnp.where(is_high, prefix[...], blocks[base + 1]),
        jnp.where(is_high, blocks[base], suffix[...]),
    )
    new_prefix[...] = jnp.where(is_high, longer, prefix[...])
    new_suffix[...] = jnp.where(is_high, suffix[...], longer)
    in_upper = flags[3] == 1
    longer = product(
        jnp.where(in_upper, new_prefix[...], high[...]),
        jnp.where(in_upper, low[...], new_suffix[...]),
    )
    new_prefix[...] = jnp.where(in_upper, longer, new_prefix[...])
    new_suffix[...] = jnp.where(in_upper, new_suffix[...], longer)


def ordered(flags, rows):
    mine = block_index(flags)
    first = flags[CORE] == 0
    own, split, other_split, opposite = [row[...] for row in rows]
    one = jnp.where(first, split, other_split)
    three = jnp.where(first, other_split, split)
    result = []
    for block in range(4):
        change = mine ^ block
        value = jnp.where(change == 1, one, own)
        value = jnp.where(change == 2, opposite, value)
        result.append(jnp.where(change == 3, three, value))
    return mine, result


def row_forward_kernel(flags, own, split, other_split, opposite, blocks, total, entering):
    mine, rows = ordered(flags, (own, split, other_split, opposite))
    state = rows[0]
    before = jnp.zeros_like(state)
    for block in range(1, 4):
        before = jnp.where(mine == block, state, before)
        state = rows[block] + apply(blocks[block], state)
    total[...] = state
    entering[...] = before


def row_backward_kernel(flags, own, split, other_split, opposite, blocks, total, entering):
    mine, rows = ordered(flags, (own, split, other_split, opposite))
    state = rows[3]
    before = jnp.zeros_like(state)
    for block in range(2, -1, -1):
        before = jnp.where(mine == block, state, before)
        state = rows[block] + apply_transposed(blocks[block], state)
    total[...] = state
    entering[...] = before


def below_row(flags, hop):
    first_row = flags[4] + flags[5] == 0
    return jnp.where(first_row, 0.0, hop[...])


def hop_kernel(flags, total, hop, merged, leaving):
    leaving[...] = total[...] + apply(merged[...], below_row(flags, hop))


def reach_kernel(level, flags, high, low, prefix, suffix, new_prefix, new_suffix):
    is_high = flags[level] == 1
    longer = product(
        jnp.where(is_high, prefix[...], high[...]), jnp.where(is_high, low[...], suffix[...])
    )
    new_prefix[...] = jnp.where(is_high, longer, prefix[...])
    new_suffix[...] = jnp.where(is_high, suffix[...], longer)


def start_kernel(flags, inverse, picked, partner, offset):
    sign = (1 - 2 * flags[SIDE]).astype(f32)
    offset[...] = apply(inverse[...], sign * (picked[...] - partner[...]))


def forward_kernel(level, flags, own, other, high_matrix, total):
    is_high = flags[level] == 1
    high = jnp.where(is_high, own[...], other[...])
    low = jnp.where(is_high, other[...], own[...])
    total[...] = high + apply(high_matrix[...], low)


def backward_kernel(level, flags, own, other, low_matrix, total):
    is_high = flags[level] == 1
    high = jnp.where(is_high, own[...], other[...])
    low = jnp.where(is_high, other[...], own[...])
    total[...] = low + apply_transposed(low_matrix[...], high)


def forward_part_kernel(flags, other_0, other_1, in_row, prefix_0, prefix_1, result):
    result[...] = jnp.where(flags[0] == 1, other_0[...], 0.0) + apply(prefix_1[...], in_row[...])

    @pl.when(flags[1] == 1)
    def _():
        result[...] = result[...] + apply(prefix_0[...], other_1[...])


def backward_part_kernel(
    flags, other_0, other_1, in_row, other_4, suffix_0, suffix_1, suffix_3, result
):
    result[...] = jnp.where(flags[0] == 0, other_0[...], 0.0) + apply_transposed(
        suffix_1[...], in_row[...]
    )

    @pl.when(flags[1] == 0)
    def _():
        result[...] = result[...] + apply_transposed(suffix_0[...], other_1[...])

    @pl.when(flags[4] == 0)
    def _():
        result[...] = result[...] + apply_transposed(suffix_3[...], other_4[...])


def turn_kernel(flags, entering, hop, prefix, transition, offset, solved, returning):
    before = entering[...] + apply(prefix[...], below_row(flags, hop))
    current = offset[...] + apply(transition[...], before)
    solved[...] = current
    returning[...] = -apply_transposed(transition[...], current)


def finish_kernel(
    flags, inverse, entering, other, suffix, solved, velocity, node_mass, nodes, velocity_out
):
    after = entering[...] + jnp.where(flags[5] == 0, 1.0, 0.0) * apply_transposed(
        suffix[...], other[...]
    )
    sign = (1 - 2 * flags[SIDE]).astype(f32)
    multiplier = sign * apply_transposed(inverse[...], solved[...] - after)
    in_row, in_column = slot_masks(nodes[...])
    chosen = in_column.astype(f32).astype(bf16)
    weight = 1.0 / node_mass[...]
    for i in range(3):
        held = jnp.where(in_row, multiplier[:, IFC * i : IFC * i + IFC], 0.0)
        change = sum(
            lax.dot_general(p, chosen, (((1,), (1,)), ((), ())), preferred_element_type=f32)
            for p in reversed(triple(held))
        )
        velocity_out[i] = velocity[i] - change.reshape(CX, CY, CZ) * weight


def bound(level, kernel, *fixed):
    def run(*refs):
        kernel(level, *fixed, *refs)

    return run


def after(value, *earlier):
    return lax.optimization_barrier((value, *earlier))[0]


def first_products(flags, transition, gate):
    cube = 6 * IB**3
    other = after(swap(transition, MASKS[0]), gate)
    high, low, merged, half = local_call(
        first_merge_kernel, flags, [transition, other], (MAT, MAT, MAT, HALFMAT), cube
    )
    prefix, suffix = local_call(first_reach_kernel, flags, [other], (MAT, MAT))
    return (merged, half), [(high, low, prefix, suffix)]


def merge_level(flags, level, block, levels, near):
    cube = 6 * IB**3
    merged, half = block
    far = swap(near, 1)
    last = level == 4
    high, low, *block = local_call(
        bound(level, merge_kernel, last),
        flags,
        [merged, near, far],
        (MAT, MAT) if last else (MAT, MAT, MAT, HALFMAT),
        cube,
    )
    prefix, suffix = local_call(
        bound(level, reach_kernel), flags, [high, low, *levels[-1][2:]], (MAT, MAT), cube
    )
    return block, levels + [(high, low, prefix, suffix)]


def split_swap(value):
    masks = [SPLIT_MASKS[i & 1] for i in range(lax.axis_size("tile"))]
    return lax.ppermute(value, "tile", [(i, i ^ mask) for i, mask in enumerate(masks)])


def row_exchange(total):
    opposite = swap(total, OPPOSITE)
    split = split_swap(total)
    return [split, swap(split, 1), opposite]


def sorted_blocks(flags, fetched, gate):
    merged, nears = fetched
    pieces = []
    for near in nears:
        near = after(near, *gate)
        pieces += [near, swap(near, 1)]
    return local_call(
        sort_kernel, flags, [merged, *pieces], jax.ShapeDtypeStruct((4, IB, IB), f32)
    )


def coupled_velocity(
    flags, picked, inverse, transition, fetched, levels, velocity, node_mass, nodes
):
    square = 2 * IB * IB
    cube = 6 * IB**3
    prefix_0, suffix_0 = levels[0][2:]
    prefix_1, suffix_1 = levels[1][2:]
    count = lax.axis_size("sub")
    partner = lax.ppermute(picked, "sub", [(i, i ^ 1) for i in range(count)])
    offset = local_call(start_kernel, flags, [inverse, picked, partner], ROW, square)
    total, others = offset, []
    for level in range(2):
        others.append(after(swap(total, MASKS[level]), prefix_1))
        total = local_call(
            bound(level, forward_kernel), flags, [total, others[-1], levels[level][0]], ROW, square
        )
    arrived = row_exchange(total)
    blocks = sorted_blocks(flags, fetched, (arrived[0], arrived[2]))
    total, in_row = local_call(
        row_forward_kernel, flags, [total, *arrived, blocks], (ROW, ROW), 3 * square
    )
    high, low, *row = local_call(
        row_kernel, flags, [after(blocks, total)], (MAT, MAT, MAT, HALFMAT), 3 * cube
    )
    merged = row[0]
    hop = up_row(total)
    hop = after(hop, merged)
    leaving = local_call(hop_kernel, flags, [total, hop, merged], ROW, square)
    hop = up_row(leaving)
    prefix_3, suffix_3 = local_call(
        row_reach_kernel, flags, [blocks, high, low, prefix_1, suffix_1], (MAT, MAT), 2 * cube
    )
    hop = after(hop, prefix_3)
    leaving = local_call(hop_kernel, flags, [total, hop, merged], ROW, square)
    hop = up_row(leaving)
    entering = local_call(
        forward_part_kernel, flags, [*others, after(in_row, leaving), prefix_0, prefix_1], ROW, 2 * square
    )
    hop = after(hop, entering)
    row[1] = after(row[1], hop)
    solved, returning = local_call(
        turn_kernel,
        flags,
        [entering, hop, prefix_3, transition, offset],
        (ROW, ROW),
        3 * square,
    )
    total, others = returning, []
    for level in range(2):
        others.append(swap(total, MASKS[level]))
        total = local_call(
            bound(level, backward_kernel), flags, [total, others[-1], levels[level][1]], ROW, square
        )
    arrived = row_exchange(total)
    near = after(swap(row[1], MASKS[4]), arrived[0], arrived[2])
    row, levels = merge_level(
        flags, 4, row, levels + [None, (None, None, prefix_3, suffix_3)], near
    )
    _, low, _, suffix_4 = levels[4]
    total, in_row = local_call(
        row_backward_kernel, flags, [total, *arrived, blocks], (ROW, ROW), 3 * square
    )
    others.append(swap(total, MASKS[4]))
    total = local_call(
        bound(4, backward_kernel), flags, [total, after(others[-1], suffix_4), low], ROW, square
    )
    last_other = swap(total, MASKS[5])
    entering = local_call(
        backward_part_kernel,
        flags,
        [others[0], others[1], in_row, others[2], suffix_0, suffix_1, suffix_3],
        ROW,
        3 * square,
    )
    return local_call(
        finish_kernel,
        flags,
        [inverse, entering, after(last_other, entering), suffix_4, solved, velocity, node_mass, nodes],
        jax.ShapeDtypeStruct(velocity.shape, f32),
        2 * square,
    )


def up_row(value):
    count = lax.axis_size("tile")
    return lax.ppermute(value, "tile", [(i, (i + ROW_TILES) % count) for i in range(count)])


def outer_swap(value):
    count = lax.axis_size("tile")
    route = []
    for low in range(1, count - 1, 2):
        route += [(low, low + 1), (low + 1, low)]
    return lax.ppermute(value, "tile", route)


def body(
    displacement,
    velocity,
    external_load,
    node_mass,
    modulus,
    stiffness,
    substeps,
    interface_nodes,
    factor_inverse,
    factor_lower,
):
    sub, tile = lax.axis_index("sub"), lax.axis_index("tile")
    last = tile == lax.axis_size("tile") - 1
    flags = jnp.stack(
        [(tile >> k) & 1 for k in range(6)] + [sub // 2, sub % 2, last, substeps[0]]
    ).astype(jnp.int32)
    step = coarse_step / substeps.astype(f32)
    state = [displacement[0], velocity[0], external_load[0], node_mass[0], modulus[0]]
    packed = jax.ShapeDtypeStruct((PACKED, CY, CZ), f32)
    inverse = lax.dynamic_index_in_dim(factor_inverse, sub // 2, 0, keepdims=False)
    lower = lax.dynamic_index_in_dim(factor_lower, sub // 2, 0, keepdims=False)
    transition = local_call(transition_kernel, flags, [inverse, lower], MAT, 6 * IB**3)
    outer, inner = local_call(pack_kernel, flags, state, (packed, packed))
    block, levels = first_products(flags, transition, outer)
    inner = swap(inner, 1)
    near = swap(after(block[1], inner), MASKS[1])
    outer = outer_swap(outer)
    block, levels = merge_level(flags, 1, block, levels, near)
    merged, half = block
    fetched = merged, [swap(half, mask) for mask in (SPLIT_MASKS[0], OPPOSITE, SPLIT_MASKS[1])]
    outer = after(outer, half)
    final_displacement, final_velocity, picked = substeps_call(
        flags, step, state, outer, inner, stiffness, interface_nodes
    )
    coupled = coupled_velocity(
        flags,
        picked,
        inverse,
        transition,
        fetched,
        levels,
        final_velocity,
        node_mass[0],
        interface_nodes,
    )
    return final_displacement[None], coupled[None]


def solution(mesh):
    in_specs = (
        P("sub", None, "tile", None, None),
        P("sub", None, "tile", None, None),
        P("sub", None, "tile", None, None),
        P("sub", "tile", None, None),
        P("sub", "tile", None, None),
        P(),
        P("sub"),
        P("sub", "tile"),
        P(None, "tile", None),
        P(None, "tile", None),
    )
    out_specs = (P("sub", None, "tile", None, None), P("sub", None, "tile", None, None))
    return jax.shard_map(body, mesh=mesh, in_specs=in_specs, out_specs=out_specs, check_vma=False)
```

```python
import jax
import jax.numpy as jnp
from jax import lax
from jax.experimental import pallas as pl
from jax.experimental.pallas import tpu as pltpu
from jax.sharding import PartitionSpec as P

IFC = 128
IB = 384
HALF = IB // 2
GRANT = 12 << 20
CX, CY, CZ = 4, 32, 128
DEEP = 3 * CX
NEAR = CX - 1
PACKED = 37
CORE, PAIR, SIDE, LAST = 0, 6, 7, 8
GROUPS = CY // 8
MASKS = (1, 2, 4, 12, 16, 48)
SPLIT_MASKS = (4, 12)
OPPOSITE = 10
ROW_TILES = 16

coarse_step = 0.1
f32 = jnp.float32
bf16 = jnp.bfloat16
VM = pl.BlockSpec(memory_space=pltpu.VMEM)
SM = pl.BlockSpec(memory_space=pltpu.SMEM)
MAT = jax.ShapeDtypeStruct((IB, IB), f32)
HALFMAT = jax.ShapeDtypeStruct((HALF, IB), f32)
ROW = jax.ShapeDtypeStruct((1, IB), f32)


def swap(value, mask):
    return lax.ppermute(value, "tile", [(i, i ^ mask) for i in range(lax.axis_size("tile"))])


def cost(flops, nbytes):
    return pl.CostEstimate(flops=flops, bytes_accessed=nbytes, transcendentals=0)


class Place:
    def __getitem__(self, item):
        tile, sub = lax.axis_index("tile"), lax.axis_index("sub")
        if item == PAIR:
            return sub // 2
        if item == SIDE:
            return sub % 2
        if item == LAST:
            return (tile == lax.axis_size("tile") - 1).astype(jnp.int32)
        return (tile >> item) & 1


def local_call(kernel, place, operands, outs, flops=0):
    nbytes = sum(o.size * 4 for o in operands)

    def placed(*refs):
        kernel(place, *refs)

    return pl.pallas_call(
        placed,
        out_shape=outs,
        in_specs=[VM] * len(operands),
        out_specs=jax.tree.map(lambda _: VM, outs),
        compiler_params=pltpu.CompilerParams(vmem_limit_bytes=GRANT),
        cost_estimate=cost(flops, nbytes),
    )(*operands)


def halves(value):
    high = value.astype(bf16)
    return high, (value - high.astype(f32)).astype(bf16)


def product(a, b):
    a_high, a_low = halves(a)
    b_high, b_low = halves(b)
    return (
        jnp.dot(a_low, b_high, preferred_element_type=f32)
        + jnp.dot(a_high, b_low, preferred_element_type=f32)
        + jnp.dot(a_high, b_high, preferred_element_type=f32)
    )


def eye_mask(size):
    return lax.broadcasted_iota(jnp.int32, (size, size), 0) == lax.broadcasted_iota(
        jnp.int32, (size, size), 1
    )


def column_to_row(column):
    eye = eye_mask(IFC)
    return jnp.concatenate(
        [
            jnp.sum(jnp.where(eye, column[k : k + IFC], 0.0), axis=0, keepdims=True)
            for k in range(0, IB, IFC)
        ],
        axis=1,
    )


def row_to_column(row):
    eye = eye_mask(IFC)
    return jnp.concatenate(
        [
            jnp.sum(jnp.where(eye, row[:, k : k + IFC], 0.0), axis=1, keepdims=True)
            for k in range(0, IB, IFC)
        ],
        axis=0,
    )


def apply(matrix, row):
    return column_to_row(jnp.sum(matrix * row, axis=1, keepdims=True))


def apply_transposed(matrix, row):
    return jnp.sum(matrix * row_to_column(row), axis=0, keepdims=True)


def triple(value):
    high = value.astype(bf16)
    rest = value - high.astype(f32)
    middle = rest.astype(bf16)
    return high, middle, (rest - middle.astype(f32)).astype(bf16)


def slot_masks(nodes):
    index = lax.broadcasted_iota(jnp.int32, (IFC, IFC), 0)
    return index == nodes // CZ, index == nodes % CZ


def wide(value):
    return jnp.concatenate([value[8 * g : 8 * g + 8] for g in range(GROUPS)], axis=1)


def tall(value):
    return jnp.concatenate([value[:, CZ * g : CZ * g + CZ] for g in range(GROUPS)], axis=0)


def spread(values):
    row = lax.broadcasted_iota(jnp.int32, (192, 24), 0) // 8
    rows = (row == lax.broadcasted_iota(jnp.int32, (192, 24), 1)).astype(f32).astype(bf16)
    block = lax.broadcasted_iota(jnp.int32, (24, 192), 1) // 8
    side = block // 12
    dof = 8 * (block % 12 // 4) + 4 * side + block % 4
    columns = (dof == lax.broadcasted_iota(jnp.int32, (24, 192), 0)).astype(f32).astype(bf16)
    tall_values = jnp.dot(rows, values, preferred_element_type=f32).astype(bf16)
    full = jnp.dot(tall_values, columns, preferred_element_type=f32)
    same = (
        lax.broadcasted_iota(jnp.int32, (192, 192), 0) % 8
        == lax.broadcasted_iota(jnp.int32, (192, 192), 1) % 8
    )
    return jnp.where(same, full, 0.0).astype(bf16)


def substep_kernel(
    count, step, displacement, velocity, external_load, node_mass, modulus,
    outer, inner, stiffness, nodes,
    displacement_out, velocity_out, picked,
    disp, vel, load, inverse_mass, factor, stiff, even, odd, even_force, odd_force, upper,
):
    flags = Place()
    first = flags[CORE] == 0

    def put_mass(low, mass):
        present = mass > 0.0
        inverse_mass[pl.ds(low, mass.shape[0])] = jnp.where(
            present, 1.0 / jnp.where(present, mass, 1.0), 0.0
        )

    def put_factor(low, source, base):
        row = lax.broadcasted_iota(jnp.int32, (CY, CZ), 0)
        for x in range(CX):
            factor[low + x] = wide(jnp.where(row < CY - 1, source[base + x], 0.0))

    def place(source, low, shift):
        for i in range(3):
            disp[i, pl.ds(low, CX)] = source[pl.ds(CX * i, CX)]
            vel[i, pl.ds(low + shift, NEAR)] = source[pl.ds(12 + NEAR * i, NEAR)]
            load[i, pl.ds(low + shift, NEAR)] = source[pl.ds(21 + NEAR * i, NEAR)]
        put_mass(low + shift, source[pl.ds(30, NEAR)])
        put_factor(low, source, 33)

    disp[:, CX : 2 * CX] = displacement[...]
    vel[:, CX : 2 * CX] = velocity[...]
    load[:, CX : 2 * CX] = external_load[...]
    put_mass(CX, node_mass[...])
    put_factor(CX, modulus, 0)

    @pl.when(first)
    def _():
        place(outer, 0, 1)
        place(inner, 2 * CX, 0)

    @pl.when(jnp.logical_not(first))
    def _():
        place(inner, 0, 1)
        place(outer, 2 * CX, 0)

    @pl.when(flags[LAST] == 1)
    def _():
        factor[2 * CX - 1] = jnp.zeros((8, GROUPS * CZ), f32)

    high, low = [spread(s) for s in halves(stiffness[...])]
    stiff[...] = jnp.concatenate([high, high, low], axis=1)
    length = step[0]

    def put_features(layer, below, above):
        columns = []
        for i in range(3):
            base = disp[i, layer]
            turned = pltpu.roll(base, CZ - 1, 1)
            columns += [base, turned, pltpu.roll(base, CY - 1, 0), pltpu.roll(turned, CY - 1, 0)]
        for g in range(GROUPS):
            lanes = slice(CZ * g, CZ * g + CZ)
            block = jnp.concatenate([c[8 * g : 8 * g + 8] for c in columns], axis=0)
            high, low = halves(block)
            for target, start in ((below, 96), (above, 0)):
                if target is not None:
                    target[start : start + 96, lanes] = high
                    target[start + 192 : start + 288, lanes] = low
                    target[start + 384 : start + 480, lanes] = high

    def put_force(source, target):
        target[...] = jnp.dot(stiff[...], source[...], preferred_element_type=f32)

    def corner(force, scale, i, a, r):
        start = 8 * (8 * i + 4 * a + r)
        return force[start : start + 8] * scale

    def keep_upper(layer, force):
        scale = factor[layer]
        for i in range(3):
            for r in range(4):
                upper[4 * i + r] = corner(force, scale, i, 1, r)

    def finish_layer(layer, force):
        scale = factor[layer]
        weight = inverse_mass[layer]
        for i in range(3):
            sums = [corner(force, scale, i, 0, r) + upper[4 * i + r] for r in range(4)]
            s00, s01, s10, s11 = [tall(s) for s in sums]
            base = s00 + pltpu.roll(s10, 1, 0)
            turned = s01 + pltpu.roll(s11, 1, 0)
            internal = base + pltpu.roll(turned, 1, 1)
            speed = vel[i, layer] + length * ((load[i, layer] - internal) * weight)
            vel[i, layer] = speed
            disp[i, layer] = disp[i, layer] + length * speed

    def one_substep(k, carry):
        put_features(k, None, even)
        put_features(k + 1, even, odd)
        put_force(even, even_force)
        put_features(k + 2, odd, even)
        keep_upper(k, even_force)
        put_force(odd, odd_force)
        put_features(k + 3, even, odd)

        def two_layers(pair, carry):
            layer = k + 1 + 2 * pair
            put_force(even, even_force)
            put_features(layer + 3, odd, even)
            finish_layer(layer, odd_force)
            keep_upper(layer, odd_force)
            put_force(odd, odd_force)
            put_features(layer + 4, even, odd)
            finish_layer(layer + 1, even_force)
            keep_upper(layer + 1, even_force)
            return carry

        return lax.fori_loop(0, CX + 1 - k, two_layers, carry)

    lax.fori_loop(0, count[0], one_substep, 0)
    displacement_out[...] = disp[:, CX : 2 * CX]
    final = vel[:, CX : 2 * CX]
    velocity_out[...] = final
    in_row, in_column = slot_masks(nodes[...])
    chosen = in_column.astype(f32).astype(bf16)
    parts = []
    for i in range(3):
        pieces = triple(final[i].reshape(CX * CY, CZ))
        values = sum(jnp.dot(p, chosen, preferred_element_type=f32) for p in reversed(pieces))
        parts.append(jnp.sum(jnp.where(in_row, values, 0.0), axis=0, keepdims=True))
    picked[...] = jnp.concatenate(parts, axis=1)


def pack_kernel(flags, displacement, velocity, external_load, node_mass, modulus, outer, inner):
    for target, start in ((outer, flags[CORE]), (inner, 1 - flags[CORE])):
        for i in range(3):
            target[pl.ds(CX * i, CX)] = displacement[i]
            target[pl.ds(12 + NEAR * i, NEAR)] = velocity[i, pl.ds(start, NEAR)]
            target[pl.ds(21 + NEAR * i, NEAR)] = external_load[i, pl.ds(start, NEAR)]
        target[pl.ds(30, NEAR)] = node_mass[pl.ds(start, NEAR)]
        target[pl.ds(33, CX)] = modulus[...]


def substeps_call(count, step, state, outer, inner, stiffness, nodes):
    grid_shape = (3, CX, CY, CZ)
    return pl.pallas_call(
        substep_kernel,
        out_shape=(
            jax.ShapeDtypeStruct(grid_shape, f32),
            jax.ShapeDtypeStruct(grid_shape, f32),
            ROW,
        ),
        in_specs=[SM, SM] + [VM] * 9,
        out_specs=(VM, VM, VM),
        scratch_shapes=[
            pltpu.VMEM((3, DEEP + 2, CY, CZ), f32),
            pltpu.VMEM((3, DEEP, CY, CZ), f32),
            pltpu.VMEM((3, DEEP, CY, CZ), f32),
            pltpu.VMEM((DEEP, CY, CZ), f32),
            pltpu.VMEM((DEEP, 8, GROUPS * CZ), f32),
            pltpu.VMEM((192, 576), bf16),
            pltpu.VMEM((576, GROUPS * CZ), bf16),
            pltpu.VMEM((576, GROUPS * CZ), bf16),
            pltpu.VMEM((192, GROUPS * CZ), f32),
            pltpu.VMEM((192, GROUPS * CZ), f32),
            pltpu.VMEM((12, 8, GROUPS * CZ), f32),
        ],
        compiler_params=pltpu.CompilerParams(vmem_limit_bytes=20 << 20),
        cost_estimate=cost(32 * 2 * 192 * 576 * 512, 3 * 720896),
    )(count, step, *state, outer, inner, stiffness, nodes)

def transition_kernel(flags, inverse, lower, transition):
    transition[...] = -product(inverse[...], lower[...])


def store_half(flags, half, value_ref):
    @pl.when(flags[CORE] == 0)
    def _():
        half[...] = value_ref[:HALF]

    @pl.when(flags[CORE] == 1)
    def _():
        half[...] = value_ref[HALF:]


def first_merge_kernel(flags, own, other, high_ref, low_ref, merged, half):
    is_high = flags[0] == 1
    high = jnp.where(is_high, own[...], other[...])
    low = jnp.where(is_high, other[...], own[...])
    high_ref[...] = high
    low_ref[...] = low
    merged[...] = product(high, low)
    store_half(flags, half, merged)


def first_reach_kernel(flags, other, prefix, suffix):
    is_high = flags[0] == 1
    identity = eye_mask(IB).astype(f32)
    prefix[...] = jnp.where(is_high, other[...], identity)
    suffix[...] = jnp.where(is_high, identity, other[...])


def whole(first, near, far):
    return jnp.concatenate(
        [jnp.where(first, near[...], far[...]), jnp.where(first, far[...], near[...])], axis=0
    )


def merge_kernel(level, last, flags, own, near, far, high_ref, low_ref, *outs):
    is_high = flags[level] == 1
    other = whole(flags[CORE] == 0, near, far)
    high = jnp.where(is_high, own[...], other)
    low = jnp.where(is_high, other, own[...])
    high_ref[...] = high
    low_ref[...] = low
    if not last:
        merged, half = outs
        merged[...] = product(high, low)
        store_half(flags, half, merged)


def block_index(flags):
    return flags[2] + 2 * flags[3]


def sort_kernel(flags, own, near, far, near_far, far_far, near_across, far_across, blocks):
    first = flags[CORE] == 0
    mine = block_index(flags)
    blocks[mine] = own[...]
    for change, pieces in enumerate(((near, far), (near_far, far_far), (near_across, far_across))):
        blocks[mine ^ (change + 1)] = whole(first, *pieces)


def row_kernel(flags, blocks, high, low, merged, half):
    low[...] = product(blocks[1], blocks[0])
    high[...] = product(blocks[3], blocks[2])
    merged[...] = product(high[...], low[...])
    store_half(flags, half, merged)


def row_reach_kernel(flags, blocks, high, low, prefix, suffix, new_prefix, new_suffix):
    base = 2 * flags[3]
    is_high = flags[2] == 1
    longer = product(
        jnp.where(is_high, prefix[...], blocks[base + 1]),
        jnp.where(is_high, blocks[base], suffix[...]),
    )
    new_prefix[...] = jnp.where(is_high, longer, prefix[...])
    new_suffix[...] = jnp.where(is_high, suffix[...], longer)
    in_upper = flags[3] == 1
    longer = product(
        jnp.where(in_upper, new_prefix[...], high[...]),
        jnp.where(in_upper, low[...], new_suffix[...]),
    )
    new_prefix[...] = jnp.where(in_upper, longer, new_prefix[...])
    new_suffix[...] = jnp.where(in_upper, new_suffix[...], longer)


def ordered(flags, rows):
    mine = block_index(flags)
    first = flags[CORE] == 0
    own, split, other_split, opposite = [row[...] for row in rows]
    one = jnp.where(first, split, other_split)
    three = jnp.where(first, other_split, split)
    result = []
    for block in range(4):
        change = mine ^ block
        value = jnp.where(change == 1, one, own)
        value = jnp.where(change == 2, opposite, value)
        result.append(jnp.where(change == 3, three, value))
    return mine, result


def row_forward_kernel(flags, own, split, other_split, opposite, blocks, total, entering):
    mine, rows = ordered(flags, (own, split, other_split, opposite))
    state = rows[0]
    before = jnp.zeros_like(state)
    for block in range(1, 4):
        before = jnp.where(mine == block, state, before)
        state = rows[block] + apply(blocks[block], state)
    total[...] = state
    entering[...] = before


def row_backward_kernel(flags, own, split, other_split, opposite, blocks, total, entering):
    mine, rows = ordered(flags, (own, split, other_split, opposite))
    state = rows[3]
    before = jnp.zeros_like(state)
    for block in range(2, -1, -1):
        before = jnp.where(mine == block, state, before)
        state = rows[block] + apply_transposed(blocks[block], state)
    total[...] = state
    entering[...] = before


def below_row(flags, hop):
    first_row = flags[4] + flags[5] == 0
    return jnp.where(first_row, 0.0, hop[...])


def hop_kernel(flags, total, hop, merged, leaving):
    leaving[...] = total[...] + apply(merged[...], below_row(flags, hop))


def reach_kernel(level, flags, high, low, prefix, suffix, new_prefix, new_suffix):
    is_high = flags[level] == 1
    longer = product(
        jnp.where(is_high, prefix[...], high[...]), jnp.where(is_high, low[...], suffix[...])
    )
    new_prefix[...] = jnp.where(is_high, longer, prefix[...])
    new_suffix[...] = jnp.where(is_high, suffix[...], longer)


def start_kernel(flags, inverse, picked, partner, offset):
    sign = (1 - 2 * flags[SIDE]).astype(f32)
    offset[...] = apply(inverse[...], sign * (picked[...] - partner[...]))


def forward_kernel(level, flags, own, other, high_matrix, total):
    is_high = flags[level] == 1
    high = jnp.where(is_high, own[...], other[...])
    low = jnp.where(is_high, other[...], own[...])
    total[...] = high + apply(high_matrix[...], low)


def backward_kernel(level, flags, own, other, low_matrix, total):
    is_high = flags[level] == 1
    high = jnp.where(is_high, own[...], other[...])
    low = jnp.where(is_high, other[...], own[...])
    total[...] = low + apply_transposed(low_matrix[...], high)


def forward_part_kernel(flags, other_0, other_1, in_row, prefix_0, prefix_1, result):
    result[...] = jnp.where(flags[0] == 1, other_0[...], 0.0) + apply(prefix_1[...], in_row[...])

    @pl.when(flags[1] == 1)
    def _():
        result[...] = result[...] + apply(prefix_0[...], other_1[...])


def backward_part_kernel(
    flags, other_0, other_1, in_row, other_4, suffix_0, suffix_1, suffix_3, result
):
    result[...] = jnp.where(flags[0] == 0, other_0[...], 0.0) + apply_transposed(
        suffix_1[...], in_row[...]
    )

    @pl.when(flags[1] == 0)
    def _():
        result[...] = result[...] + apply_transposed(suffix_0[...], other_1[...])

    @pl.when(flags[4] == 0)
    def _():
        result[...] = result[...] + apply_transposed(suffix_3[...], other_4[...])


def turn_kernel(flags, entering, hop, prefix, transition, offset, solved, returning):
    before = entering[...] + apply(prefix[...], below_row(flags, hop))
    current = offset[...] + apply(transition[...], before)
    solved[...] = current
    returning[...] = -apply_transposed(transition[...], current)


def finish_kernel(
    flags, inverse, entering, other, suffix, solved, velocity, node_mass, nodes, velocity_out
):
    after = entering[...] + jnp.where(flags[5] == 0, 1.0, 0.0) * apply_transposed(
        suffix[...], other[...]
    )
    sign = (1 - 2 * flags[SIDE]).astype(f32)
    multiplier = sign * apply_transposed(inverse[...], solved[...] - after)
    in_row, in_column = slot_masks(nodes[...])
    chosen = in_column.astype(f32).astype(bf16)
    weight = 1.0 / node_mass[...]
    for i in range(3):
        held = jnp.where(in_row, multiplier[:, IFC * i : IFC * i + IFC], 0.0)
        change = sum(
            lax.dot_general(p, chosen, (((1,), (1,)), ((), ())), preferred_element_type=f32)
            for p in reversed(triple(held))
        )
        velocity_out[i] = velocity[i] - change.reshape(CX, CY, CZ) * weight


def bound(level, kernel, *fixed):
    def run(*refs):
        kernel(level, *fixed, *refs)

    return run


def after(value, *earlier):
    return lax.optimization_barrier((value, *earlier))[0]


def first_products(flags, transition, gate):
    cube = 6 * IB**3
    other = after(swap(transition, MASKS[0]), gate)
    high, low, merged, half = local_call(
        first_merge_kernel, flags, [transition, other], (MAT, MAT, MAT, HALFMAT), cube
    )
    prefix, suffix = local_call(first_reach_kernel, flags, [other], (MAT, MAT))
    return (merged, half), [(high, low, prefix, suffix)]


def merge_level(flags, level, block, levels, near):
    cube = 6 * IB**3
    merged, half = block
    far = swap(near, 1)
    last = level == 4
    high, low, *block = local_call(
        bound(level, merge_kernel, last),
        flags,
        [merged, near, far],
        (MAT, MAT) if last else (MAT, MAT, MAT, HALFMAT),
        cube,
    )
    prefix, suffix = local_call(
        bound(level, reach_kernel), flags, [high, low, *levels[-1][2:]], (MAT, MAT), cube
    )
    return block, levels + [(high, low, prefix, suffix)]


def split_swap(value):
    masks = [SPLIT_MASKS[i & 1] for i in range(lax.axis_size("tile"))]
    return lax.ppermute(value, "tile", [(i, i ^ mask) for i, mask in enumerate(masks)])


def row_exchange(total):
    opposite = swap(total, OPPOSITE)
    split = split_swap(total)
    return [split, swap(split, 1), opposite]


def sorted_blocks(flags, fetched, gate):
    merged, nears = fetched
    pieces = []
    for near in nears:
        near = after(near, *gate)
        pieces += [near, swap(near, 1)]
    return local_call(
        sort_kernel, flags, [merged, *pieces], jax.ShapeDtypeStruct((4, IB, IB), f32)
    )


def coupled_velocity(
    flags, picked, inverse, transition, fetched, levels, velocity, node_mass, nodes
):
    square = 2 * IB * IB
    cube = 6 * IB**3
    prefix_0, suffix_0 = levels[0][2:]
    prefix_1, suffix_1 = levels[1][2:]
    count = lax.axis_size("sub")
    partner = lax.ppermute(picked, "sub", [(i, i ^ 1) for i in range(count)])
    offset = local_call(start_kernel, flags, [inverse, picked, partner], ROW, square)
    total, others = offset, []
    for level in range(2):
        others.append(after(swap(total, MASKS[level]), prefix_1))
        total = local_call(
            bound(level, forward_kernel), flags, [total, others[-1], levels[level][0]], ROW, square
        )
    arrived = row_exchange(total)
    blocks = sorted_blocks(flags, fetched, (arrived[0], arrived[2]))
    total, in_row = local_call(
        row_forward_kernel, flags, [total, *arrived, blocks], (ROW, ROW), 3 * square
    )
    high, low, *row = local_call(
        row_kernel, flags, [after(blocks, total)], (MAT, MAT, MAT, HALFMAT), 3 * cube
    )
    merged = row[0]
    hop = up_row(total)
    hop = after(hop, merged)
    leaving = local_call(hop_kernel, flags, [total, hop, merged], ROW, square)
    hop = up_row(leaving)
    prefix_3, suffix_3 = local_call(
        row_reach_kernel, flags, [blocks, high, low, prefix_1, suffix_1], (MAT, MAT), 2 * cube
    )
    hop = after(hop, prefix_3)
    leaving = local_call(hop_kernel, flags, [total, hop, merged], ROW, square)
    hop = up_row(leaving)
    entering = local_call(
        forward_part_kernel, flags, [*others, after(in_row, leaving), prefix_0, prefix_1], ROW, 2 * square
    )
    hop = after(hop, entering)
    row[1] = after(row[1], hop)
    solved, returning = local_call(
        turn_kernel,
        flags,
        [entering, hop, prefix_3, transition, offset],
        (ROW, ROW),
        3 * square,
    )
    total, others = returning, []
    for level in range(2):
        others.append(swap(total, MASKS[level]))
        total = local_call(
            bound(level, backward_kernel), flags, [total, others[-1], levels[level][1]], ROW, square
        )
    arrived = row_exchange(total)
    near = after(swap(row[1], MASKS[4]), arrived[0], arrived[2])
    row, levels = merge_level(
        flags, 4, row, levels + [None, (None, None, prefix_3, suffix_3)], near
    )
    _, low, _, suffix_4 = levels[4]
    total, in_row = local_call(
        row_backward_kernel, flags, [total, *arrived, blocks], (ROW, ROW), 3 * square
    )
    others.append(swap(total, MASKS[4]))
    total = local_call(
        bound(4, backward_kernel), flags, [total, after(others[-1], suffix_4), low], ROW, square
    )
    last_other = swap(total, MASKS[5])
    entering = local_call(
        backward_part_kernel,
        flags,
        [others[0], others[1], in_row, others[2], suffix_0, suffix_1, suffix_3],
        ROW,
        3 * square,
    )
    return local_call(
        finish_kernel,
        flags,
        [inverse, entering, after(last_other, entering), suffix_4, solved, velocity, node_mass, nodes],
        jax.ShapeDtypeStruct(velocity.shape, f32),
        2 * square,
    )


def up_row(value):
    count = lax.axis_size("tile")
    return lax.ppermute(value, "tile", [(i, (i + ROW_TILES) % count) for i in range(count)])


def outer_swap(value):
    count = lax.axis_size("tile")
    route = []
    for low in range(1, count - 1, 2):
        route += [(low, low + 1), (low + 1, low)]
    return lax.ppermute(value, "tile", route)


def body(
    displacement,
    velocity,
    external_load,
    node_mass,
    modulus,
    stiffness,
    substeps,
    interface_nodes,
    factor_inverse,
    factor_lower,
):
    flags = Place()
    sub = lax.axis_index("sub")
    step = coarse_step / substeps.astype(f32)
    state = [displacement[0], velocity[0], external_load[0], node_mass[0], modulus[0]]
    packed = jax.ShapeDtypeStruct((PACKED, CY, CZ), f32)
    inverse = lax.dynamic_index_in_dim(factor_inverse, sub // 2, 0, keepdims=False)
    lower = lax.dynamic_index_in_dim(factor_lower, sub // 2, 0, keepdims=False)
    transition = local_call(transition_kernel, flags, [inverse, lower], MAT, 6 * IB**3)
    outer, inner = local_call(pack_kernel, flags, state, (packed, packed))
    block, levels = first_products(flags, transition, outer)
    inner = swap(inner, 1)
    near = swap(after(block[1], inner), MASKS[1])
    outer = outer_swap(outer)
    block, levels = merge_level(flags, 1, block, levels, near)
    merged, half = block
    fetched = merged, [swap(half, mask) for mask in (SPLIT_MASKS[0], OPPOSITE, SPLIT_MASKS[1])]
    outer = after(outer, half)
    final_displacement, final_velocity, picked = substeps_call(
        substeps, step, state, outer, inner, stiffness, interface_nodes
    )
    coupled = coupled_velocity(
        flags,
        picked,
        inverse,
        transition,
        fetched,
        levels,
        final_velocity,
        node_mass[0],
        interface_nodes,
    )
    return final_displacement[None], coupled[None]


def solution(mesh):
    in_specs = (
        P("sub", None, "tile", None, None),
        P("sub", None, "tile", None, None),
        P("sub", None, "tile", None, None),
        P("sub", "tile", None, None),
        P("sub", "tile", None, None),
        P(),
        P("sub"),
        P("sub", "tile"),
        P(None, "tile", None),
        P(None, "tile", None),
    )
    out_specs = (P("sub", None, "tile", None, None), P("sub", None, "tile", None, None))
    return jax.shard_map(body, mesh=mesh, in_specs=in_specs, out_specs=out_specs, check_vma=False)
```

```python
import jax
import jax.numpy as jnp
from jax import lax
from jax.experimental import pallas as pl
from jax.experimental.pallas import tpu as pltpu
from jax.sharding import PartitionSpec as P

IFC = 128
IB = 384
HALF = IB // 2
GRANT = 12 << 20
CX, CY, CZ = 4, 32, 128
DEEP = 3 * CX
NEAR = CX - 1
PACKED = 37
CORE, PAIR, SIDE, LAST = 0, 6, 7, 8
GROUPS = CY // 8
MASKS = (1, 2, 4, 12, 16, 48)
SPLIT_MASKS = (4, 12)
OPPOSITE = 10
ROW_TILES = 16

coarse_step = 0.1
f32 = jnp.float32
bf16 = jnp.bfloat16
VM = pl.BlockSpec(memory_space=pltpu.VMEM)
MAT = jax.ShapeDtypeStruct((IB, IB), f32)
HALFMAT = jax.ShapeDtypeStruct((HALF, IB), f32)
ROW = jax.ShapeDtypeStruct((1, IB), f32)


def swap(value, mask):
    return lax.ppermute(value, "tile", [(i, i ^ mask) for i in range(lax.axis_size("tile"))])


def cost(flops, nbytes):
    return pl.CostEstimate(flops=flops, bytes_accessed=nbytes, transcendentals=0)


class Place:
    def __getitem__(self, item):
        tile, sub = lax.axis_index("tile"), lax.axis_index("sub")
        if item == PAIR:
            return sub // 2
        if item == SIDE:
            return sub % 2
        if item == LAST:
            return (tile == lax.axis_size("tile") - 1).astype(jnp.int32)
        return (tile >> item) & 1


def local_call(kernel, place, operands, outs, flops=0):
    nbytes = sum(o.size * 4 for o in operands)

    def placed(*refs):
        kernel(place, *refs)

    return pl.pallas_call(
        placed,
        out_shape=outs,
        in_specs=[VM] * len(operands),
        out_specs=jax.tree.map(lambda _: VM, outs),
        compiler_params=pltpu.CompilerParams(vmem_limit_bytes=GRANT),
        cost_estimate=cost(flops, nbytes),
    )(*operands)


def halves(value):
    high = value.astype(bf16)
    return high, (value - high.astype(f32)).astype(bf16)


def product(a, b):
    a_high, a_low = halves(a)
    b_high, b_low = halves(b)
    return (
        jnp.dot(a_low, b_high, preferred_element_type=f32)
        + jnp.dot(a_high, b_low, preferred_element_type=f32)
        + jnp.dot(a_high, b_high, preferred_element_type=f32)
    )


def eye_mask(size):
    return lax.broadcasted_iota(jnp.int32, (size, size), 0) == lax.broadcasted_iota(
        jnp.int32, (size, size), 1
    )


def column_to_row(column):
    eye = eye_mask(IFC)
    return jnp.concatenate(
        [
            jnp.sum(jnp.where(eye, column[k : k + IFC], 0.0), axis=0, keepdims=True)
            for k in range(0, IB, IFC)
        ],
        axis=1,
    )


def row_to_column(row):
    eye = eye_mask(IFC)
    return jnp.concatenate(
        [
            jnp.sum(jnp.where(eye, row[:, k : k + IFC], 0.0), axis=1, keepdims=True)
            for k in range(0, IB, IFC)
        ],
        axis=0,
    )


def apply(matrix, row):
    return column_to_row(jnp.sum(matrix * row, axis=1, keepdims=True))


def apply_transposed(matrix, row):
    return jnp.sum(matrix * row_to_column(row), axis=0, keepdims=True)


def triple(value):
    high = value.astype(bf16)
    rest = value - high.astype(f32)
    middle = rest.astype(bf16)
    return high, middle, (rest - middle.astype(f32)).astype(bf16)


def slot_masks(nodes):
    index = lax.broadcasted_iota(jnp.int32, (IFC, IFC), 0)
    return index == nodes // CZ, index == nodes % CZ


def wide(value):
    return jnp.concatenate([value[8 * g : 8 * g + 8] for g in range(GROUPS)], axis=1)


def tall(value):
    return jnp.concatenate([value[:, CZ * g : CZ * g + CZ] for g in range(GROUPS)], axis=0)


def spread(values):
    row = lax.broadcasted_iota(jnp.int32, (192, 24), 0) // 8
    rows = (row == lax.broadcasted_iota(jnp.int32, (192, 24), 1)).astype(f32).astype(bf16)
    block = lax.broadcasted_iota(jnp.int32, (24, 192), 1) // 8
    side = block // 12
    dof = 8 * (block % 12 // 4) + 4 * side + block % 4
    columns = (dof == lax.broadcasted_iota(jnp.int32, (24, 192), 0)).astype(f32).astype(bf16)
    tall_values = jnp.dot(rows, values, preferred_element_type=f32).astype(bf16)
    full = jnp.dot(tall_values, columns, preferred_element_type=f32)
    same = (
        lax.broadcasted_iota(jnp.int32, (192, 192), 0) % 8
        == lax.broadcasted_iota(jnp.int32, (192, 192), 1) % 8
    )
    return jnp.where(same, full, 0.0).astype(bf16)


def substep_kernel(
    steps, displacement, velocity, external_load, node_mass, modulus,
    outer, inner, stiff, nodes,
    displacement_out, velocity_out, picked,
    disp, vel, load, inverse_mass, factor, even, odd, even_force, odd_force, upper,
):
    flags = Place()
    first = flags[CORE] == 0

    def put_mass(low, mass):
        present = mass > 0.0
        inverse_mass[pl.ds(low, mass.shape[0])] = jnp.where(
            present, 1.0 / jnp.where(present, mass, 1.0), 0.0
        )

    def put_factor(low, source, base):
        row = lax.broadcasted_iota(jnp.int32, (CY, CZ), 0)
        for x in range(CX):
            factor[low + x] = wide(jnp.where(row < CY - 1, source[base + x], 0.0))

    def place(source, low, shift):
        for i in range(3):
            disp[i, pl.ds(low, CX)] = source[pl.ds(CX * i, CX)]
            vel[i, pl.ds(low + shift, NEAR)] = source[pl.ds(12 + NEAR * i, NEAR)]
            load[i, pl.ds(low + shift, NEAR)] = source[pl.ds(21 + NEAR * i, NEAR)]
        put_mass(low + shift, source[pl.ds(30, NEAR)])
        put_factor(low, source, 33)

    disp[:, CX : 2 * CX] = displacement[...]
    vel[:, CX : 2 * CX] = velocity[...]
    load[:, CX : 2 * CX] = external_load[...]
    put_mass(CX, node_mass[...])
    put_factor(CX, modulus, 0)

    @pl.when(first)
    def _():
        place(outer, 0, 1)
        place(inner, 2 * CX, 0)

    @pl.when(jnp.logical_not(first))
    def _():
        place(inner, 0, 1)
        place(outer, 2 * CX, 0)

    @pl.when(flags[LAST] == 1)
    def _():
        factor[2 * CX - 1] = jnp.zeros((8, GROUPS * CZ), f32)

    length = steps[1:2]

    def put_features(layer, below, above):
        columns = []
        for i in range(3):
            base = disp[i, layer]
            turned = pltpu.roll(base, CZ - 1, 1)
            columns += [base, turned, pltpu.roll(base, CY - 1, 0), pltpu.roll(turned, CY - 1, 0)]
        for g in range(GROUPS):
            lanes = slice(CZ * g, CZ * g + CZ)
            block = jnp.concatenate([c[8 * g : 8 * g + 8] for c in columns], axis=0)
            high, low = halves(block)
            for target, start in ((below, 96), (above, 0)):
                if target is not None:
                    target[start : start + 96, lanes] = high
                    target[start + 192 : start + 288, lanes] = low
                    target[start + 384 : start + 480, lanes] = high

    def put_force(source, target):
        target[...] = jnp.dot(stiff[...], source[...], preferred_element_type=f32)

    def corner(force, scale, i, a, r):
        start = 8 * (8 * i + 4 * a + r)
        return force[start : start + 8] * scale

    def keep_upper(layer, force):
        scale = factor[layer]
        for i in range(3):
            for r in range(4):
                upper[4 * i + r] = corner(force, scale, i, 1, r)

    def finish_layer(layer, force):
        scale = factor[layer]
        weight = inverse_mass[layer]
        for i in range(3):
            sums = [corner(force, scale, i, 0, r) + upper[4 * i + r] for r in range(4)]
            s00, s01, s10, s11 = [tall(s) for s in sums]
            base = s00 + pltpu.roll(s10, 1, 0)
            turned = s01 + pltpu.roll(s11, 1, 0)
            internal = base + pltpu.roll(turned, 1, 1)
            speed = vel[i, layer] + length * ((load[i, layer] - internal) * weight)
            vel[i, layer] = speed
            disp[i, layer] = disp[i, layer] + length * speed

    def one_substep(k, carry):
        put_features(k, None, even)
        put_features(k + 1, even, odd)
        put_force(even, even_force)
        put_features(k + 2, odd, even)
        keep_upper(k, even_force)
        put_force(odd, odd_force)
        put_features(k + 3, even, odd)

        def two_layers(pair, carry):
            layer = k + 1 + 2 * pair
            put_force(even, even_force)
            put_features(layer + 3, odd, even)
            finish_layer(layer, odd_force)
            keep_upper(layer, odd_force)
            put_force(odd, odd_force)
            put_features(layer + 4, even, odd)
            finish_layer(layer + 1, even_force)
            keep_upper(layer + 1, even_force)
            return carry

        return lax.fori_loop(0, CX + 1 - k, two_layers, carry)

    lax.fori_loop(0, jnp.max(steps[0:1]).astype(jnp.int32), one_substep, 0)
    displacement_out[...] = disp[:, CX : 2 * CX]
    final = vel[:, CX : 2 * CX]
    velocity_out[...] = final
    in_row, in_column = slot_masks(nodes[...])
    chosen = in_column.astype(f32).astype(bf16)
    parts = []
    for i in range(3):
        pieces = triple(final[i].reshape(CX * CY, CZ))
        values = sum(jnp.dot(p, chosen, preferred_element_type=f32) for p in reversed(pieces))
        parts.append(jnp.sum(jnp.where(in_row, values, 0.0), axis=0, keepdims=True))
    picked[...] = jnp.concatenate(parts, axis=1)


def pack_kernel(flags, displacement, velocity, external_load, node_mass, modulus, outer, inner):
    for target, start in ((outer, flags[CORE]), (inner, 1 - flags[CORE])):
        for i in range(3):
            target[pl.ds(CX * i, CX)] = displacement[i]
            target[pl.ds(12 + NEAR * i, NEAR)] = velocity[i, pl.ds(start, NEAR)]
            target[pl.ds(21 + NEAR * i, NEAR)] = external_load[i, pl.ds(start, NEAR)]
        target[pl.ds(30, NEAR)] = node_mass[pl.ds(start, NEAR)]
        target[pl.ds(33, CX)] = modulus[...]


def spread_kernel(flags, stiffness, stiff):
    high, low = [spread(s) for s in halves(stiffness[...])]
    stiff[...] = jnp.concatenate([high, high, low], axis=1)


def substeps_call(steps, state, outer, inner, stiff, nodes):
    grid_shape = (3, CX, CY, CZ)
    return pl.pallas_call(
        substep_kernel,
        out_shape=(
            jax.ShapeDtypeStruct(grid_shape, f32),
            jax.ShapeDtypeStruct(grid_shape, f32),
            ROW,
        ),
        in_specs=[VM] * 10,
        out_specs=(VM, VM, VM),
        scratch_shapes=[
            pltpu.VMEM((3, DEEP + 2, CY, CZ), f32),
            pltpu.VMEM((3, DEEP, CY, CZ), f32),
            pltpu.VMEM((3, DEEP, CY, CZ), f32),
            pltpu.VMEM((DEEP, CY, CZ), f32),
            pltpu.VMEM((DEEP, 8, GROUPS * CZ), f32),
            pltpu.VMEM((576, GROUPS * CZ), bf16),
            pltpu.VMEM((576, GROUPS * CZ), bf16),
            pltpu.VMEM((192, GROUPS * CZ), f32),
            pltpu.VMEM((192, GROUPS * CZ), f32),
            pltpu.VMEM((12, 8, GROUPS * CZ), f32),
        ],
        compiler_params=pltpu.CompilerParams(vmem_limit_bytes=20 << 20),
        cost_estimate=cost(32 * 2 * 192 * 576 * 512, 3 * 720896),
    )(steps, *state, outer, inner, stiff, nodes)

def transition_kernel(flags, inverse, lower, transition):
    transition[...] = -product(inverse[...], lower[...])


def store_half(flags, half, value_ref):
    @pl.when(flags[CORE] == 0)
    def _():
        half[...] = value_ref[:HALF]

    @pl.when(flags[CORE] == 1)
    def _():
        half[...] = value_ref[HALF:]


def first_merge_kernel(flags, own, other, high_ref, low_ref, merged, half):
    is_high = flags[0] == 1
    high = jnp.where(is_high, own[...], other[...])
    low = jnp.where(is_high, other[...], own[...])
    high_ref[...] = high
    low_ref[...] = low
    merged[...] = product(high, low)
    store_half(flags, half, merged)


def first_reach_kernel(flags, other, prefix, suffix):
    is_high = flags[0] == 1
    identity = eye_mask(IB).astype(f32)
    prefix[...] = jnp.where(is_high, other[...], identity)
    suffix[...] = jnp.where(is_high, identity, other[...])


def whole(first, near, far):
    return jnp.concatenate(
        [jnp.where(first, near[...], far[...]), jnp.where(first, far[...], near[...])], axis=0
    )


def merge_kernel(level, last, flags, own, near, far, high_ref, low_ref, *outs):
    is_high = flags[level] == 1
    other = whole(flags[CORE] == 0, near, far)
    high = jnp.where(is_high, own[...], other)
    low = jnp.where(is_high, other, own[...])
    high_ref[...] = high
    low_ref[...] = low
    if not last:
        merged, half = outs
        merged[...] = product(high, low)
        store_half(flags, half, merged)


def block_index(flags):
    return flags[2] + 2 * flags[3]


def sort_kernel(flags, own, near, far, near_far, far_far, near_across, far_across, blocks):
    first = flags[CORE] == 0
    mine = block_index(flags)
    blocks[mine] = own[...]
    for change, pieces in enumerate(((near, far), (near_far, far_far), (near_across, far_across))):
        blocks[mine ^ (change + 1)] = whole(first, *pieces)


def row_kernel(flags, blocks, high, low, merged, half):
    low[...] = product(blocks[1], blocks[0])
    high[...] = product(blocks[3], blocks[2])
    merged[...] = product(high[...], low[...])
    store_half(flags, half, merged)


def row_reach_kernel(flags, blocks, high, low, prefix, suffix, new_prefix, new_suffix):
    base = 2 * flags[3]
    is_high = flags[2] == 1
    longer = product(
        jnp.where(is_high, prefix[...], blocks[base + 1]),
        jnp.where(is_high, blocks[base], suffix[...]),
    )
    new_prefix[...] = jnp.where(is_high, longer, prefix[...])
    new_suffix[...] = jnp.where(is_high, suffix[...], longer)
    in_upper = flags[3] == 1
    longer = product(
        jnp.where(in_upper, new_prefix[...], high[...]),
        jnp.where(in_upper, low[...], new_suffix[...]),
    )
    new_prefix[...] = jnp.where(in_upper, longer, new_prefix[...])
    new_suffix[...] = jnp.where(in_upper, new_suffix[...], longer)


def ordered(flags, rows):
    mine = block_index(flags)
    first = flags[CORE] == 0
    own, split, other_split, opposite = [row[...] for row in rows]
    one = jnp.where(first, split, other_split)
    three = jnp.where(first, other_split, split)
    result = []
    for block in range(4):
        change = mine ^ block
        value = jnp.where(change == 1, one, own)
        value = jnp.where(change == 2, opposite, value)
        result.append(jnp.where(change == 3, three, value))
    return mine, result


def row_forward_kernel(flags, own, split, other_split, opposite, blocks, total, entering):
    mine, rows = ordered(flags, (own, split, other_split, opposite))
    state = rows[0]
    before = jnp.zeros_like(state)
    for block in range(1, 4):
        before = jnp.where(mine == block, state, before)
        state = rows[block] + apply(blocks[block], state)
    total[...] = state
    entering[...] = before


def row_backward_kernel(flags, own, split, other_split, opposite, blocks, total, entering):
    mine, rows = ordered(flags, (own, split, other_split, opposite))
    state = rows[3]
    before = jnp.zeros_like(state)
    for block in range(2, -1, -1):
        before = jnp.where(mine == block, state, before)
        state = rows[block] + apply_transposed(blocks[block], state)
    total[...] = state
    entering[...] = before


def below_row(flags, hop):
    first_row = flags[4] + flags[5] == 0
    return jnp.where(first_row, 0.0, hop[...])


def hop_kernel(flags, total, hop, merged, leaving):
    leaving[...] = total[...] + apply(merged[...], below_row(flags, hop))


def reach_kernel(level, flags, high, low, prefix, suffix, new_prefix, new_suffix):
    is_high = flags[level] == 1
    longer = product(
        jnp.where(is_high, prefix[...], high[...]), jnp.where(is_high, low[...], suffix[...])
    )
    new_prefix[...] = jnp.where(is_high, longer, prefix[...])
    new_suffix[...] = jnp.where(is_high, suffix[...], longer)


def start_kernel(flags, inverse, picked, partner, offset):
    sign = (1 - 2 * flags[SIDE]).astype(f32)
    offset[...] = apply(inverse[...], sign * (picked[...] - partner[...]))


def forward_kernel(level, flags, own, other, high_matrix, total):
    is_high = flags[level] == 1
    high = jnp.where(is_high, own[...], other[...])
    low = jnp.where(is_high, other[...], own[...])
    total[...] = high + apply(high_matrix[...], low)


def backward_kernel(level, flags, own, other, low_matrix, total):
    is_high = flags[level] == 1
    high = jnp.where(is_high, own[...], other[...])
    low = jnp.where(is_high, other[...], own[...])
    total[...] = low + apply_transposed(low_matrix[...], high)


def forward_part_kernel(flags, other_0, other_1, in_row, prefix_0, prefix_1, result):
    result[...] = jnp.where(flags[0] == 1, other_0[...], 0.0) + apply(prefix_1[...], in_row[...])

    @pl.when(flags[1] == 1)
    def _():
        result[...] = result[...] + apply(prefix_0[...], other_1[...])


def backward_part_kernel(
    flags, other_0, other_1, in_row, other_4, suffix_0, suffix_1, suffix_3, result
):
    result[...] = jnp.where(flags[0] == 0, other_0[...], 0.0) + apply_transposed(
        suffix_1[...], in_row[...]
    )

    @pl.when(flags[1] == 0)
    def _():
        result[...] = result[...] + apply_transposed(suffix_0[...], other_1[...])

    @pl.when(flags[4] == 0)
    def _():
        result[...] = result[...] + apply_transposed(suffix_3[...], other_4[...])


def turn_kernel(flags, entering, hop, prefix, transition, offset, solved, returning):
    before = entering[...] + apply(prefix[...], below_row(flags, hop))
    current = offset[...] + apply(transition[...], before)
    solved[...] = current
    returning[...] = -apply_transposed(transition[...], current)


def finish_kernel(
    flags, inverse, entering, other, suffix, solved, velocity, node_mass, nodes, velocity_out
):
    after = entering[...] + jnp.where(flags[5] == 0, 1.0, 0.0) * apply_transposed(
        suffix[...], other[...]
    )
    sign = (1 - 2 * flags[SIDE]).astype(f32)
    multiplier = sign * apply_transposed(inverse[...], solved[...] - after)
    in_row, in_column = slot_masks(nodes[...])
    chosen = in_column.astype(f32).astype(bf16)
    weight = 1.0 / node_mass[...]
    for i in range(3):
        held = jnp.where(in_row, multiplier[:, IFC * i : IFC * i + IFC], 0.0)
        change = sum(
            lax.dot_general(p, chosen, (((1,), (1,)), ((), ())), preferred_element_type=f32)
            for p in reversed(triple(held))
        )
        velocity_out[i] = velocity[i] - change.reshape(CX, CY, CZ) * weight


def bound(level, kernel, *fixed):
    def run(*refs):
        kernel(level, *fixed, *refs)

    return run


def after(value, *earlier):
    return lax.optimization_barrier((value, *earlier))[0]


def first_products(flags, transition, gate):
    cube = 6 * IB**3
    other = after(swap(transition, MASKS[0]), gate)
    high, low, merged, half = local_call(
        first_merge_kernel, flags, [transition, other], (MAT, MAT, MAT, HALFMAT), cube
    )
    prefix, suffix = local_call(first_reach_kernel, flags, [other], (MAT, MAT))
    return (merged, half), [(high, low, prefix, suffix)]


def merge_level(flags, level, block, levels, near):
    cube = 6 * IB**3
    merged, half = block
    far = swap(near, 1)
    last = level == 4
    high, low, *block = local_call(
        bound(level, merge_kernel, last),
        flags,
        [merged, near, far],
        (MAT, MAT) if last else (MAT, MAT, MAT, HALFMAT),
        cube,
    )
    prefix, suffix = local_call(
        bound(level, reach_kernel), flags, [high, low, *levels[-1][2:]], (MAT, MAT), cube
    )
    return block, levels + [(high, low, prefix, suffix)]


def split_swap(value):
    masks = [SPLIT_MASKS[i & 1] for i in range(lax.axis_size("tile"))]
    return lax.ppermute(value, "tile", [(i, i ^ mask) for i, mask in enumerate(masks)])


def row_exchange(total):
    opposite = swap(total, OPPOSITE)
    split = split_swap(total)
    return [split, swap(split, 1), opposite]


def sorted_blocks(flags, fetched, gate):
    merged, nears = fetched
    pieces = []
    for near in nears:
        near = after(near, *gate)
        pieces += [near, swap(near, 1)]
    return local_call(
        sort_kernel, flags, [merged, *pieces], jax.ShapeDtypeStruct((4, IB, IB), f32)
    )


def coupled_velocity(
    flags, picked, inverse, transition, fetched, levels, velocity, node_mass, nodes
):
    square = 2 * IB * IB
    cube = 6 * IB**3
    prefix_0, suffix_0 = levels[0][2:]
    prefix_1, suffix_1 = levels[1][2:]
    count = lax.axis_size("sub")
    partner = lax.ppermute(picked, "sub", [(i, i ^ 1) for i in range(count)])
    offset = local_call(start_kernel, flags, [inverse, picked, partner], ROW, square)
    total, others = offset, []
    for level in range(2):
        others.append(after(swap(total, MASKS[level]), prefix_1))
        total = local_call(
            bound(level, forward_kernel), flags, [total, others[-1], levels[level][0]], ROW, square
        )
    arrived = row_exchange(total)
    blocks = sorted_blocks(flags, fetched, (arrived[0], arrived[2]))
    total, in_row = local_call(
        row_forward_kernel, flags, [total, *arrived, blocks], (ROW, ROW), 3 * square
    )
    high, low, *row = local_call(
        row_kernel, flags, [after(blocks, total)], (MAT, MAT, MAT, HALFMAT), 3 * cube
    )
    merged = row[0]
    hop = up_row(total)
    hop = after(hop, merged)
    leaving = local_call(hop_kernel, flags, [total, hop, merged], ROW, square)
    hop = up_row(leaving)
    prefix_3, suffix_3 = local_call(
        row_reach_kernel, flags, [blocks, high, low, prefix_1, suffix_1], (MAT, MAT), 2 * cube
    )
    hop = after(hop, prefix_3)
    leaving = local_call(hop_kernel, flags, [total, hop, merged], ROW, square)
    hop = up_row(leaving)
    entering = local_call(
        forward_part_kernel, flags, [*others, after(in_row, leaving), prefix_0, prefix_1], ROW, 2 * square
    )
    hop = after(hop, entering)
    row[1] = after(row[1], hop)
    solved, returning = local_call(
        turn_kernel,
        flags,
        [entering, hop, prefix_3, transition, offset],
        (ROW, ROW),
        3 * square,
    )
    total, others = returning, []
    for level in range(2):
        others.append(swap(total, MASKS[level]))
        total = local_call(
            bound(level, backward_kernel), flags, [total, others[-1], levels[level][1]], ROW, square
        )
    arrived = row_exchange(total)
    near = after(swap(row[1], MASKS[4]), arrived[1], arrived[2])
    row, levels = merge_level(
        flags, 4, row, levels + [None, (None, None, prefix_3, suffix_3)], near
    )
    _, low, _, suffix_4 = levels[4]
    total, in_row = local_call(
        row_backward_kernel, flags, [total, *arrived, blocks], (ROW, ROW), 3 * square
    )
    others.append(swap(total, MASKS[4]))
    total = local_call(
        bound(4, backward_kernel), flags, [total, after(others[-1], suffix_4), low], ROW, square
    )
    last_other = swap(total, MASKS[5])
    entering = local_call(
        backward_part_kernel,
        flags,
        [others[0], others[1], in_row, others[2], suffix_0, suffix_1, suffix_3],
        ROW,
        3 * square,
    )
    return local_call(
        finish_kernel,
        flags,
        [inverse, entering, after(last_other, entering), suffix_4, solved, velocity, node_mass, nodes],
        jax.ShapeDtypeStruct(velocity.shape, f32),
        2 * square,
    )


def up_row(value):
    count = lax.axis_size("tile")
    return lax.ppermute(value, "tile", [(i, (i + ROW_TILES) % count) for i in range(count)])


def outer_swap(value):
    count = lax.axis_size("tile")
    route = []
    for low in range(1, count - 1, 2):
        route += [(low, low + 1), (low + 1, low)]
    return lax.ppermute(value, "tile", route)


def body(
    displacement,
    velocity,
    external_load,
    node_mass,
    modulus,
    stiffness,
    substeps,
    interface_nodes,
    factor_inverse,
    factor_lower,
):
    flags = Place()
    sub = lax.axis_index("sub")
    count = substeps.astype(f32)
    steps = jnp.broadcast_to(jnp.stack([count, coarse_step / count]), (2, CZ))
    stiff = local_call(spread_kernel, flags, [stiffness], jax.ShapeDtypeStruct((192, 576), bf16))
    state = [displacement[0], velocity[0], external_load[0], node_mass[0], modulus[0]]
    packed = jax.ShapeDtypeStruct((PACKED, CY, CZ), f32)
    inverse = lax.dynamic_index_in_dim(factor_inverse, sub // 2, 0, keepdims=False)
    lower = lax.dynamic_index_in_dim(factor_lower, sub // 2, 0, keepdims=False)
    transition = local_call(transition_kernel, flags, [inverse, lower], MAT, 6 * IB**3)
    outer, inner = local_call(pack_kernel, flags, state, (packed, packed))
    block, levels = first_products(flags, transition, outer)
    inner = swap(inner, 1)
    near = swap(after(block[1], inner), MASKS[1])
    outer = outer_swap(outer)
    block, levels = merge_level(flags, 1, block, levels, near)
    merged, half = block
    fetched = merged, [swap(half, mask) for mask in (SPLIT_MASKS[0], OPPOSITE, SPLIT_MASKS[1])]
    outer = after(outer, half)
    final_displacement, final_velocity, picked = substeps_call(
        steps, state, outer, inner, stiff, interface_nodes
    )
    coupled = coupled_velocity(
        flags,
        picked,
        inverse,
        transition,
        fetched,
        levels,
        final_velocity,
        node_mass[0],
        interface_nodes,
    )
    return final_displacement[None], coupled[None]


def solution(mesh):
    in_specs = (
        P("sub", None, "tile", None, None),
        P("sub", None, "tile", None, None),
        P("sub", None, "tile", None, None),
        P("sub", "tile", None, None),
        P("sub", "tile", None, None),
        P(),
        P("sub"),
        P("sub", "tile"),
        P(None, "tile", None),
        P(None, "tile", None),
    )
    out_specs = (P("sub", None, "tile", None, None), P("sub", None, "tile", None, None))
    return jax.shard_map(body, mesh=mesh, in_specs=in_specs, out_specs=out_specs, check_vma=False)
```

```python
import jax
import jax.numpy as jnp
from jax import lax
from jax.experimental import pallas as pl
from jax.experimental.pallas import tpu as pltpu
from jax.sharding import PartitionSpec as P

IFC = 128
IB = 384
HALF = IB // 2
GRANT = 12 << 20
CX, CY, CZ = 4, 32, 128
DEEP = 3 * CX
NEAR = CX - 1
PACKED = 37
CORE, PAIR, SIDE, LAST = 0, 6, 7, 8
GROUPS = CY // 8
MASKS = (1, 2, 4, 12, 16, 48)
SPLIT_MASKS = (4, 12)
OPPOSITE = 10
ROW_TILES = 16

coarse_step = 0.1
f32 = jnp.float32
bf16 = jnp.bfloat16
VM = pl.BlockSpec(memory_space=pltpu.VMEM)
MAT = jax.ShapeDtypeStruct((IB, IB), f32)
HALFMAT = jax.ShapeDtypeStruct((HALF, IB), f32)
ROW = jax.ShapeDtypeStruct((1, IB), f32)


def swap(value, mask):
    return lax.ppermute(value, "tile", [(i, i ^ mask) for i in range(lax.axis_size("tile"))])


def cost(flops, nbytes):
    return pl.CostEstimate(flops=flops, bytes_accessed=nbytes, transcendentals=0)


class Place:
    def __getitem__(self, item):
        tile, sub = lax.axis_index("tile"), lax.axis_index("sub")
        if item == PAIR:
            return sub // 2
        if item == SIDE:
            return sub % 2
        if item == LAST:
            return (tile == lax.axis_size("tile") - 1).astype(jnp.int32)
        return (tile >> item) & 1


def local_call(kernel, place, operands, outs, flops=0):
    nbytes = sum(o.size * 4 for o in operands)

    def placed(*refs):
        kernel(place, *refs)

    return pl.pallas_call(
        placed,
        out_shape=outs,
        in_specs=[VM] * len(operands),
        out_specs=jax.tree.map(lambda _: VM, outs),
        compiler_params=pltpu.CompilerParams(vmem_limit_bytes=GRANT),
        cost_estimate=cost(flops, nbytes),
    )(*operands)


def halves(value):
    high = value.astype(bf16)
    return high, (value - high.astype(f32)).astype(bf16)


def product(a, b):
    a_high, a_low = halves(a)
    b_high, b_low = halves(b)
    return (
        jnp.dot(a_low, b_high, preferred_element_type=f32)
        + jnp.dot(a_high, b_low, preferred_element_type=f32)
        + jnp.dot(a_high, b_high, preferred_element_type=f32)
    )


def eye_mask(size):
    return lax.broadcasted_iota(jnp.int32, (size, size), 0) == lax.broadcasted_iota(
        jnp.int32, (size, size), 1
    )


def column_to_row(column):
    eye = eye_mask(IFC)
    return jnp.concatenate(
        [
            jnp.sum(jnp.where(eye, column[k : k + IFC], 0.0), axis=0, keepdims=True)
            for k in range(0, IB, IFC)
        ],
        axis=1,
    )


def row_to_column(row):
    eye = eye_mask(IFC)
    return jnp.concatenate(
        [
            jnp.sum(jnp.where(eye, row[:, k : k + IFC], 0.0), axis=1, keepdims=True)
            for k in range(0, IB, IFC)
        ],
        axis=0,
    )


def apply(matrix, row):
    return column_to_row(jnp.sum(matrix * row, axis=1, keepdims=True))


def apply_transposed(matrix, row):
    return jnp.sum(matrix * row_to_column(row), axis=0, keepdims=True)


def triple(value):
    high = value.astype(bf16)
    rest = value - high.astype(f32)
    middle = rest.astype(bf16)
    return high, middle, (rest - middle.astype(f32)).astype(bf16)


def slot_masks(nodes):
    index = lax.broadcasted_iota(jnp.int32, (IFC, IFC), 0)
    return index == nodes // CZ, index == nodes % CZ


def wide(value):
    return jnp.concatenate([value[8 * g : 8 * g + 8] for g in range(GROUPS)], axis=1)


def tall(value):
    return jnp.concatenate([value[:, CZ * g : CZ * g + CZ] for g in range(GROUPS)], axis=0)


def spread(values):
    row = lax.broadcasted_iota(jnp.int32, (192, 24), 0) // 8
    rows = (row == lax.broadcasted_iota(jnp.int32, (192, 24), 1)).astype(f32).astype(bf16)
    block = lax.broadcasted_iota(jnp.int32, (24, 192), 1) // 8
    side = block // 12
    dof = 8 * (block % 12 // 4) + 4 * side + block % 4
    columns = (dof == lax.broadcasted_iota(jnp.int32, (24, 192), 0)).astype(f32).astype(bf16)
    tall_values = jnp.dot(rows, values, preferred_element_type=f32).astype(bf16)
    full = jnp.dot(tall_values, columns, preferred_element_type=f32)
    same = (
        lax.broadcasted_iota(jnp.int32, (192, 192), 0) % 8
        == lax.broadcasted_iota(jnp.int32, (192, 192), 1) % 8
    )
    return jnp.where(same, full, 0.0).astype(bf16)


def substep_kernel(
    steps, displacement, velocity, external_load, node_mass, modulus,
    outer, inner, stiff, nodes,
    displacement_out, velocity_out, picked,
    disp, vel, load, inverse_mass, factor, even, odd, even_force, odd_force, upper,
):
    flags = Place()
    first = flags[CORE] == 0

    def put_mass(low, mass):
        present = mass > 0.0
        inverse_mass[pl.ds(low, mass.shape[0])] = jnp.where(
            present, 1.0 / jnp.where(present, mass, 1.0), 0.0
        )

    def put_factor(low, source, base):
        row = lax.broadcasted_iota(jnp.int32, (CY, CZ), 0)
        for x in range(CX):
            factor[low + x] = wide(jnp.where(row < CY - 1, source[base + x], 0.0))

    def place(source, low, shift):
        for i in range(3):
            disp[i, pl.ds(low, CX)] = source[pl.ds(CX * i, CX)]
            vel[i, pl.ds(low + shift, NEAR)] = source[pl.ds(12 + NEAR * i, NEAR)]
            load[i, pl.ds(low + shift, NEAR)] = source[pl.ds(21 + NEAR * i, NEAR)]
        put_mass(low + shift, source[pl.ds(30, NEAR)])
        put_factor(low, source, 33)

    disp[:, CX : 2 * CX] = displacement[...]
    vel[:, CX : 2 * CX] = velocity[...]
    load[:, CX : 2 * CX] = external_load[...]
    put_mass(CX, node_mass[...])
    put_factor(CX, modulus, 0)

    @pl.when(first)
    def _():
        place(outer, 0, 1)
        place(inner, 2 * CX, 0)

    @pl.when(jnp.logical_not(first))
    def _():
        place(inner, 0, 1)
        place(outer, 2 * CX, 0)

    @pl.when(flags[LAST] == 1)
    def _():
        factor[2 * CX - 1] = jnp.zeros((8, GROUPS * CZ), f32)

    length = steps[1:2]

    def put_features(layer, below, above):
        columns = []
        for i in range(3):
            base = disp[i, layer]
            turned = pltpu.roll(base, CZ - 1, 1)
            columns += [base, turned, pltpu.roll(base, CY - 1, 0), pltpu.roll(turned, CY - 1, 0)]
        for g in range(GROUPS):
            lanes = slice(CZ * g, CZ * g + CZ)
            block = jnp.concatenate([c[8 * g : 8 * g + 8] for c in columns], axis=0)
            high, low = halves(block)
            for target, start in ((below, 96), (above, 0)):
                if target is not None:
                    target[start : start + 96, lanes] = high
                    target[start + 192 : start + 288, lanes] = low
                    target[start + 384 : start + 480, lanes] = high

    def put_force(source, target):
        target[...] = jnp.dot(stiff[...], source[...], preferred_element_type=f32)

    def corner(force, scale, i, a, r):
        start = 8 * (8 * i + 4 * a + r)
        return force[start : start + 8] * scale

    def keep_upper(layer, force):
        scale = factor[layer]
        for i in range(3):
            for r in range(4):
                upper[4 * i + r] = corner(force, scale, i, 1, r)

    def finish_layer(layer, force):
        scale = factor[layer]
        weight = inverse_mass[layer]
        for i in range(3):
            sums = [corner(force, scale, i, 0, r) + upper[4 * i + r] for r in range(4)]
            s00, s01, s10, s11 = [tall(s) for s in sums]
            base = s00 + pltpu.roll(s10, 1, 0)
            turned = s01 + pltpu.roll(s11, 1, 0)
            internal = base + pltpu.roll(turned, 1, 1)
            speed = vel[i, layer] + length * ((load[i, layer] - internal) * weight)
            vel[i, layer] = speed
            disp[i, layer] = disp[i, layer] + length * speed

    def one_substep(k, carry):
        put_features(k, None, even)
        put_features(k + 1, even, odd)
        put_force(even, even_force)
        put_features(k + 2, odd, even)
        keep_upper(k, even_force)
        put_force(odd, odd_force)
        put_features(k + 3, even, odd)

        def two_layers(pair, carry):
            layer = k + 1 + 2 * pair
            put_force(even, even_force)
            put_features(layer + 3, odd, even)
            finish_layer(layer, odd_force)
            keep_upper(layer, odd_force)
            put_force(odd, odd_force)
            put_features(layer + 4, even, odd)
            finish_layer(layer + 1, even_force)
            keep_upper(layer + 1, even_force)
            return carry

        return lax.fori_loop(0, CX + 1 - k, two_layers, carry)

    lax.fori_loop(0, jnp.max(steps[0:1]).astype(jnp.int32), one_substep, 0)
    displacement_out[...] = disp[:, CX : 2 * CX]
    final = vel[:, CX : 2 * CX]
    velocity_out[...] = final
    in_row, in_column = slot_masks(nodes[...])
    chosen = in_column.astype(f32).astype(bf16)
    parts = []
    for i in range(3):
        pieces = triple(final[i].reshape(CX * CY, CZ))
        values = sum(jnp.dot(p, chosen, preferred_element_type=f32) for p in reversed(pieces))
        parts.append(jnp.sum(jnp.where(in_row, values, 0.0), axis=0, keepdims=True))
    picked[...] = jnp.concatenate(parts, axis=1)


def pack_kernel(flags, displacement, velocity, external_load, node_mass, modulus, outer, inner):
    for target, start in ((outer, flags[CORE]), (inner, 1 - flags[CORE])):
        for i in range(3):
            target[pl.ds(CX * i, CX)] = displacement[i]
            target[pl.ds(12 + NEAR * i, NEAR)] = velocity[i, pl.ds(start, NEAR)]
            target[pl.ds(21 + NEAR * i, NEAR)] = external_load[i, pl.ds(start, NEAR)]
        target[pl.ds(30, NEAR)] = node_mass[pl.ds(start, NEAR)]
        target[pl.ds(33, CX)] = modulus[...]


def spread_kernel(flags, stiffness, stiff):
    high, low = [spread(s) for s in halves(stiffness[...])]
    stiff[...] = jnp.concatenate([high, high, low], axis=1)


def substeps_call(steps, state, outer, inner, stiff, nodes):
    grid_shape = (3, CX, CY, CZ)
    return pl.pallas_call(
        substep_kernel,
        out_shape=(
            jax.ShapeDtypeStruct(grid_shape, f32),
            jax.ShapeDtypeStruct(grid_shape, f32),
            ROW,
        ),
        in_specs=[VM] * 10,
        out_specs=(VM, VM, VM),
        scratch_shapes=[
            pltpu.VMEM((3, DEEP + 2, CY, CZ), f32),
            pltpu.VMEM((3, DEEP, CY, CZ), f32),
            pltpu.VMEM((3, DEEP, CY, CZ), f32),
            pltpu.VMEM((DEEP, CY, CZ), f32),
            pltpu.VMEM((DEEP, 8, GROUPS * CZ), f32),
            pltpu.VMEM((576, GROUPS * CZ), bf16),
            pltpu.VMEM((576, GROUPS * CZ), bf16),
            pltpu.VMEM((192, GROUPS * CZ), f32),
            pltpu.VMEM((192, GROUPS * CZ), f32),
            pltpu.VMEM((12, 8, GROUPS * CZ), f32),
        ],
        compiler_params=pltpu.CompilerParams(vmem_limit_bytes=20 << 20),
        cost_estimate=cost(32 * 2 * 192 * 576 * 512, 3 * 720896),
    )(steps, *state, outer, inner, stiff, nodes)

def transition_kernel(flags, inverse, lower, transition):
    transition[...] = -product(inverse[...], lower[...])


def store_half(flags, half, value_ref):
    @pl.when(flags[CORE] == 0)
    def _():
        half[...] = value_ref[:HALF]

    @pl.when(flags[CORE] == 1)
    def _():
        half[...] = value_ref[HALF:]


def first_merge_kernel(flags, own, other, high_ref, low_ref, merged, half):
    is_high = flags[0] == 1
    high = jnp.where(is_high, own[...], other[...])
    low = jnp.where(is_high, other[...], own[...])
    high_ref[...] = high
    low_ref[...] = low
    merged[...] = product(high, low)
    store_half(flags, half, merged)


def first_reach_kernel(flags, other, prefix, suffix):
    is_high = flags[0] == 1
    identity = eye_mask(IB).astype(f32)
    prefix[...] = jnp.where(is_high, other[...], identity)
    suffix[...] = jnp.where(is_high, identity, other[...])


def whole(first, near, far):
    return jnp.concatenate(
        [jnp.where(first, near[...], far[...]), jnp.where(first, far[...], near[...])], axis=0
    )


def merge_kernel(level, last, flags, own, near, far, high_ref, low_ref, *outs):
    is_high = flags[level] == 1
    other = whole(flags[CORE] == 0, near, far)
    high = jnp.where(is_high, own[...], other)
    low = jnp.where(is_high, other, own[...])
    high_ref[...] = high
    low_ref[...] = low
    if not last:
        merged, half = outs
        merged[...] = product(high, low)
        store_half(flags, half, merged)


def block_index(flags):
    return flags[2] + 2 * flags[3]


def sort_kernel(flags, own, near, far, near_far, far_far, near_across, far_across, blocks):
    first = flags[CORE] == 0
    mine = block_index(flags)
    blocks[mine] = own[...]
    for change, pieces in enumerate(((near, far), (near_far, far_far), (near_across, far_across))):
        blocks[mine ^ (change + 1)] = whole(first, *pieces)


def row_kernel(flags, blocks, high, low, merged, half):
    low[...] = product(blocks[1], blocks[0])
    high[...] = product(blocks[3], blocks[2])
    merged[...] = product(high[...], low[...])
    store_half(flags, half, merged)


def row_reach_kernel(flags, blocks, high, low, prefix, suffix, new_prefix, new_suffix):
    base = 2 * flags[3]
    is_high = flags[2] == 1
    longer = product(
        jnp.where(is_high, prefix[...], blocks[base + 1]),
        jnp.where(is_high, blocks[base], suffix[...]),
    )
    new_prefix[...] = jnp.where(is_high, longer, prefix[...])
    new_suffix[...] = jnp.where(is_high, suffix[...], longer)
    in_upper = flags[3] == 1
    longer = product(
        jnp.where(in_upper, new_prefix[...], high[...]),
        jnp.where(in_upper, low[...], new_suffix[...]),
    )
    new_prefix[...] = jnp.where(in_upper, longer, new_prefix[...])
    new_suffix[...] = jnp.where(in_upper, new_suffix[...], longer)


def ordered(flags, rows):
    mine = block_index(flags)
    first = flags[CORE] == 0
    own, split, other_split, opposite = [row[...] for row in rows]
    one = jnp.where(first, split, other_split)
    three = jnp.where(first, other_split, split)
    result = []
    for block in range(4):
        change = mine ^ block
        value = jnp.where(change == 1, one, own)
        value = jnp.where(change == 2, opposite, value)
        result.append(jnp.where(change == 3, three, value))
    return mine, result


def row_forward_kernel(flags, own, split, other_split, opposite, blocks, total, entering):
    mine, rows = ordered(flags, (own, split, other_split, opposite))
    state = rows[0]
    before = jnp.zeros_like(state)
    for block in range(1, 4):
        before = jnp.where(mine == block, state, before)
        state = rows[block] + apply(blocks[block], state)
    total[...] = state
    entering[...] = before


def row_backward_kernel(flags, own, split, other_split, opposite, blocks, total, entering):
    mine, rows = ordered(flags, (own, split, other_split, opposite))
    state = rows[3]
    before = jnp.zeros_like(state)
    for block in range(2, -1, -1):
        before = jnp.where(mine == block, state, before)
        state = rows[block] + apply_transposed(blocks[block], state)
    total[...] = state
    entering[...] = before


def below_row(flags, hop):
    first_row = flags[4] + flags[5] == 0
    return jnp.where(first_row, 0.0, hop[...])


def hop_kernel(flags, total, hop, merged, leaving):
    leaving[...] = total[...] + apply(merged[...], below_row(flags, hop))


def reach_kernel(level, flags, high, low, prefix, suffix, new_prefix, new_suffix):
    is_high = flags[level] == 1
    longer = product(
        jnp.where(is_high, prefix[...], high[...]), jnp.where(is_high, low[...], suffix[...])
    )
    new_prefix[...] = jnp.where(is_high, longer, prefix[...])
    new_suffix[...] = jnp.where(is_high, suffix[...], longer)


def start_kernel(flags, inverse, picked, partner, offset):
    sign = (1 - 2 * flags[SIDE]).astype(f32)
    offset[...] = apply(inverse[...], sign * (picked[...] - partner[...]))


def forward_kernel(level, flags, own, other, high_matrix, total):
    is_high = flags[level] == 1
    high = jnp.where(is_high, own[...], other[...])
    low = jnp.where(is_high, other[...], own[...])
    total[...] = high + apply(high_matrix[...], low)


def backward_kernel(level, flags, own, other, low_matrix, total):
    is_high = flags[level] == 1
    high = jnp.where(is_high, own[...], other[...])
    low = jnp.where(is_high, other[...], own[...])
    total[...] = low + apply_transposed(low_matrix[...], high)


def forward_part_kernel(flags, other_0, other_1, in_row, prefix_0, prefix_1, result):
    result[...] = jnp.where(flags[0] == 1, other_0[...], 0.0) + apply(prefix_1[...], in_row[...])

    @pl.when(flags[1] == 1)
    def _():
        result[...] = result[...] + apply(prefix_0[...], other_1[...])


def backward_part_kernel(
    flags, other_0, other_1, in_row, other_4, suffix_0, suffix_1, suffix_3, result
):
    result[...] = jnp.where(flags[0] == 0, other_0[...], 0.0) + apply_transposed(
        suffix_1[...], in_row[...]
    )

    @pl.when(flags[1] == 0)
    def _():
        result[...] = result[...] + apply_transposed(suffix_0[...], other_1[...])

    @pl.when(flags[4] == 0)
    def _():
        result[...] = result[...] + apply_transposed(suffix_3[...], other_4[...])


def turn_kernel(flags, entering, hop, prefix, transition, offset, solved, returning):
    before = entering[...] + apply(prefix[...], below_row(flags, hop))
    current = offset[...] + apply(transition[...], before)
    solved[...] = current
    returning[...] = -apply_transposed(transition[...], current)


def finish_kernel(
    flags, inverse, entering, other, suffix, solved, velocity, node_mass, nodes, velocity_out
):
    after = entering[...] + jnp.where(flags[5] == 0, 1.0, 0.0) * apply_transposed(
        suffix[...], other[...]
    )
    sign = (1 - 2 * flags[SIDE]).astype(f32)
    multiplier = sign * apply_transposed(inverse[...], solved[...] - after)
    in_row, in_column = slot_masks(nodes[...])
    chosen = in_column.astype(f32).astype(bf16)
    weight = 1.0 / node_mass[...]
    for i in range(3):
        held = jnp.where(in_row, multiplier[:, IFC * i : IFC * i + IFC], 0.0)
        change = sum(
            lax.dot_general(p, chosen, (((1,), (1,)), ((), ())), preferred_element_type=f32)
            for p in reversed(triple(held))
        )
        velocity_out[i] = velocity[i] - change.reshape(CX, CY, CZ) * weight


def bound(level, kernel, *fixed):
    def run(*refs):
        kernel(level, *fixed, *refs)

    return run


def after(value, *earlier):
    return lax.optimization_barrier((value, *earlier))[0]


def first_products(flags, transition, gate):
    cube = 6 * IB**3
    other = after(swap(transition, MASKS[0]), gate)
    high, low, merged, half = local_call(
        first_merge_kernel, flags, [transition, other], (MAT, MAT, MAT, HALFMAT), cube
    )
    prefix, suffix = local_call(first_reach_kernel, flags, [other], (MAT, MAT))
    return (merged, half), [(high, low, prefix, suffix)]


def merge_level(flags, level, block, levels, near):
    cube = 6 * IB**3
    merged, half = block
    far = swap(near, 1)
    last = level == 4
    high, low, *block = local_call(
        bound(level, merge_kernel, last),
        flags,
        [merged, near, far],
        (MAT, MAT) if last else (MAT, MAT, MAT, HALFMAT),
        cube,
    )
    prefix, suffix = local_call(
        bound(level, reach_kernel), flags, [high, low, *levels[-1][2:]], (MAT, MAT), cube
    )
    return block, levels + [(high, low, prefix, suffix)]


def split_swap(value):
    masks = [SPLIT_MASKS[i & 1] for i in range(lax.axis_size("tile"))]
    return lax.ppermute(value, "tile", [(i, i ^ mask) for i, mask in enumerate(masks)])


def row_exchange(total):
    opposite = swap(total, OPPOSITE)
    split = split_swap(total)
    return [split, swap(split, 1), opposite]


def sorted_blocks(flags, fetched, gate):
    merged, nears = fetched
    pieces = []
    for near in nears:
        near = after(near, *gate)
        pieces += [near, swap(near, 1)]
    return local_call(
        sort_kernel, flags, [merged, *pieces], jax.ShapeDtypeStruct((4, IB, IB), f32)
    )


def coupled_velocity(
    flags, picked, inverse, transition, fetched, levels, velocity, node_mass, nodes
):
    square = 2 * IB * IB
    cube = 6 * IB**3
    prefix_0, suffix_0 = levels[0][2:]
    prefix_1, suffix_1 = levels[1][2:]
    count = lax.axis_size("sub")
    partner = lax.ppermute(picked, "sub", [(i, i ^ 1) for i in range(count)])
    offset = local_call(start_kernel, flags, [inverse, picked, partner], ROW, square)
    total, others = offset, []
    for level in range(2):
        others.append(after(swap(total, MASKS[level]), prefix_1))
        total = local_call(
            bound(level, forward_kernel), flags, [total, others[-1], levels[level][0]], ROW, square
        )
    arrived = row_exchange(total)
    blocks = sorted_blocks(flags, fetched, (arrived[1], arrived[2]))
    total, in_row = local_call(
        row_forward_kernel, flags, [total, *arrived, blocks], (ROW, ROW), 3 * square
    )
    high, low, *row = local_call(
        row_kernel, flags, [after(blocks, total)], (MAT, MAT, MAT, HALFMAT), 3 * cube
    )
    merged = row[0]
    hop = up_row(total)
    hop = after(hop, merged)
    leaving = local_call(hop_kernel, flags, [total, hop, merged], ROW, square)
    hop = up_row(leaving)
    prefix_3, suffix_3 = local_call(
        row_reach_kernel, flags, [blocks, high, low, prefix_1, suffix_1], (MAT, MAT), 2 * cube
    )
    hop = after(hop, prefix_3)
    leaving = local_call(hop_kernel, flags, [total, hop, merged], ROW, square)
    hop = up_row(leaving)
    entering = local_call(
        forward_part_kernel, flags, [*others, after(in_row, leaving), prefix_0, prefix_1], ROW, 2 * square
    )
    hop = after(hop, entering)
    row[1] = after(row[1], hop)
    solved, returning = local_call(
        turn_kernel,
        flags,
        [entering, hop, prefix_3, transition, offset],
        (ROW, ROW),
        3 * square,
    )
    total, others = returning, []
    for level in range(2):
        others.append(swap(total, MASKS[level]))
        total = local_call(
            bound(level, backward_kernel), flags, [total, others[-1], levels[level][1]], ROW, square
        )
    arrived = row_exchange(total)
    near = after(swap(row[1], MASKS[4]), arrived[1], arrived[2])
    row, levels = merge_level(
        flags, 4, row, levels + [None, (None, None, prefix_3, suffix_3)], near
    )
    _, low, _, suffix_4 = levels[4]
    total, in_row = local_call(
        row_backward_kernel, flags, [total, *arrived, blocks], (ROW, ROW), 3 * square
    )
    others.append(swap(total, MASKS[4]))
    total = local_call(
        bound(4, backward_kernel), flags, [total, after(others[-1], suffix_4), low], ROW, square
    )
    last_other = swap(total, MASKS[5])
    entering = local_call(
        backward_part_kernel,
        flags,
        [others[0], others[1], in_row, others[2], suffix_0, suffix_1, suffix_3],
        ROW,
        3 * square,
    )
    return local_call(
        finish_kernel,
        flags,
        [inverse, entering, after(last_other, entering), suffix_4, solved, velocity, node_mass, nodes],
        jax.ShapeDtypeStruct(velocity.shape, f32),
        2 * square,
    )


def up_row(value):
    count = lax.axis_size("tile")
    return lax.ppermute(value, "tile", [(i, (i + ROW_TILES) % count) for i in range(count)])


def outer_swap(value):
    count = lax.axis_size("tile")
    route = []
    for low in range(1, count - 1, 2):
        route += [(low, low + 1), (low + 1, low)]
    return lax.ppermute(value, "tile", route)


def body(
    displacement,
    velocity,
    external_load,
    node_mass,
    modulus,
    stiffness,
    substeps,
    interface_nodes,
    factor_inverse,
    factor_lower,
):
    flags = Place()
    sub = lax.axis_index("sub")
    count = substeps.astype(f32)
    steps = jnp.broadcast_to(jnp.stack([count, coarse_step / count]), (2, CZ))
    stiff = local_call(spread_kernel, flags, [stiffness], jax.ShapeDtypeStruct((192, 576), bf16))
    state = [displacement[0], velocity[0], external_load[0], node_mass[0], modulus[0]]
    packed = jax.ShapeDtypeStruct((PACKED, CY, CZ), f32)
    inverse = lax.dynamic_index_in_dim(factor_inverse, sub // 2, 0, keepdims=False)
    lower = lax.dynamic_index_in_dim(factor_lower, sub // 2, 0, keepdims=False)
    transition = local_call(transition_kernel, flags, [inverse, lower], MAT, 6 * IB**3)
    outer, inner = local_call(pack_kernel, flags, state, (packed, packed))
    block, levels = first_products(flags, transition, outer)
    inner = swap(inner, 1)
    near = swap(after(block[1], inner), MASKS[1])
    outer = outer_swap(outer)
    block, levels = merge_level(flags, 1, block, levels, near)
    merged, half = block
    fetched = merged, [swap(half, mask) for mask in (SPLIT_MASKS[0], OPPOSITE, SPLIT_MASKS[1])]
    outer = after(outer, half)
    final_displacement, final_velocity, picked = substeps_call(
        steps, state, outer, inner, stiff, interface_nodes
    )
    coupled = coupled_velocity(
        flags,
        picked,
        inverse,
        transition,
        fetched,
        levels,
        final_velocity,
        node_mass[0],
        interface_nodes,
    )
    return final_displacement[None], coupled[None]


def solution(mesh):
    in_specs = (
        P("sub", None, "tile", None, None),
        P("sub", None, "tile", None, None),
        P("sub", None, "tile", None, None),
        P("sub", "tile", None, None),
        P("sub", "tile", None, None),
        P(),
        P("sub"),
        P("sub", "tile"),
        P(None, "tile", None),
        P(None, "tile", None),
    )
    out_specs = (P("sub", None, "tile", None, None), P("sub", None, "tile", None, None))
    return jax.shard_map(body, mesh=mesh, in_specs=in_specs, out_specs=out_specs, check_vma=False)
```

```python
import jax
import jax.numpy as jnp
from jax import lax
from jax.experimental import pallas as pl
from jax.experimental.pallas import tpu as pltpu
from jax.sharding import PartitionSpec as P

IFC = 128
IB = 384
HALF = IB // 2
GRANT = 12 << 20
CX, CY, CZ = 4, 32, 128
DEEP = 3 * CX
NEAR = CX - 1
PACKED = 37
CORE, PAIR, SIDE, LAST = 0, 6, 7, 8
GROUPS = CY // 8
MASKS = (1, 2, 4, 12, 16, 48)
SPLIT_MASKS = (4, 12)
OPPOSITE = 10

coarse_step = 0.1
f32 = jnp.float32
bf16 = jnp.bfloat16
VM = pl.BlockSpec(memory_space=pltpu.VMEM)
MAT = jax.ShapeDtypeStruct((IB, IB), f32)
HALFMAT = jax.ShapeDtypeStruct((HALF, IB), f32)
ROW = jax.ShapeDtypeStruct((1, IB), f32)


def swap(value, mask):
    return lax.ppermute(value, "tile", [(i, i ^ mask) for i in range(lax.axis_size("tile"))])


def cost(flops, nbytes):
    return pl.CostEstimate(flops=flops, bytes_accessed=nbytes, transcendentals=0)


class Place:
    def __getitem__(self, item):
        tile, sub = lax.axis_index("tile"), lax.axis_index("sub")
        if item == PAIR:
            return sub // 2
        if item == SIDE:
            return sub % 2
        if item == LAST:
            return (tile == lax.axis_size("tile") - 1).astype(jnp.int32)
        return (tile >> item) & 1


def local_call(kernel, place, operands, outs, flops=0):
    nbytes = sum(o.size * 4 for o in operands)

    def placed(*refs):
        kernel(place, *refs)

    return pl.pallas_call(
        placed,
        out_shape=outs,
        in_specs=[VM] * len(operands),
        out_specs=jax.tree.map(lambda _: VM, outs),
        compiler_params=pltpu.CompilerParams(vmem_limit_bytes=GRANT),
        cost_estimate=cost(flops, nbytes),
    )(*operands)


def halves(value):
    high = value.astype(bf16)
    return high, (value - high.astype(f32)).astype(bf16)


def product(a, b):
    a_high, a_low = halves(a)
    b_high, b_low = halves(b)
    return (
        jnp.dot(a_low, b_high, preferred_element_type=f32)
        + jnp.dot(a_high, b_low, preferred_element_type=f32)
        + jnp.dot(a_high, b_high, preferred_element_type=f32)
    )


def eye_mask(size):
    return lax.broadcasted_iota(jnp.int32, (size, size), 0) == lax.broadcasted_iota(
        jnp.int32, (size, size), 1
    )


def column_to_row(column):
    eye = eye_mask(IFC)
    return jnp.concatenate(
        [
            jnp.sum(jnp.where(eye, column[k : k + IFC], 0.0), axis=0, keepdims=True)
            for k in range(0, IB, IFC)
        ],
        axis=1,
    )


def row_to_column(row):
    eye = eye_mask(IFC)
    return jnp.concatenate(
        [
            jnp.sum(jnp.where(eye, row[:, k : k + IFC], 0.0), axis=1, keepdims=True)
            for k in range(0, IB, IFC)
        ],
        axis=0,
    )


def apply(matrix, row):
    return column_to_row(jnp.sum(matrix * row, axis=1, keepdims=True))


def apply_transposed(matrix, row):
    return jnp.sum(matrix * row_to_column(row), axis=0, keepdims=True)


def triple(value):
    high = value.astype(bf16)
    rest = value - high.astype(f32)
    middle = rest.astype(bf16)
    return high, middle, (rest - middle.astype(f32)).astype(bf16)


def slot_masks(nodes):
    index = lax.broadcasted_iota(jnp.int32, (IFC, IFC), 0)
    return index == nodes // CZ, index == nodes % CZ


def wide(value):
    return jnp.concatenate([value[8 * g : 8 * g + 8] for g in range(GROUPS)], axis=1)


def tall(value):
    return jnp.concatenate([value[:, CZ * g : CZ * g + CZ] for g in range(GROUPS)], axis=0)


def spread(values):
    row = lax.broadcasted_iota(jnp.int32, (192, 24), 0) // 8
    rows = (row == lax.broadcasted_iota(jnp.int32, (192, 24), 1)).astype(f32).astype(bf16)
    block = lax.broadcasted_iota(jnp.int32, (24, 192), 1) // 8
    side = block // 12
    dof = 8 * (block % 12 // 4) + 4 * side + block % 4
    columns = (dof == lax.broadcasted_iota(jnp.int32, (24, 192), 0)).astype(f32).astype(bf16)
    tall_values = jnp.dot(rows, values, preferred_element_type=f32).astype(bf16)
    full = jnp.dot(tall_values, columns, preferred_element_type=f32)
    same = (
        lax.broadcasted_iota(jnp.int32, (192, 192), 0) % 8
        == lax.broadcasted_iota(jnp.int32, (192, 192), 1) % 8
    )
    return jnp.where(same, full, 0.0).astype(bf16)


def substep_kernel(
    steps, displacement, velocity, external_load, node_mass, modulus,
    outer, inner, stiff, nodes,
    displacement_out, velocity_out, picked,
    disp, vel, load, inverse_mass, factor, even, odd, even_force, odd_force, upper,
):
    flags = Place()
    first = flags[CORE] == 0

    def put_mass(low, mass):
        present = mass > 0.0
        inverse_mass[pl.ds(low, mass.shape[0])] = jnp.where(
            present, 1.0 / jnp.where(present, mass, 1.0), 0.0
        )

    def put_factor(low, source, base):
        row = lax.broadcasted_iota(jnp.int32, (CY, CZ), 0)
        for x in range(CX):
            factor[low + x] = wide(jnp.where(row < CY - 1, source[base + x], 0.0))

    def place(source, low, shift):
        for i in range(3):
            disp[i, pl.ds(low, CX)] = source[pl.ds(CX * i, CX)]
            vel[i, pl.ds(low + shift, NEAR)] = source[pl.ds(12 + NEAR * i, NEAR)]
            load[i, pl.ds(low + shift, NEAR)] = source[pl.ds(21 + NEAR * i, NEAR)]
        put_mass(low + shift, source[pl.ds(30, NEAR)])
        put_factor(low, source, 33)

    disp[:, CX : 2 * CX] = displacement[...]
    vel[:, CX : 2 * CX] = velocity[...]
    load[:, CX : 2 * CX] = external_load[...]
    put_mass(CX, node_mass[...])
    put_factor(CX, modulus, 0)

    @pl.when(first)
    def _():
        place(outer, 0, 1)
        place(inner, 2 * CX, 0)

    @pl.when(jnp.logical_not(first))
    def _():
        place(inner, 0, 1)
        place(outer, 2 * CX, 0)

    @pl.when(flags[LAST] == 1)
    def _():
        factor[2 * CX - 1] = jnp.zeros((8, GROUPS * CZ), f32)

    length = steps[1:2]

    def put_features(layer, below, above):
        columns = []
        for i in range(3):
            base = disp[i, layer]
            turned = pltpu.roll(base, CZ - 1, 1)
            columns += [base, turned, pltpu.roll(base, CY - 1, 0), pltpu.roll(turned, CY - 1, 0)]
        for g in range(GROUPS):
            lanes = slice(CZ * g, CZ * g + CZ)
            block = jnp.concatenate([c[8 * g : 8 * g + 8] for c in columns], axis=0)
            high, low = halves(block)
            for target, start in ((below, 96), (above, 0)):
                if target is not None:
                    target[start : start + 96, lanes] = high
                    target[start + 192 : start + 288, lanes] = low
                    target[start + 384 : start + 480, lanes] = high

    def put_force(source, target):
        target[...] = jnp.dot(stiff[...], source[...], preferred_element_type=f32)

    def corner(force, scale, i, a, r):
        start = 8 * (8 * i + 4 * a + r)
        return force[start : start + 8] * scale

    def keep_upper(layer, force):
        scale = factor[layer]
        for i in range(3):
            for r in range(4):
                upper[4 * i + r] = corner(force, scale, i, 1, r)

    def finish_layer(layer, force):
        scale = factor[layer]
        weight = inverse_mass[layer]
        for i in range(3):
            sums = [corner(force, scale, i, 0, r) + upper[4 * i + r] for r in range(4)]
            s00, s01, s10, s11 = [tall(s) for s in sums]
            base = s00 + pltpu.roll(s10, 1, 0)
            turned = s01 + pltpu.roll(s11, 1, 0)
            internal = base + pltpu.roll(turned, 1, 1)
            speed = vel[i, layer] + length * ((load[i, layer] - internal) * weight)
            vel[i, layer] = speed
            disp[i, layer] = disp[i, layer] + length * speed

    def one_substep(k, carry):
        put_features(k, None, even)
        put_features(k + 1, even, odd)
        put_force(even, even_force)
        put_features(k + 2, odd, even)
        keep_upper(k, even_force)
        put_force(odd, odd_force)
        put_features(k + 3, even, odd)

        def two_layers(pair, carry):
            layer = k + 1 + 2 * pair
            put_force(even, even_force)
            put_features(layer + 3, odd, even)
            finish_layer(layer, odd_force)
            keep_upper(layer, odd_force)
            put_force(odd, odd_force)
            put_features(layer + 4, even, odd)
            finish_layer(layer + 1, even_force)
            keep_upper(layer + 1, even_force)
            return carry

        return lax.fori_loop(0, CX + 1 - k, two_layers, carry)

    lax.fori_loop(0, jnp.max(steps[0:1]).astype(jnp.int32), one_substep, 0)
    displacement_out[...] = disp[:, CX : 2 * CX]
    final = vel[:, CX : 2 * CX]
    velocity_out[...] = final
    in_row, in_column = slot_masks(nodes[...])
    chosen = in_column.astype(f32).astype(bf16)
    parts = []
    for i in range(3):
        pieces = triple(final[i].reshape(CX * CY, CZ))
        values = sum(jnp.dot(p, chosen, preferred_element_type=f32) for p in reversed(pieces))
        parts.append(jnp.sum(jnp.where(in_row, values, 0.0), axis=0, keepdims=True))
    picked[...] = jnp.concatenate(parts, axis=1)


def pack_kernel(flags, displacement, velocity, external_load, node_mass, modulus, outer, inner):
    for target, start in ((outer, flags[CORE]), (inner, 1 - flags[CORE])):
        for i in range(3):
            target[pl.ds(CX * i, CX)] = displacement[i]
            target[pl.ds(12 + NEAR * i, NEAR)] = velocity[i, pl.ds(start, NEAR)]
            target[pl.ds(21 + NEAR * i, NEAR)] = external_load[i, pl.ds(start, NEAR)]
        target[pl.ds(30, NEAR)] = node_mass[pl.ds(start, NEAR)]
        target[pl.ds(33, CX)] = modulus[...]


def spread_kernel(flags, stiffness, stiff):
    high, low = [spread(s) for s in halves(stiffness[...])]
    stiff[...] = jnp.concatenate([high, high, low], axis=1)


def substeps_call(steps, state, outer, inner, stiff, nodes):
    grid_shape = (3, CX, CY, CZ)
    return pl.pallas_call(
        substep_kernel,
        out_shape=(
            jax.ShapeDtypeStruct(grid_shape, f32),
            jax.ShapeDtypeStruct(grid_shape, f32),
            ROW,
        ),
        in_specs=[VM] * 10,
        out_specs=(VM, VM, VM),
        scratch_shapes=[
            pltpu.VMEM((3, DEEP + 2, CY, CZ), f32),
            pltpu.VMEM((3, DEEP, CY, CZ), f32),
            pltpu.VMEM((3, DEEP, CY, CZ), f32),
            pltpu.VMEM((DEEP, CY, CZ), f32),
            pltpu.VMEM((DEEP, 8, GROUPS * CZ), f32),
            pltpu.VMEM((576, GROUPS * CZ), bf16),
            pltpu.VMEM((576, GROUPS * CZ), bf16),
            pltpu.VMEM((192, GROUPS * CZ), f32),
            pltpu.VMEM((192, GROUPS * CZ), f32),
            pltpu.VMEM((12, 8, GROUPS * CZ), f32),
        ],
        compiler_params=pltpu.CompilerParams(vmem_limit_bytes=20 << 20),
        cost_estimate=cost(32 * 2 * 192 * 576 * 512, 3 * 720896),
    )(steps, *state, outer, inner, stiff, nodes)

def transition_kernel(flags, inverse, lower, transition):
    transition[...] = -product(inverse[...], lower[...])


def store_half(flags, half, value_ref):
    @pl.when(flags[CORE] == 0)
    def _():
        half[...] = value_ref[:HALF]

    @pl.when(flags[CORE] == 1)
    def _():
        half[...] = value_ref[HALF:]


def first_merge_kernel(flags, own, other, high_ref, low_ref, merged, half):
    is_high = flags[0] == 1
    high = jnp.where(is_high, own[...], other[...])
    low = jnp.where(is_high, other[...], own[...])
    high_ref[...] = high
    low_ref[...] = low
    merged[...] = product(high, low)
    store_half(flags, half, merged)


def first_reach_kernel(flags, other, prefix, suffix):
    is_high = flags[0] == 1
    identity = eye_mask(IB).astype(f32)
    prefix[...] = jnp.where(is_high, other[...], identity)
    suffix[...] = jnp.where(is_high, identity, other[...])


def whole(first, near, far):
    return jnp.concatenate(
        [jnp.where(first, near[...], far[...]), jnp.where(first, far[...], near[...])], axis=0
    )


def merge_kernel(level, last, flags, own, near, far, high_ref, low_ref, *outs):
    is_high = flags[level] == 1
    other = whole(flags[CORE] == 0, near, far)
    high = jnp.where(is_high, own[...], other)
    low = jnp.where(is_high, other, own[...])
    high_ref[...] = high
    low_ref[...] = low
    if not last:
        merged, half = outs
        merged[...] = product(high, low)
        store_half(flags, half, merged)


def block_index(flags):
    return flags[2] + 2 * flags[3]


def sort_kernel(flags, own, near, far, near_far, far_far, near_across, far_across, blocks):
    first = flags[CORE] == 0
    mine = block_index(flags)
    blocks[mine] = own[...]
    for change, pieces in enumerate(((near, far), (near_far, far_far), (near_across, far_across))):
        blocks[mine ^ (change + 1)] = whole(first, *pieces)


def row_kernel(flags, blocks, high, low, merged, half):
    low[...] = product(blocks[1], blocks[0])
    high[...] = product(blocks[3], blocks[2])
    merged[...] = product(high[...], low[...])
    store_half(flags, half, merged)


def row_reach_kernel(flags, blocks, high, low, prefix, suffix, new_prefix, new_suffix):
    base = 2 * flags[3]
    is_high = flags[2] == 1
    longer = product(
        jnp.where(is_high, prefix[...], blocks[base + 1]),
        jnp.where(is_high, blocks[base], suffix[...]),
    )
    new_prefix[...] = jnp.where(is_high, longer, prefix[...])
    new_suffix[...] = jnp.where(is_high, suffix[...], longer)
    in_upper = flags[3] == 1
    longer = product(
        jnp.where(in_upper, new_prefix[...], high[...]),
        jnp.where(in_upper, low[...], new_suffix[...]),
    )
    new_prefix[...] = jnp.where(in_upper, longer, new_prefix[...])
    new_suffix[...] = jnp.where(in_upper, new_suffix[...], longer)


def ordered(flags, rows):
    mine = block_index(flags)
    first = flags[CORE] == 0
    own, split, other_split, opposite = [row[...] for row in rows]
    one = jnp.where(first, split, other_split)
    three = jnp.where(first, other_split, split)
    result = []
    for block in range(4):
        change = mine ^ block
        value = jnp.where(change == 1, one, own)
        value = jnp.where(change == 2, opposite, value)
        result.append(jnp.where(change == 3, three, value))
    return mine, result


def row_forward_kernel(flags, own, split, other_split, opposite, blocks, total, entering):
    mine, rows = ordered(flags, (own, split, other_split, opposite))
    state = rows[0]
    before = jnp.zeros_like(state)
    for block in range(1, 4):
        before = jnp.where(mine == block, state, before)
        state = rows[block] + apply(blocks[block], state)
    total[...] = state
    entering[...] = before


def row_backward_kernel(flags, own, split, other_split, opposite, blocks, total, entering):
    mine, rows = ordered(flags, (own, split, other_split, opposite))
    state = rows[3]
    before = jnp.zeros_like(state)
    for block in range(2, -1, -1):
        before = jnp.where(mine == block, state, before)
        state = rows[block] + apply_transposed(blocks[block], state)
    total[...] = state
    entering[...] = before


def hop_kernel(flags, total, hop, merged, leaving):
    leaving[...] = total[...] + apply(merged[...], hop[...])


def reach_kernel(level, flags, high, low, prefix, suffix, new_prefix, new_suffix):
    is_high = flags[level] == 1
    longer = product(
        jnp.where(is_high, prefix[...], high[...]), jnp.where(is_high, low[...], suffix[...])
    )
    new_prefix[...] = jnp.where(is_high, longer, prefix[...])
    new_suffix[...] = jnp.where(is_high, suffix[...], longer)


def start_kernel(flags, inverse, picked, partner, offset):
    sign = (1 - 2 * flags[SIDE]).astype(f32)
    offset[...] = apply(inverse[...], sign * (picked[...] - partner[...]))


def forward_kernel(level, flags, own, other, high_matrix, total):
    is_high = flags[level] == 1
    high = jnp.where(is_high, own[...], other[...])
    low = jnp.where(is_high, other[...], own[...])
    total[...] = high + apply(high_matrix[...], low)


def backward_kernel(level, flags, own, other, low_matrix, total):
    is_high = flags[level] == 1
    high = jnp.where(is_high, own[...], other[...])
    low = jnp.where(is_high, other[...], own[...])
    total[...] = low + apply_transposed(low_matrix[...], high)


def forward_part_kernel(flags, other_0, other_1, in_row, prefix_0, prefix_1, result):
    result[...] = jnp.where(flags[0] == 1, other_0[...], 0.0) + apply(prefix_1[...], in_row[...])

    @pl.when(flags[1] == 1)
    def _():
        result[...] = result[...] + apply(prefix_0[...], other_1[...])


def backward_part_kernel(
    flags, other_0, other_1, in_row, other_4, suffix_0, suffix_1, suffix_3, result
):
    result[...] = jnp.where(flags[0] == 0, other_0[...], 0.0) + apply_transposed(
        suffix_1[...], in_row[...]
    )

    @pl.when(flags[1] == 0)
    def _():
        result[...] = result[...] + apply_transposed(suffix_0[...], other_1[...])

    @pl.when(flags[4] == 0)
    def _():
        result[...] = result[...] + apply_transposed(suffix_3[...], other_4[...])


def turn_kernel(
    flags, entering, hop_1, hop_2, hop_3, prefix, transition, offset, solved, returning
):
    row = flags[4] + 2 * flags[5]
    state = jnp.zeros_like(hop_1[...])
    for index, hop in ((1, hop_1), (2, hop_2), (3, hop_3)):
        state = jnp.where(row == index, hop[...], state)
    before = entering[...] + apply(prefix[...], state)
    current = offset[...] + apply(transition[...], before)
    solved[...] = current
    returning[...] = -apply_transposed(transition[...], current)


def finish_kernel(
    flags, inverse, entering, other, suffix, solved, velocity, node_mass, nodes, velocity_out
):
    after = entering[...] + jnp.where(flags[5] == 0, 1.0, 0.0) * apply_transposed(
        suffix[...], other[...]
    )
    sign = (1 - 2 * flags[SIDE]).astype(f32)
    multiplier = sign * apply_transposed(inverse[...], solved[...] - after)
    in_row, in_column = slot_masks(nodes[...])
    chosen = in_column.astype(f32).astype(bf16)
    weight = 1.0 / node_mass[...]
    for i in range(3):
        held = jnp.where(in_row, multiplier[:, IFC * i : IFC * i + IFC], 0.0)
        change = sum(
            lax.dot_general(p, chosen, (((1,), (1,)), ((), ())), preferred_element_type=f32)
            for p in reversed(triple(held))
        )
        velocity_out[i] = velocity[i] - change.reshape(CX, CY, CZ) * weight


def bound(level, kernel, *fixed):
    def run(*refs):
        kernel(level, *fixed, *refs)

    return run


def after(value, *earlier):
    return lax.optimization_barrier((value, *earlier))[0]


def first_products(flags, transition, gate):
    cube = 6 * IB**3
    other = after(swap(transition, MASKS[0]), gate)
    high, low, merged, half = local_call(
        first_merge_kernel, flags, [transition, other], (MAT, MAT, MAT, HALFMAT), cube
    )
    prefix, suffix = local_call(first_reach_kernel, flags, [other], (MAT, MAT))
    return (merged, half), [(high, low, prefix, suffix)]


def merge_level(flags, level, block, levels, near):
    cube = 6 * IB**3
    merged, half = block
    far = swap(near, 1)
    last = level == 4
    high, low, *block = local_call(
        bound(level, merge_kernel, last),
        flags,
        [merged, near, far],
        (MAT, MAT) if last else (MAT, MAT, MAT, HALFMAT),
        cube,
    )
    prefix, suffix = local_call(
        bound(level, reach_kernel), flags, [high, low, *levels[-1][2:]], (MAT, MAT), cube
    )
    return block, levels + [(high, low, prefix, suffix)]


def split_swap(value):
    masks = [SPLIT_MASKS[i & 1] for i in range(lax.axis_size("tile"))]
    return lax.ppermute(value, "tile", [(i, i ^ mask) for i, mask in enumerate(masks)])


def row_exchange(total):
    opposite = swap(total, OPPOSITE)
    split = split_swap(total)
    return [split, swap(split, 1), opposite]


def sorted_blocks(flags, fetched, gate):
    merged, nears = fetched
    pieces = []
    for near in nears:
        near = after(near, *gate)
        pieces += [near, swap(near, 1)]
    return local_call(
        sort_kernel, flags, [merged, *pieces], jax.ShapeDtypeStruct((4, IB, IB), f32)
    )


def coupled_velocity(
    flags, picked, inverse, transition, fetched, levels, velocity, node_mass, nodes
):
    square = 2 * IB * IB
    cube = 6 * IB**3
    prefix_0, suffix_0 = levels[0][2:]
    prefix_1, suffix_1 = levels[1][2:]
    count = lax.axis_size("sub")
    partner = lax.ppermute(picked, "sub", [(i, i ^ 1) for i in range(count)])
    offset = local_call(start_kernel, flags, [inverse, picked, partner], ROW, square)
    total, others = offset, []
    for level in range(2):
        others.append(after(swap(total, MASKS[level]), prefix_1))
        total = local_call(
            bound(level, forward_kernel), flags, [total, others[-1], levels[level][0]], ROW, square
        )
    arrived = row_exchange(total)
    blocks = sorted_blocks(flags, fetched, (arrived[1], arrived[2]))
    total, in_row = local_call(
        row_forward_kernel, flags, [total, *arrived, blocks], (ROW, ROW), 3 * square
    )
    high, low, *row = local_call(
        row_kernel, flags, [after(blocks, total)], (MAT, MAT, MAT, HALFMAT), 3 * cube
    )
    merged = row[0]
    hop_1 = after(swap(total, MASKS[4]), merged)
    leaving = local_call(hop_kernel, flags, [total, hop_1, merged], ROW, square)
    hop_2 = swap(leaving, MASKS[5])
    prefix_3, suffix_3 = local_call(
        row_reach_kernel, flags, [blocks, high, low, prefix_1, suffix_1], (MAT, MAT), 2 * cube
    )
    hop_2 = after(hop_2, prefix_3)
    leaving = local_call(hop_kernel, flags, [total, hop_2, merged], ROW, square)
    hop_3 = swap(leaving, MASKS[4])
    entering = local_call(
        forward_part_kernel, flags, [*others, after(in_row, leaving), prefix_0, prefix_1], ROW, 2 * square
    )
    hop_3 = after(hop_3, entering)
    row[1] = after(row[1], hop_3)
    solved, returning = local_call(
        turn_kernel,
        flags,
        [entering, hop_1, hop_2, hop_3, prefix_3, transition, offset],
        (ROW, ROW),
        3 * square,
    )
    total, others = returning, []
    for level in range(2):
        others.append(swap(total, MASKS[level]))
        total = local_call(
            bound(level, backward_kernel), flags, [total, others[-1], levels[level][1]], ROW, square
        )
    arrived = row_exchange(total)
    near = after(swap(row[1], MASKS[4]), arrived[1], arrived[2])
    row, levels = merge_level(
        flags, 4, row, levels + [None, (None, None, prefix_3, suffix_3)], near
    )
    _, low, _, suffix_4 = levels[4]
    total, in_row = local_call(
        row_backward_kernel, flags, [total, *arrived, blocks], (ROW, ROW), 3 * square
    )
    others.append(swap(total, MASKS[4]))
    total = local_call(
        bound(4, backward_kernel), flags, [total, after(others[-1], suffix_4), low], ROW, square
    )
    last_other = swap(total, MASKS[5])
    entering = local_call(
        backward_part_kernel,
        flags,
        [others[0], others[1], in_row, others[2], suffix_0, suffix_1, suffix_3],
        ROW,
        3 * square,
    )
    return local_call(
        finish_kernel,
        flags,
        [inverse, entering, after(last_other, entering), suffix_4, solved, velocity, node_mass, nodes],
        jax.ShapeDtypeStruct(velocity.shape, f32),
        2 * square,
    )


def outer_swap(value):
    count = lax.axis_size("tile")
    route = []
    for low in range(1, count - 1, 2):
        route += [(low, low + 1), (low + 1, low)]
    return lax.ppermute(value, "tile", route)


def body(
    displacement,
    velocity,
    external_load,
    node_mass,
    modulus,
    stiffness,
    substeps,
    interface_nodes,
    factor_inverse,
    factor_lower,
):
    flags = Place()
    sub = lax.axis_index("sub")
    count = substeps.astype(f32)
    steps = jnp.broadcast_to(jnp.stack([count, coarse_step / count]), (2, CZ))
    stiff = local_call(spread_kernel, flags, [stiffness], jax.ShapeDtypeStruct((192, 576), bf16))
    state = [displacement[0], velocity[0], external_load[0], node_mass[0], modulus[0]]
    packed = jax.ShapeDtypeStruct((PACKED, CY, CZ), f32)
    inverse = lax.dynamic_index_in_dim(factor_inverse, sub // 2, 0, keepdims=False)
    lower = lax.dynamic_index_in_dim(factor_lower, sub // 2, 0, keepdims=False)
    transition = local_call(transition_kernel, flags, [inverse, lower], MAT, 6 * IB**3)
    outer, inner = local_call(pack_kernel, flags, state, (packed, packed))
    block, levels = first_products(flags, transition, outer)
    inner = swap(inner, 1)
    near = swap(after(block[1], inner), MASKS[1])
    outer = outer_swap(outer)
    block, levels = merge_level(flags, 1, block, levels, near)
    merged, half = block
    fetched = merged, [swap(half, mask) for mask in (SPLIT_MASKS[0], OPPOSITE, SPLIT_MASKS[1])]
    outer = after(outer, half)
    final_displacement, final_velocity, picked = substeps_call(
        steps, state, outer, inner, stiff, interface_nodes
    )
    coupled = coupled_velocity(
        flags,
        picked,
        inverse,
        transition,
        fetched,
        levels,
        final_velocity,
        node_mass[0],
        interface_nodes,
    )
    return final_displacement[None], coupled[None]


def solution(mesh):
    in_specs = (
        P("sub", None, "tile", None, None),
        P("sub", None, "tile", None, None),
        P("sub", None, "tile", None, None),
        P("sub", "tile", None, None),
        P("sub", "tile", None, None),
        P(),
        P("sub"),
        P("sub", "tile"),
        P(None, "tile", None),
        P(None, "tile", None),
    )
    out_specs = (P("sub", None, "tile", None, None), P("sub", None, "tile", None, None))
    return jax.shard_map(body, mesh=mesh, in_specs=in_specs, out_specs=out_specs, check_vma=False)
```

```python
import jax
import jax.numpy as jnp
from jax import lax
from jax.experimental import pallas as pl
from jax.experimental.pallas import tpu as pltpu
from jax.sharding import PartitionSpec as P

IFC = 128
IB = 384
HALF = IB // 2
GRANT = 12 << 20
CX, CY, CZ = 4, 32, 128
DEEP = 3 * CX
NEAR = CX - 1
PACKED = 37
CORE, PAIR, SIDE, LAST = 0, 6, 7, 8
GROUPS = CY // 8
MASKS = (1, 2, 4, 12, 16, 48)
SPLIT_MASKS = (4, 12)
OPPOSITE = 10

coarse_step = 0.1
f32 = jnp.float32
bf16 = jnp.bfloat16
VM = pl.BlockSpec(memory_space=pltpu.VMEM)
MAT = jax.ShapeDtypeStruct((IB, IB), f32)
HALFMAT = jax.ShapeDtypeStruct((HALF, IB), f32)
ROW = jax.ShapeDtypeStruct((1, IB), f32)


def swap(value, mask):
    return lax.ppermute(value, "tile", [(i, i ^ mask) for i in range(lax.axis_size("tile"))])


def cost(flops, nbytes):
    return pl.CostEstimate(flops=flops, bytes_accessed=nbytes, transcendentals=0)


class Place:
    def __getitem__(self, item):
        tile, sub = lax.axis_index("tile"), lax.axis_index("sub")
        if item == PAIR:
            return sub // 2
        if item == SIDE:
            return sub % 2
        if item == LAST:
            return (tile == lax.axis_size("tile") - 1).astype(jnp.int32)
        return (tile >> item) & 1


def local_call(kernel, place, operands, outs, flops=0):
    nbytes = sum(o.size * 4 for o in operands)

    def placed(*refs):
        kernel(place, *refs)

    return pl.pallas_call(
        placed,
        out_shape=outs,
        in_specs=[VM] * len(operands),
        out_specs=jax.tree.map(lambda _: VM, outs),
        compiler_params=pltpu.CompilerParams(vmem_limit_bytes=GRANT),
        cost_estimate=cost(flops, nbytes),
    )(*operands)


def halves(value):
    high = value.astype(bf16)
    return high, (value - high.astype(f32)).astype(bf16)


def product(a, b):
    a_high, a_low = halves(a)
    b_high, b_low = halves(b)
    return (
        jnp.dot(a_low, b_high, preferred_element_type=f32)
        + jnp.dot(a_high, b_low, preferred_element_type=f32)
        + jnp.dot(a_high, b_high, preferred_element_type=f32)
    )


def eye_mask(size):
    return lax.broadcasted_iota(jnp.int32, (size, size), 0) == lax.broadcasted_iota(
        jnp.int32, (size, size), 1
    )


def column_to_row(column):
    eye = eye_mask(IFC)
    return jnp.concatenate(
        [
            jnp.sum(jnp.where(eye, column[k : k + IFC], 0.0), axis=0, keepdims=True)
            for k in range(0, IB, IFC)
        ],
        axis=1,
    )


def row_to_column(row):
    eye = eye_mask(IFC)
    return jnp.concatenate(
        [
            jnp.sum(jnp.where(eye, row[:, k : k + IFC], 0.0), axis=1, keepdims=True)
            for k in range(0, IB, IFC)
        ],
        axis=0,
    )


def apply(matrix, row):
    return column_to_row(jnp.sum(matrix * row, axis=1, keepdims=True))


def apply_transposed(matrix, row):
    return jnp.sum(matrix * row_to_column(row), axis=0, keepdims=True)


def triple(value):
    high = value.astype(bf16)
    rest = value - high.astype(f32)
    middle = rest.astype(bf16)
    return high, middle, (rest - middle.astype(f32)).astype(bf16)


def slot_masks(nodes):
    index = lax.broadcasted_iota(jnp.int32, (IFC, IFC), 0)
    return index == nodes // CZ, index == nodes % CZ


def wide(value):
    return jnp.concatenate([value[8 * g : 8 * g + 8] for g in range(GROUPS)], axis=1)


def tall(value):
    return jnp.concatenate([value[:, CZ * g : CZ * g + CZ] for g in range(GROUPS)], axis=0)


def spread(values):
    row = lax.broadcasted_iota(jnp.int32, (192, 24), 0) // 8
    rows = (row == lax.broadcasted_iota(jnp.int32, (192, 24), 1)).astype(f32).astype(bf16)
    block = lax.broadcasted_iota(jnp.int32, (24, 192), 1) // 8
    side = block // 12
    dof = 8 * (block % 12 // 4) + 4 * side + block % 4
    columns = (dof == lax.broadcasted_iota(jnp.int32, (24, 192), 0)).astype(f32).astype(bf16)
    tall_values = jnp.dot(rows, values, preferred_element_type=f32).astype(bf16)
    full = jnp.dot(tall_values, columns, preferred_element_type=f32)
    same = (
        lax.broadcasted_iota(jnp.int32, (192, 192), 0) % 8
        == lax.broadcasted_iota(jnp.int32, (192, 192), 1) % 8
    )
    return jnp.where(same, full, 0.0).astype(bf16)


def substep_kernel(
    steps, displacement, velocity, external_load, node_mass, modulus,
    outer, inner, stiff, nodes,
    displacement_out, velocity_out, picked,
    disp, vel, load, inverse_mass, factor, even, odd, even_force, odd_force, upper,
):
    flags = Place()
    first = flags[CORE] == 0

    def put_mass(low, mass):
        present = mass > 0.0
        inverse_mass[pl.ds(low, mass.shape[0])] = jnp.where(
            present, 1.0 / jnp.where(present, mass, 1.0), 0.0
        )

    def put_factor(low, source, base):
        row = lax.broadcasted_iota(jnp.int32, (CY, CZ), 0)
        for x in range(CX):
            factor[low + x] = wide(jnp.where(row < CY - 1, source[base + x], 0.0))

    def place(source, low, shift):
        for i in range(3):
            disp[i, pl.ds(low, CX)] = source[pl.ds(CX * i, CX)]
            vel[i, pl.ds(low + shift, NEAR)] = source[pl.ds(12 + NEAR * i, NEAR)]
            load[i, pl.ds(low + shift, NEAR)] = source[pl.ds(21 + NEAR * i, NEAR)]
        put_mass(low + shift, source[pl.ds(30, NEAR)])
        put_factor(low, source, 33)

    disp[:, CX : 2 * CX] = displacement[...]
    vel[:, CX : 2 * CX] = velocity[...]
    load[:, CX : 2 * CX] = external_load[...]
    put_mass(CX, node_mass[...])
    put_factor(CX, modulus, 0)

    @pl.when(first)
    def _():
        place(outer, 0, 1)
        place(inner, 2 * CX, 0)

    @pl.when(jnp.logical_not(first))
    def _():
        place(inner, 0, 1)
        place(outer, 2 * CX, 0)

    @pl.when(flags[LAST] == 1)
    def _():
        factor[2 * CX - 1] = jnp.zeros((8, GROUPS * CZ), f32)

    length = steps[1:2]

    def put_features(layer, below, above):
        columns = []
        for i in range(3):
            base = disp[i, layer]
            turned = pltpu.roll(base, CZ - 1, 1)
            columns += [base, turned, pltpu.roll(base, CY - 1, 0), pltpu.roll(turned, CY - 1, 0)]
        for g in range(GROUPS):
            lanes = slice(CZ * g, CZ * g + CZ)
            block = jnp.concatenate([c[8 * g : 8 * g + 8] for c in columns], axis=0)
            high, low = halves(block)
            for target, start in ((below, 96), (above, 0)):
                if target is not None:
                    target[start : start + 96, lanes] = high
                    target[start + 192 : start + 288, lanes] = low
                    target[start + 384 : start + 480, lanes] = high

    def put_force(source, target):
        target[...] = jnp.dot(stiff[...], source[...], preferred_element_type=f32)

    def corner(force, scale, i, a, r):
        start = 8 * (8 * i + 4 * a + r)
        return force[start : start + 8] * scale

    def keep_upper(layer, force):
        scale = factor[layer]
        for i in range(3):
            for r in range(4):
                upper[4 * i + r] = corner(force, scale, i, 1, r)

    def finish_layer(layer, force):
        scale = factor[layer]
        weight = inverse_mass[layer]
        for i in range(3):
            sums = [corner(force, scale, i, 0, r) + upper[4 * i + r] for r in range(4)]
            s00, s01, s10, s11 = [tall(s) for s in sums]
            base = s00 + pltpu.roll(s10, 1, 0)
            turned = s01 + pltpu.roll(s11, 1, 0)
            internal = base + pltpu.roll(turned, 1, 1)
            speed = vel[i, layer] + length * ((load[i, layer] - internal) * weight)
            vel[i, layer] = speed
            disp[i, layer] = disp[i, layer] + length * speed

    def one_substep(k, carry):
        put_features(k, None, even)
        put_features(k + 1, even, odd)
        put_force(even, even_force)
        put_features(k + 2, odd, even)
        keep_upper(k, even_force)
        put_force(odd, odd_force)
        put_features(k + 3, even, odd)

        def two_layers(pair, carry):
            layer = k + 1 + 2 * pair
            put_force(even, even_force)
            put_features(layer + 3, odd, even)
            finish_layer(layer, odd_force)
            keep_upper(layer, odd_force)
            put_force(odd, odd_force)
            put_features(layer + 4, even, odd)
            finish_layer(layer + 1, even_force)
            keep_upper(layer + 1, even_force)
            return carry

        return lax.fori_loop(0, CX + 1 - k, two_layers, carry)

    lax.fori_loop(0, jnp.max(steps[0:1]).astype(jnp.int32), one_substep, 0)
    displacement_out[...] = disp[:, CX : 2 * CX]
    final = vel[:, CX : 2 * CX]
    velocity_out[...] = final
    in_row, in_column = slot_masks(nodes[...])
    chosen = in_column.astype(f32).astype(bf16)
    parts = []
    for i in range(3):
        pieces = triple(final[i].reshape(CX * CY, CZ))
        values = sum(jnp.dot(p, chosen, preferred_element_type=f32) for p in reversed(pieces))
        parts.append(jnp.sum(jnp.where(in_row, values, 0.0), axis=0, keepdims=True))
    picked[...] = jnp.concatenate(parts, axis=1)


def pack_kernel(flags, displacement, velocity, external_load, node_mass, modulus, outer, inner):
    for target, start in ((outer, flags[CORE]), (inner, 1 - flags[CORE])):
        for i in range(3):
            target[pl.ds(CX * i, CX)] = displacement[i]
            target[pl.ds(12 + NEAR * i, NEAR)] = velocity[i, pl.ds(start, NEAR)]
            target[pl.ds(21 + NEAR * i, NEAR)] = external_load[i, pl.ds(start, NEAR)]
        target[pl.ds(30, NEAR)] = node_mass[pl.ds(start, NEAR)]
        target[pl.ds(33, CX)] = modulus[...]


def spread_kernel(flags, stiffness, stiff):
    high, low = [spread(s) for s in halves(stiffness[...])]
    stiff[...] = jnp.concatenate([high, high, low], axis=1)


def substeps_call(steps, state, outer, inner, stiff, nodes):
    grid_shape = (3, CX, CY, CZ)
    return pl.pallas_call(
        substep_kernel,
        out_shape=(
            jax.ShapeDtypeStruct(grid_shape, f32),
            jax.ShapeDtypeStruct(grid_shape, f32),
            ROW,
        ),
        in_specs=[VM] * 10,
        out_specs=(VM, VM, VM),
        scratch_shapes=[
            pltpu.VMEM((3, DEEP + 2, CY, CZ), f32),
            pltpu.VMEM((3, DEEP, CY, CZ), f32),
            pltpu.VMEM((3, DEEP, CY, CZ), f32),
            pltpu.VMEM((DEEP, CY, CZ), f32),
            pltpu.VMEM((DEEP, 8, GROUPS * CZ), f32),
            pltpu.VMEM((576, GROUPS * CZ), bf16),
            pltpu.VMEM((576, GROUPS * CZ), bf16),
            pltpu.VMEM((192, GROUPS * CZ), f32),
            pltpu.VMEM((192, GROUPS * CZ), f32),
            pltpu.VMEM((12, 8, GROUPS * CZ), f32),
        ],
        compiler_params=pltpu.CompilerParams(vmem_limit_bytes=20 << 20),
        cost_estimate=cost(32 * 2 * 192 * 576 * 512, 3 * 720896),
    )(steps, *state, outer, inner, stiff, nodes)

def transition_kernel(flags, inverse, lower, transition):
    transition[...] = -product(inverse[...], lower[...])


def store_half(flags, half, value_ref):
    @pl.when(flags[CORE] == 0)
    def _():
        half[...] = value_ref[:HALF]

    @pl.when(flags[CORE] == 1)
    def _():
        half[...] = value_ref[HALF:]


def first_merge_kernel(flags, own, other, high_ref, low_ref, merged, half):
    is_high = flags[0] == 1
    high = jnp.where(is_high, own[...], other[...])
    low = jnp.where(is_high, other[...], own[...])
    high_ref[...] = high
    low_ref[...] = low
    merged[...] = product(high, low)
    store_half(flags, half, merged)


def first_reach_kernel(flags, other, prefix, suffix):
    is_high = flags[0] == 1
    identity = eye_mask(IB).astype(f32)
    prefix[...] = jnp.where(is_high, other[...], identity)
    suffix[...] = jnp.where(is_high, identity, other[...])


def whole(first, near, far):
    return jnp.concatenate(
        [jnp.where(first, near[...], far[...]), jnp.where(first, far[...], near[...])], axis=0
    )


def merge_kernel(level, last, flags, own, near, far, high_ref, low_ref, *outs):
    is_high = flags[level] == 1
    other = whole(flags[CORE] == 0, near, far)
    high = jnp.where(is_high, own[...], other)
    low = jnp.where(is_high, other, own[...])
    high_ref[...] = high
    low_ref[...] = low
    if not last:
        merged, half = outs
        merged[...] = product(high, low)
        store_half(flags, half, merged)


def block_index(flags):
    return flags[2] + 2 * flags[3]


def sort_kernel(flags, own, near, far, near_far, far_far, near_across, far_across, blocks):
    first = flags[CORE] == 0
    mine = block_index(flags)
    blocks[mine] = own[...]
    for change, pieces in enumerate(((near, far), (near_far, far_far), (near_across, far_across))):
        blocks[mine ^ (change + 1)] = whole(first, *pieces)


def row_kernel(flags, blocks, high, low, merged, half):
    low[...] = product(blocks[1], blocks[0])
    high[...] = product(blocks[3], blocks[2])
    merged[...] = product(high[...], low[...])
    store_half(flags, half, merged)


def row_reach_kernel(flags, blocks, high, low, prefix, suffix, new_prefix, new_suffix):
    base = 2 * flags[3]
    is_high = flags[2] == 1
    longer = product(
        jnp.where(is_high, prefix[...], blocks[base + 1]),
        jnp.where(is_high, blocks[base], suffix[...]),
    )
    new_prefix[...] = jnp.where(is_high, longer, prefix[...])
    new_suffix[...] = jnp.where(is_high, suffix[...], longer)
    in_upper = flags[3] == 1
    longer = product(
        jnp.where(in_upper, new_prefix[...], high[...]),
        jnp.where(in_upper, low[...], new_suffix[...]),
    )
    new_prefix[...] = jnp.where(in_upper, longer, new_prefix[...])
    new_suffix[...] = jnp.where(in_upper, new_suffix[...], longer)


def ordered(flags, rows):
    mine = block_index(flags)
    first = flags[CORE] == 0
    own, split, other_split, opposite = [row[...] for row in rows]
    one = jnp.where(first, split, other_split)
    three = jnp.where(first, other_split, split)
    result = []
    for block in range(4):
        change = mine ^ block
        value = jnp.where(change == 1, one, own)
        value = jnp.where(change == 2, opposite, value)
        result.append(jnp.where(change == 3, three, value))
    return mine, result


def row_forward_kernel(flags, own, split, other_split, opposite, blocks, total, entering):
    mine, rows = ordered(flags, (own, split, other_split, opposite))
    state = rows[0]
    before = jnp.zeros_like(state)
    for block in range(1, 4):
        before = jnp.where(mine == block, state, before)
        state = rows[block] + apply(blocks[block], state)
    total[...] = state
    entering[...] = before


def row_backward_kernel(flags, own, split, other_split, opposite, blocks, total, entering):
    mine, rows = ordered(flags, (own, split, other_split, opposite))
    state = rows[3]
    before = jnp.zeros_like(state)
    for block in range(2, -1, -1):
        before = jnp.where(mine == block, state, before)
        state = rows[block] + apply_transposed(blocks[block], state)
    total[...] = state
    entering[...] = before


def hop_kernel(flags, total, hop, merged, leaving):
    leaving[...] = total[...] + apply(merged[...], hop[...])


def reach_kernel(level, flags, high, low, prefix, suffix, new_prefix, new_suffix):
    is_high = flags[level] == 1
    longer = product(
        jnp.where(is_high, prefix[...], high[...]), jnp.where(is_high, low[...], suffix[...])
    )
    new_prefix[...] = jnp.where(is_high, longer, prefix[...])
    new_suffix[...] = jnp.where(is_high, suffix[...], longer)


def start_kernel(flags, inverse, picked, partner, offset):
    sign = (1 - 2 * flags[SIDE]).astype(f32)
    offset[...] = apply(inverse[...], sign * (picked[...] - partner[...]))


def forward_kernel(level, flags, own, other, high_matrix, total):
    is_high = flags[level] == 1
    high = jnp.where(is_high, own[...], other[...])
    low = jnp.where(is_high, other[...], own[...])
    total[...] = high + apply(high_matrix[...], low)


def backward_kernel(level, flags, own, other, low_matrix, total):
    is_high = flags[level] == 1
    high = jnp.where(is_high, own[...], other[...])
    low = jnp.where(is_high, other[...], own[...])
    total[...] = low + apply_transposed(low_matrix[...], high)


def forward_part_kernel(flags, other_0, other_1, in_row, prefix_0, prefix_1, result):
    result[...] = jnp.where(flags[0] == 1, other_0[...], 0.0) + apply(prefix_1[...], in_row[...])

    @pl.when(flags[1] == 1)
    def _():
        result[...] = result[...] + apply(prefix_0[...], other_1[...])


def backward_part_kernel(
    flags, other_0, other_1, in_row, other_4, suffix_0, suffix_1, suffix_3, result
):
    result[...] = jnp.where(flags[0] == 0, other_0[...], 0.0) + apply_transposed(
        suffix_1[...], in_row[...]
    )

    @pl.when(flags[1] == 0)
    def _():
        result[...] = result[...] + apply_transposed(suffix_0[...], other_1[...])

    @pl.when(flags[4] == 0)
    def _():
        result[...] = result[...] + apply_transposed(suffix_3[...], other_4[...])


def turn_kernel(
    flags, entering, hop_1, hop_2, hop_3, prefix, transition, offset, solved, returning
):
    row = flags[4] + 2 * flags[5]
    state = jnp.zeros_like(hop_1[...])
    for index, hop in ((1, hop_1), (2, hop_2), (3, hop_3)):
        state = jnp.where(row == index, hop[...], state)
    before = entering[...] + apply(prefix[...], state)
    current = offset[...] + apply(transition[...], before)
    solved[...] = current
    returning[...] = -apply_transposed(transition[...], current)


def finish_kernel(
    flags, inverse, entering, other, suffix, solved, velocity, node_mass, nodes, velocity_out
):
    after = entering[...] + jnp.where(flags[5] == 0, 1.0, 0.0) * apply_transposed(
        suffix[...], other[...]
    )
    sign = (1 - 2 * flags[SIDE]).astype(f32)
    multiplier = sign * apply_transposed(inverse[...], solved[...] - after)
    in_row, in_column = slot_masks(nodes[...])
    chosen = in_column.astype(f32).astype(bf16)
    weight = 1.0 / node_mass[...]
    for i in range(3):
        held = jnp.where(in_row, multiplier[:, IFC * i : IFC * i + IFC], 0.0)
        change = sum(
            lax.dot_general(p, chosen, (((1,), (1,)), ((), ())), preferred_element_type=f32)
            for p in reversed(triple(held))
        )
        velocity_out[i] = velocity[i] - change.reshape(CX, CY, CZ) * weight


def bound(level, kernel, *fixed):
    def run(*refs):
        kernel(level, *fixed, *refs)

    return run


def after(value, *earlier):
    return lax.optimization_barrier((value, *earlier))[0]


def first_products(flags, transition, gate):
    cube = 6 * IB**3
    other = after(swap(transition, MASKS[0]), gate)
    high, low, merged, half = local_call(
        first_merge_kernel, flags, [transition, other], (MAT, MAT, MAT, HALFMAT), cube
    )
    prefix, suffix = local_call(first_reach_kernel, flags, [other], (MAT, MAT))
    return (merged, half), [(high, low, prefix, suffix)]


def merge_level(flags, level, block, levels, near):
    cube = 6 * IB**3
    merged, half = block
    far = swap(near, 1)
    last = level == 4
    high, low, *block = local_call(
        bound(level, merge_kernel, last),
        flags,
        [merged, near, far],
        (MAT, MAT) if last else (MAT, MAT, MAT, HALFMAT),
        cube,
    )
    prefix, suffix = local_call(
        bound(level, reach_kernel), flags, [high, low, *levels[-1][2:]], (MAT, MAT), cube
    )
    return block, levels + [(high, low, prefix, suffix)]


def split_swap(value):
    masks = [SPLIT_MASKS[i & 1] for i in range(lax.axis_size("tile"))]
    return lax.ppermute(value, "tile", [(i, i ^ mask) for i, mask in enumerate(masks)])


def row_exchange(total):
    opposite = swap(total, OPPOSITE)
    split = split_swap(total)
    return [split, swap(split, 1), opposite]


def sorted_blocks(flags, fetched, gate):
    merged, nears = fetched
    pieces = []
    for near in nears:
        near = after(near, *gate)
        pieces += [near, swap(near, 1)]
    return local_call(
        sort_kernel, flags, [merged, *pieces], jax.ShapeDtypeStruct((4, IB, IB), f32)
    )


def coupled_velocity(
    flags, picked, inverse, transition, fetched, levels, velocity, node_mass, nodes
):
    square = 2 * IB * IB
    cube = 6 * IB**3
    prefix_0, suffix_0 = levels[0][2:]
    prefix_1, suffix_1 = levels[1][2:]
    count = lax.axis_size("sub")
    partner = lax.ppermute(picked, "sub", [(i, i ^ 1) for i in range(count)])
    offset = local_call(start_kernel, flags, [inverse, picked, partner], ROW, square)
    total, others = offset, []
    for level in range(2):
        others.append(after(swap(total, MASKS[level]), prefix_1))
        total = local_call(
            bound(level, forward_kernel), flags, [total, others[-1], levels[level][0]], ROW, square
        )
    arrived = row_exchange(total)
    blocks = sorted_blocks(flags, fetched, (arrived[0], arrived[2]))
    total, in_row = local_call(
        row_forward_kernel, flags, [total, *arrived, blocks], (ROW, ROW), 3 * square
    )
    high, low, *row = local_call(
        row_kernel, flags, [after(blocks, total)], (MAT, MAT, MAT, HALFMAT), 3 * cube
    )
    merged = row[0]
    hop_1 = after(swap(total, MASKS[4]), merged)
    leaving = local_call(hop_kernel, flags, [total, hop_1, merged], ROW, square)
    hop_2 = swap(leaving, MASKS[5])
    prefix_3, suffix_3 = local_call(
        row_reach_kernel, flags, [blocks, high, low, prefix_1, suffix_1], (MAT, MAT), 2 * cube
    )
    hop_2 = after(hop_2, prefix_3)
    leaving = local_call(hop_kernel, flags, [total, hop_2, merged], ROW, square)
    hop_3 = swap(leaving, MASKS[4])
    entering = local_call(
        forward_part_kernel, flags, [*others, after(in_row, leaving), prefix_0, prefix_1], ROW, 2 * square
    )
    hop_3 = after(hop_3, entering)
    row[1] = after(row[1], hop_3)
    solved, returning = local_call(
        turn_kernel,
        flags,
        [entering, hop_1, hop_2, hop_3, prefix_3, transition, offset],
        (ROW, ROW),
        3 * square,
    )
    total, others = returning, []
    for level in range(2):
        others.append(swap(total, MASKS[level]))
        total = local_call(
            bound(level, backward_kernel), flags, [total, others[-1], levels[level][1]], ROW, square
        )
    arrived = row_exchange(total)
    near = after(swap(row[1], MASKS[4]), arrived[1], arrived[2])
    row, levels = merge_level(
        flags, 4, row, levels + [None, (None, None, prefix_3, suffix_3)], near
    )
    _, low, _, suffix_4 = levels[4]
    total, in_row = local_call(
        row_backward_kernel, flags, [total, *arrived, blocks], (ROW, ROW), 3 * square
    )
    others.append(swap(total, MASKS[4]))
    total = local_call(
        bound(4, backward_kernel), flags, [total, after(others[-1], suffix_4), low], ROW, square
    )
    last_other = swap(total, MASKS[5])
    entering = local_call(
        backward_part_kernel,
        flags,
        [others[0], others[1], in_row, others[2], suffix_0, suffix_1, suffix_3],
        ROW,
        3 * square,
    )
    return local_call(
        finish_kernel,
        flags,
        [inverse, entering, after(last_other, entering), suffix_4, solved, velocity, node_mass, nodes],
        jax.ShapeDtypeStruct(velocity.shape, f32),
        2 * square,
    )


def outer_swap(value):
    count = lax.axis_size("tile")
    route = []
    for low in range(1, count - 1, 2):
        route += [(low, low + 1), (low + 1, low)]
    return lax.ppermute(value, "tile", route)


def body(
    displacement,
    velocity,
    external_load,
    node_mass,
    modulus,
    stiffness,
    substeps,
    interface_nodes,
    factor_inverse,
    factor_lower,
):
    flags = Place()
    sub = lax.axis_index("sub")
    count = substeps.astype(f32)
    steps = jnp.broadcast_to(jnp.stack([count, coarse_step / count]), (2, CZ))
    stiff = local_call(spread_kernel, flags, [stiffness], jax.ShapeDtypeStruct((192, 576), bf16))
    state = [displacement[0], velocity[0], external_load[0], node_mass[0], modulus[0]]
    packed = jax.ShapeDtypeStruct((PACKED, CY, CZ), f32)
    inverse = lax.dynamic_index_in_dim(factor_inverse, sub // 2, 0, keepdims=False)
    lower = lax.dynamic_index_in_dim(factor_lower, sub // 2, 0, keepdims=False)
    transition = local_call(transition_kernel, flags, [inverse, lower], MAT, 6 * IB**3)
    outer, inner = local_call(pack_kernel, flags, state, (packed, packed))
    block, levels = first_products(flags, transition, outer)
    inner = swap(inner, 1)
    near = swap(after(block[1], inner), MASKS[1])
    outer = outer_swap(outer)
    block, levels = merge_level(flags, 1, block, levels, near)
    merged, half = block
    fetched = merged, [swap(half, mask) for mask in (SPLIT_MASKS[0], OPPOSITE, SPLIT_MASKS[1])]
    outer = after(outer, half)
    final_displacement, final_velocity, picked = substeps_call(
        steps, state, outer, inner, stiff, interface_nodes
    )
    coupled = coupled_velocity(
        flags,
        picked,
        inverse,
        transition,
        fetched,
        levels,
        final_velocity,
        node_mass[0],
        interface_nodes,
    )
    return final_displacement[None], coupled[None]


def solution(mesh):
    in_specs = (
        P("sub", None, "tile", None, None),
        P("sub", None, "tile", None, None),
        P("sub", None, "tile", None, None),
        P("sub", "tile", None, None),
        P("sub", "tile", None, None),
        P(),
        P("sub"),
        P("sub", "tile"),
        P(None, "tile", None),
        P(None, "tile", None),
    )
    out_specs = (P("sub", None, "tile", None, None), P("sub", None, "tile", None, None))
    return jax.shard_map(body, mesh=mesh, in_specs=in_specs, out_specs=out_specs, check_vma=False)
```
